128 devices in a mesh: rep: 32 (over x, z, y_lo), fsdp: 4 (over y_hi, core).
Axes of the slice: x: 4, y: 4 (y_hi: 2, y_lo: 2; y = y_hi * 2 + y_lo), z: 4, core: 2. Of those that a mesh axis runs over, the one named last changes fastest.
Arguments:
- tokens: bfloat16 [8192, 2560], P('rep', 'fsdp'), may hold values from -6 to 6
- seq_len: int32 [128], replicated, may hold values from 1 to 253, as said below
- seq_owner: int32 [128], replicated, may hold values from 0 to 31, as said below
- gain_1: bfloat16 [2560], P('fsdp'), may hold values from 0.099609375 to 1.8984375
- gain_2: bfloat16 [2560], P('fsdp'), may hold values from 0.099609375 to 1.8984375
- w_xy: bfloat16 [2, 2560, 10, 256], P(None, None, None, 'fsdp'), may hold values from -0.125 to 0.125
- conv_w: bfloat16 [4, 10, 256], P(None, None, 'fsdp'), may hold values from -3 to 3
- conv_b: bfloat16 [10, 256], P(None, 'fsdp'), may hold values from -2 to 2
- gate_w: bfloat16 [2, 10, 256, 256], P(None, None, None, 'fsdp'), may hold values from -0.375 to 0.375
- gate_b: bfloat16 [2, 10, 256], P(None, None, 'fsdp'), may hold values from -3 to 3
- a_param: float32 [10, 256], P(None, 'fsdp'), may hold values from -9 to -4
- w_out: bfloat16 [10, 256, 2560], P(None, 'fsdp'), may hold values from -0.3125 to 0.3125
- w_in: bfloat16 [2, 2560, 7680], P(None, None, 'fsdp'), may hold values from -0.125 to 0.125
- w_down: bfloat16 [7680, 2560], P('fsdp'), may hold values from -0.125 to 0.125
- cotangent: bfloat16 [8192, 2560], P('rep', 'fsdp'), may hold values from -6 to 6
Outputs:
- block_out: bfloat16 [8192, 2560], P('rep', 'fsdp')
- d_tokens: float32 [8192, 2560], P('rep', 'fsdp')
- d_gain_1: float32 [2560], P('fsdp')
- d_gain_2: float32 [2560], P('fsdp')
- d_w_xy: float32 [2, 2560, 10, 256], P(None, 'rep', None, 'fsdp')
- d_conv_w: float32 [4, 10, 256], P(None, None, 'fsdp')
- d_conv_b: float32 [10, 256], P(None, 'fsdp')
- d_gate_w: float32 [2, 10, 256, 256], P(None, None, 'rep', 'fsdp')
- d_gate_b: float32 [2, 10, 256], P(None, None, 'fsdp')
- d_a_param: float32 [10, 256], P(None, 'fsdp')
- d_w_out: float32 [10, 256, 2560], P(None, 'fsdp', 'rep')
- d_w_in: float32 [2, 2560, 7680], P(None, 'rep', 'fsdp')
- d_w_down: float32 [7680, 2560], P('fsdp', 'rep')
The draws below stay inside these ranges and needn't reach their ends.
Inputs may be any that keep to these rules, and one draw needn't show every extreme that they name: `seq_len`: the sequences owned by one index of rep have lengths that sum to at most 256; in every draw one index's sequences fill all its 256 rows, and its first sequence is 253 long. `seq_owner`: each index of rep owns exactly 4 sequences.
All inputs are finite; a program needn't handle non-finite values.
Results may differ from the reference program's by a relative error of at most 0.025.
Values may be sent and summed in bfloat16 or wider, within the bound.
A program may use at most 320 MiB of HBM per device.

```python
import jax
import jax.numpy as jnp
from jax import lax

D = 2560
H = 10
BLK = 256
FF = 7680
CW = 4
SEQ_GROUP = 4
GROUP_TOK = 256
L = 2560
TOKENS = 8192
NSEQ = 128
N_REP = 32


def sequence_table(key):
    groups = NSEQ // SEQ_GROUP
    key_perm, key_total, key_full, key_weight = jax.random.split(key, 4)
    owner = (jax.random.permutation(key_perm, NSEQ) % groups).astype(jnp.int32)
    seq_index = jnp.arange(NSEQ, dtype=jnp.int32)
    same_group = owner[:, None] == owner[None, :]
    rank = jnp.sum(same_group & (seq_index[None, :] < seq_index[:, None]), axis=1).astype(jnp.int32)
    group_ids = jnp.arange(groups, dtype=jnp.int32)
    full_group = jax.random.randint(key_full, (), 0, groups, dtype=jnp.int32)
    totals = jax.random.randint(key_total, (groups,), GROUP_TOK // 2, GROUP_TOK + 1, dtype=jnp.int32)
    totals = jnp.where(group_ids == full_group, GROUP_TOK, totals)
    weights = jax.random.randint(key_weight, (groups, SEQ_GROUP), 1, 9, dtype=jnp.int32)
    spare = totals - SEQ_GROUP
    pieces = 1 + weights * spare[:, None] // jnp.sum(weights, axis=1, keepdims=True)
    remain = totals - jnp.sum(pieces, axis=1)
    last_slot = (jnp.arange(SEQ_GROUP, dtype=jnp.int32) == SEQ_GROUP - 1).astype(jnp.int32)
    pieces = pieces + remain[:, None] * last_slot[None, :]
    special = jnp.concatenate([jnp.full((1,), GROUP_TOK - SEQ_GROUP + 1, jnp.int32), jnp.ones((SEQ_GROUP - 1,), jnp.int32)])
    pieces = jnp.where((group_ids == full_group)[:, None], special[None, :], pieces)
    slots = jnp.arange(SEQ_GROUP, dtype=jnp.int32)
    picked = (owner[:, None, None] == group_ids[None, :, None]) & (rank[:, None, None] == slots[None, None, :])
    lengths = jnp.sum(jnp.where(picked, pieces[None, :, :], 0), axis=(1, 2)).astype(jnp.int32)
    return (lengths, owner)


def draw_seq_len(key, part):
    return sequence_table(key)[0]


def draw_seq_owner(key, part):
    return sequence_table(key)[1]


def steps_of(key, dims, cuts, low, high):
    loudness = 1.0
    for dim, shards_of in cuts:
        steps = jax.random.uniform(jax.random.fold_in(jax.random.fold_in(key, 6), dim), (shards_of,), jnp.float32, low / len(cuts), high / len(cuts))
        loudness = loudness * jnp.repeat(jnp.exp(steps), dims[dim] // shards_of).reshape((-1,) + (1,) * (len(dims) - 1 - dim))
    return loudness


def bell_draw(own_key, extent, spread, limit, cuts=(), kind=jnp.bfloat16):
    gain = steps_of(own_key, extent, cuts, -0.22, 0.18) if cuts else 1.0
    values = jax.random.normal(own_key, extent, jnp.float32) * spread * gain
    return jnp.minimum(jnp.maximum(values, -limit), limit).astype(kind)


def setup_inputs(seed: int = 0) -> dict:
    streams_of = jax.random.split(jax.random.key(seed), 16)
    tokens = bell_draw(streams_of[0], (TOKENS, D), 1.0, 6.0, ((0, 32), (1, 4)))
    seq_len = draw_seq_len(jax.random.fold_in(streams_of[15], 71), 0)
    seq_owner = draw_seq_owner(jax.random.fold_in(streams_of[15], 71), 0)
    gain_1 = jnp.clip(1.0 + 0.18 * jax.random.normal(streams_of[3], (D,), jnp.float32), 0.099609375, 1.8984375).astype(jnp.bfloat16)
    gain_2 = jnp.clip(1.0 + 0.18 * jax.random.normal(streams_of[4], (D,), jnp.float32), 0.099609375, 1.8984375).astype(jnp.bfloat16)
    w_xy = bell_draw(streams_of[5], (2, D, H, BLK), D ** -0.5, 0.125, ((3, 4),))
    conv_w = bell_draw(streams_of[6], (CW, H, BLK), 0.5, 3.0, ((2, 4),))
    conv_b = bell_draw(streams_of[7], (H, BLK), 0.3, 2.0, ((1, 4),))
    gate_w = bell_draw(streams_of[8], (2, H, BLK, BLK), BLK ** -0.5, 0.375, ((3, 4),))
    gate_b = bell_draw(streams_of[9], (2, H, BLK), 1.0, 3.0, ((2, 4),))
    a_param = jnp.clip(-9.0 + 5.0 * jax.random.uniform(streams_of[10], (H, BLK), jnp.float32) ** steps_of(streams_of[10], (H, BLK), ((1, 4),), -0.2, 0.2), -9.0, -4.0)
    w_out = bell_draw(streams_of[11], (H, BLK, D), (L // 8) ** -0.5, 0.3125, ((1, 4),))
    w_in = bell_draw(streams_of[12], (2, D, FF), D ** -0.5, 0.125, ((2, 4),))
    w_down = bell_draw(streams_of[13], (FF, D), (FF // 4) ** -0.5, 0.125, ((0, 4),))
    cotangent = bell_draw(streams_of[14], (TOKENS, D), 1.0, 6.0, ((0, 32), (1, 4)))
    return {"tokens": tokens, "seq_len": seq_len, "seq_owner": seq_owner, "gain_1": gain_1, "gain_2": gain_2, "w_xy": w_xy, "conv_w": conv_w, "conv_b": conv_b, "gate_w": gate_w, "gate_b": gate_b, "a_param": a_param, "w_out": w_out, "w_in": w_in, "w_down": w_down, "cotangent": cotangent}


HIGHEST = lax.Precision.HIGHEST
EPSILON = 1e-06

@jax.custom_vjp
def low(v):
    return lax.optimization_barrier(v.astype(jnp.bfloat16)).astype(jnp.float32)

@jax.custom_vjp
def low_back(v):
    return v

def low_keep(v):
    return (low(v), None)

def low_pass(kept, grad):
    return (grad,)

def back_keep(v):
    return (v, None)

def back_low(kept, grad):
    return (low(grad),)
low.defvjp(low_keep, low_pass)
low_back.defvjp(back_keep, back_low)

def gelu_tanh(value):
    return jax.nn.gelu(value, approximate=True)

def combine(earlier, later):
    return (earlier[0] * later[0], later[0] * earlier[1] + later[1])

def shift_rows(values, steps):
    if steps == 0:
        return values
    filler = jnp.zeros((steps,) + values.shape[1:], values.dtype)
    return jnp.concatenate([filler, values[:values.shape[0] - steps]], axis=0)

def tap_mask(segment, steps):
    filler = jnp.full((steps,), -1, jnp.int32)
    before = jnp.concatenate([filler, segment[:segment.shape[0] - steps]], axis=0)
    return (before == segment).astype(jnp.float32)[:, None]

def layout_of(seq_len, seq_owner, group_pos, capacity):
    seq_index = jnp.arange(seq_len.shape[0], dtype=jnp.int32)
    same_group = seq_owner[:, None] == seq_owner[None, :]
    earlier = same_group & (seq_index[None, :] < seq_index[:, None])
    offset = lax.optimization_barrier(jnp.sum(jnp.where(earlier, seq_len[None, :], 0), axis=1)).astype(jnp.int32)
    owned_here = seq_owner == group_pos
    total = jnp.sum(jnp.where(owned_here, seq_len, 0)).astype(jnp.int32)
    places = jnp.arange(capacity, dtype=jnp.int32)
    start = jnp.any(owned_here[:, None] & (offset[:, None] == places[None, :]), axis=0).astype(jnp.int32)
    valid = (places < total).astype(jnp.float32)
    return (start, valid)

def group_forward(rows, start, valid, params):
    gain_a, gain_b, w_xy, conv_w, conv_b, gate_w, gate_b, a_param, w_out, w_in, w_down = params
    segment = jnp.cumsum(start).astype(jnp.int32)
    keep = (1 - start).astype(jnp.float32)[:, None]
    is_start = (start == 1)[:, None]
    r_one = lax.rsqrt(lax.optimization_barrier(jnp.mean(rows * rows, axis=-1, keepdims=True)) + EPSILON)
    n_one = low(rows * r_one * gain_a)
    proj = low_back(jnp.einsum('td,kdc->ktc', n_one, w_xy.reshape(2, D, L), precision=HIGHEST))
    x_branch = proj[0]
    y_branch = proj[1]
    y_gelu = gelu_tanh(y_branch)
    taps_w = conv_w.reshape(CW, L)
    conv_f = conv_b.reshape(L)[None, :] + jnp.zeros_like(x_branch)
    for tap in range(CW):
        conv_f = conv_f + taps_w[tap][None, :] * shift_rows(x_branch, tap) * tap_mask(segment, tap)
    conv_low = low(conv_f)
    pre = low_back(jnp.einsum('thb,khbm->kthm', conv_low.reshape(GROUP_TOK, H, BLK), gate_w, precision=HIGHEST) + gate_b[:, None])
    gate_x = jax.nn.sigmoid(pre[0].reshape(GROUP_TOK, L))
    gate_a = jax.nn.sigmoid(pre[1].reshape(GROUP_TOK, L))
    log_a = -8.0 * gate_a * jax.nn.softplus(a_param.reshape(L))[None, :]
    decay = jnp.exp(log_a)
    mult = jnp.where(is_start, 1.0, jnp.sqrt(jnp.maximum(1.0 - decay * decay, 0.01)))
    inflow = mult * gate_x * conv_low
    states = lax.associative_scan(combine, (decay * keep, inflow), axis=0)[1]
    mixed = low(states * y_gelu)
    rec = low_back(jnp.dot(mixed, w_out.reshape(L, D), precision=HIGHEST, preferred_element_type=jnp.float32))
    h_one = rows + rec
    r_two = lax.rsqrt(lax.optimization_barrier(jnp.mean(h_one * h_one, axis=-1, keepdims=True)) + EPSILON)
    n_two = low(h_one * r_two * gain_b)
    gate_up = low_back(jnp.einsum('td,kdf->ktf', n_two, w_in, precision=HIGHEST))
    hidden = low(gelu_tanh(gate_up[0]) * gate_up[1])
    mlp = jnp.dot(hidden, w_down, precision=HIGHEST, preferred_element_type=jnp.float32)
    return valid[:, None] * (h_one + mlp)

def reference(tokens, seq_len, seq_owner, gain_1, gain_2, w_xy, conv_w, conv_b, gate_w, gate_b, a_param, w_out, w_in, w_down, cotangent):
    groups = jnp.arange(N_REP, dtype=jnp.int32)
    starts, valids = jax.vmap(lambda gid: layout_of(seq_len, seq_owner, gid, GROUP_TOK))(groups)
    params = tuple((p.astype(jnp.float32) for p in (gain_1, gain_2, w_xy, conv_w, conv_b, gate_w, gate_b, a_param, w_out, w_in, w_down)))
    rows_all = tokens.astype(jnp.float32)

    def forward(rows_in, weights):
        grouped = rows_in.reshape(N_REP, GROUP_TOK, D)
        runner = jax.checkpoint(group_forward)

        def step(carry, item):
            return (carry, runner(item[0], item[1], item[2], weights))
        _, outs = lax.scan(step, jnp.zeros((), jnp.float32), (grouped, starts, valids))
        return outs.reshape(TOKENS, D)
    result, pull = jax.vjp(forward, rows_all, params)
    d_rows, d_params = pull(cotangent.astype(jnp.float32))
    return (result.astype(jnp.bfloat16), d_rows, d_params[0], d_params[1], d_params[2], d_params[3], d_params[4], d_params[5], d_params[6], d_params[7], d_params[8], d_params[9], d_params[10])
```

```python
import functools

import jax
import jax.numpy as jnp
from jax import lax
from jax.experimental import pallas as pl
from jax.experimental.pallas import tpu as pltpu
from jax.sharding import PartitionSpec as P

EPSILON = 1e-06

MESH = pl.DeviceIdType.MESH
VM = 60 * 2**20
GC = 0.7978845608028654

def gelu_parts(v):
    v2 = v * v
    t = jnp.tanh(GC * v * (1.0 + 0.044715 * v2))
    half = 0.5 * (1.0 + t)
    g = v * half
    dg = half + 0.5 * v * (1.0 - t * t) * (GC * (1.0 + 3 * 0.044715 * v2))
    return g, dg

def dot(a, b):
    return jnp.dot(a, b, preferred_element_type=jnp.float32)

def dot_nt(a, b):
    return lax.dot_general(a, b, (((1,), (1,)), ((), ())), preferred_element_type=jnp.float32)

def ffn_kernel(n2, dt, w_in, w_dn, hid, dg, du, mlp, dn2, am, ad):
    i = pl.program_id(0)
    @pl.when(i == 0)
    def _():
        am[...] = jnp.zeros_like(am)
        ad[...] = jnp.zeros_like(ad)
    gate = dot(n2[...], w_in[0])
    up = dot(n2[...], w_in[1])
    g, dgl = gelu_parts(gate)
    h = (g * up).astype(jnp.bfloat16)
    hid[0] = h
    dh = dot_nt(dt[...], w_dn[...])
    a = (dh * up * dgl).astype(jnp.bfloat16)
    b = (dh * g).astype(jnp.bfloat16)
    dg[0] = a
    du[0] = b
    am[...] += dot(h, w_dn[...])
    ad[...] += dot_nt(a, w_in[0])
    ad[...] += dot_nt(b, w_in[1])
    @pl.when(i == 2)
    def _():
        mlp[...] = am[...].astype(jnp.bfloat16)
        dn2[...] = ad[...].astype(jnp.bfloat16)

def ffn(n2, dt, w_in, w_dn):
    R, D = n2.shape
    T = 640
    nt = w_dn.shape[0] // T
    full = pl.BlockSpec((R, D), lambda i: (0, 0))
    tile = pl.BlockSpec((1, R, T), lambda i: (i, 0, 0))
    ch = jax.ShapeDtypeStruct((nt, R, T), jnp.bfloat16)
    rd = jax.ShapeDtypeStruct((R, D), jnp.bfloat16)
    return pl.pallas_call(
        ffn_kernel, grid=(nt,),
        in_specs=[full, full, pl.BlockSpec((2, D, T), lambda i: (0, 0, i)), pl.BlockSpec((T, D), lambda i: (i, 0))],
        out_specs=[tile, tile, tile, full, full],
        out_shape=[ch, ch, ch, rd, rd],
        scratch_shapes=[pltpu.VMEM((R, D), jnp.float32)] * 2,
        compiler_params=pltpu.CompilerParams(vmem_limit_bytes=VM),
        name="ffn",
    )(n2, dt, w_in, w_dn)

def coords():
    r = lax.axis_index("rep")
    f = lax.axis_index("fsdp")
    return r // 8, (r // 2) % 4, r % 2, f

def peer(axis, d):
    x, z, y, f = coords()
    if axis == "x":
        x = (x + d) % 4
    elif axis == "z":
        z = (z + d) % 4
    elif axis == "y":
        y = 1 - y
    else:
        f = f ^ d
    return ((x * 4 + z) * 2 + y, f)

class Grads:
    def __init__(self, plan, fplan):
        self.plan = plan
        self.fplan = fplan
    def scratch(self):
        n, m = len(self.plan), len(self.fplan)
        b = jnp.bfloat16
        return [
            pltpu.VMEM((n, 4, 256, 640), b),
            pltpu.VMEM((m, 4, 160, 1024), b),
            pltpu.VMEM((n, 4, 160, 640), b),
            pltpu.VMEM((n, 3, 160, 640), b),
            pltpu.VMEM((n, 2, 80, 640), b),
            pltpu.VMEM((n, 80, 640), b),
            pltpu.SemaphoreType.DMA((n, 3)), pltpu.SemaphoreType.DMA((n, 3)),
            pltpu.SemaphoreType.DMA((m, 3)), pltpu.SemaphoreType.DMA((m, 3)),
            pltpu.SemaphoreType.DMA((n, 3)), pltpu.SemaphoreType.DMA((n, 3)),
            pltpu.SemaphoreType.DMA((n,)), pltpu.SemaphoreType.DMA((n,)),
            pltpu.SemaphoreType.DMA((n,)), pltpu.SemaphoreType.DMA((m,)),
        ]
    def bind(self, refs, usrc, fsrc, out):
        (self.ub, self.ft, self.st, self.rr, self.tt, self.yr, self.us, self.ur, self.fs, self.fr,
         self.rq, self.rv, self.ys, self.yv, self.lu, self.lf) = refs
        self.usrc, self.fsrc, self.out = usrc, fsrc, out
    def rc(self, src, dst, s, r, axis, d):
        return pltpu.make_async_remote_copy(src_ref=src, dst_ref=dst, send_sem=s, recv_sem=r, device_id=peer(axis, d), device_id_type=MESH)
    def fcopies(self, k):
        i, axis = self.fplan[k]
        x, z, y, f = coords()
        src = self.fsrc[i]
        me = x if axis == "x" else z
        pick = (lambda t: src.at[t]) if axis == "x" else (lambda t: src.at[:, t])
        loc = pltpu.make_async_copy(pick(me), self.ft.at[k, :, :, pl.ds(0, 256)], self.lf.at[k])
        rem = [self.rc(pick((me + d) % 4), self.ft.at[k, :, :, pl.ds(d * 256, 256)], self.fs.at[k, d - 1], self.fr.at[k, d - 1], axis, d) for d in (1, 3, 2)]
        return loc, rem
    def ucopies(self, c):
        k, axis = self.plan[c]
        src = self.usrc(c)
        loc = pltpu.make_async_copy(src, self.ub.at[c, 0], self.lu.at[c])
        rem = [self.rc(src, self.ub.at[c, d], self.us.at[c, d - 1], self.ur.at[c, d - 1], axis, d) for d in (1, 3, 2)]
        return loc, rem
    def rscopies(self, c):
        k, axis = self.plan[c]
        ra = "z" if axis == "x" else "x"
        x, z, y, f = coords()
        me = z if axis == "x" else x
        return me, [self.rc(self.st.at[c, (me + d) % 4], self.rr.at[c, d - 1], self.rq.at[c, d - 1], self.rv.at[c, d - 1], ra, d) for d in (1, 3, 2)]
    def ycopy(self, c):
        x, z, y, f = coords()
        return self.rc(self.tt.at[c, 1 - y], self.yr.at[c], self.ys.at[c], self.yv.at[c], "y", 0)
    def send_f(self, k):
        loc, rem = self.fcopies(k)
        loc.start()
        for r in rem: r.start()
    def send_u(self, c):
        loc, rem = self.ucopies(c)
        loc.start()
        for r in rem: r.start()
    def mm(self, c):
        k, axis = self.plan[c]
        loc, rem = self.ucopies(c)
        loc.wait()
        for r in rem: r.wait()
        if not self.fdone[k]:
            loc, rem = self.fcopies(k)
            loc.wait()
            for r in rem: r.wait()
            self.fdone[k] = True
        self.st[c] = dot(self.ft[k].reshape(640, 1024), self.ub[c].reshape(1024, 640)).astype(jnp.bfloat16).reshape(4, 160, 640)
        me, cps = self.rscopies(c)
        for r in cps: r.start()
    def rs(self, c):
        me, cps = self.rscopies(c)
        for r in cps: r.wait()
        f = jnp.float32
        t = (self.st[c, me].astype(f) + self.rr[c, 0].astype(f)) + (self.rr[c, 1].astype(f) + self.rr[c, 2].astype(f))
        self.tt[c] = t.astype(jnp.bfloat16).reshape(2, 80, 640)
        self.ycopy(c).start()
    def fin(self, c):
        x, z, y, f = coords()
        self.ycopy(c).wait()
        self.out[c] = self.tt[c, y].astype(jnp.float32) + self.yr[c].astype(jnp.float32)

def entry_barrier(peers):
    b = pltpu.get_barrier_semaphore()
    for axis, d in peers:
        pl.semaphore_signal(b, inc=1, device_id=peer(axis, d), device_id_type=MESH)
    pl.semaphore_wait(b, len(peers))

REP = [("x", 1), ("x", 2), ("x", 3), ("z", 1), ("z", 2), ("z", 3), ("y", 1)]

PLAN = [(0, "x")] * 6 + [(1, "z")] * 3 + [(2, "x"), (3, "z"), (4, "z")]
FPLAN = [(0, "x"), (1, "z"), (2, "x"), (2, "z"), (3, "z")]

def grads_kernel(g, n2t, dtt, n1t, drt, dgs, dus, hids, dxs, zs, out, *refs):
    def usrc(c):
        if c < 3: return dgs.at[c]
        if c < 6: return dus.at[c - 3]
        if c < 9: return hids.at[c - 6]
        if c < 11: return dxs.at[c - 9]
        return zs
    g.bind(refs, usrc, [n2t, dtt, n1t, drt], out)
    g.fdone = [False] * len(g.fplan)
    entry_barrier(REP)
    g.send_f(0); g.send_f(1)
    order = [0, 6, 1, 3, 7, 2, 4, 8, 5, 9, 10, 11]
    for j, c in enumerate(order):
        if j == 6:
            for k in (2, 3, 4): g.send_f(k)
        g.send_u(c)
    n = len(order)
    for j in range(n + 4):
        if j < n: g.mm(order[j])
        if 0 <= j - 2 < n: g.rs(order[j - 2])
        if 0 <= j - 4 < n: g.fin(order[j - 4])

def grads(n2t, dtt, n1t, drt, dgs, dus, hids, dxs, zs):
    g = Grads(PLAN, FPLAN)
    return pl.pallas_call(
        functools.partial(grads_kernel, g),
        out_shape=jax.ShapeDtypeStruct((12, 80, 640), jnp.float32),
        in_specs=[pl.BlockSpec(memory_space=pl.ANY)] * 9,
        out_specs=pl.BlockSpec(memory_space=pltpu.VMEM),
        scratch_shapes=g.scratch(),
        compiler_params=pltpu.CompilerParams(collective_id=7, has_side_effects=True, vmem_limit_bytes=VM),
        name="grads",
    )(n2t, dtt, n1t, drt, dgs, dus, hids, dxs, zs)


def gather_turned(arrays, axis, dims):
    turned = [jnp.moveaxis(a, dim, 0) for a, dim in zip(arrays, dims)]
    widths = [t[0].size for t in turned]
    both = jnp.concatenate([t.reshape(-1, w) for t, w in zip(turned, widths)], axis=1)
    filled = lax.all_gather(both, axis, axis=0, tiled=True)
    pieces = jnp.split(filled, [sum(widths[:k]) for k in range(1, len(widths))], axis=1)
    return tuple(
        (
            jnp.moveaxis(b.reshape(-1, *t.shape[1:]), 0, dim)
            for b, t, dim in zip(pieces, turned, dims)
        )
    )


def from_everyone(value, axis):
    devices = lax.axis_size(axis)
    return lax.all_to_all(
        jnp.broadcast_to(value[None], (devices, *value.shape)), axis, 0, 0, tiled=True
    )


def in_order(pieces, dim):
    dims = list(pieces.shape[1:])
    dims[dim] *= pieces.shape[0]
    return jnp.moveaxis(pieces, 0, dim).reshape(dims)


def gather_directly(value, axis, dim):
    pieces = from_everyone(value, axis)
    return in_order(pieces, dim)


def padded_to(lines, devices):
    spare = -len(lines) % devices
    return jnp.pad(lines, [(0, spare)] + [(0, 0)] * (lines.ndim - 1))


def sum_in_two_steps(value, axis):
    lines = value.reshape(-1, *value.shape[1:][-1:])
    padded = padded_to(lines, lax.axis_size(axis))
    own = lax.psum_scatter(padded, axis, scatter_dimension=0, tiled=True)
    whole = lax.all_gather(own, axis, axis=0, tiled=True)
    return whole[: len(lines)].reshape(value.shape)


def in_blocks(value, dim, devices):
    dims = value.shape
    pieces = value.reshape(*dims[:dim], devices, dims[dim] // devices, *dims[dim + 1 :])
    return jnp.moveaxis(pieces, dim, 0)


def sum_at_owner(value, axis, dim):
    pieces = in_blocks(value, dim, lax.axis_size(axis))
    arrived = lax.all_to_all(pieces, axis, split_axis=0, concat_axis=0, tiled=True)
    return arrived.astype(jnp.float32).sum(axis=0)


def taken_together(value, axis):
    everything = from_everyone(value, axis)
    return jnp.sum(everything, axis=0)


def sum_packed(arrays, axis, dims):
    devices = lax.axis_size(axis)
    pieces = [in_blocks(a, dim, devices) for a, dim in zip(arrays, dims)]
    lines = jnp.concatenate([b.reshape(devices, -1) for b in pieces], axis=1)
    span = max(16, -(-lines.shape[1] // 1024) * 8)
    lines = jnp.pad(lines, ((0, 0), (0, span * 128 - lines.shape[1]))).reshape(-1, 128)
    line, at, outs = (lax.psum_scatter(lines, axis, tiled=True).reshape(-1), 0, [])
    for b in pieces:
        part = b[0]
        outs.append(line[at : at + part.size].reshape(part.shape))
        at += part.size
    return tuple(outs)


def in_one(arrays, axis):
    ends = [0]
    for a in arrays:
        ends.append(ends[-1] + a.size)
    running = taken_together(jnp.concatenate([a.ravel() for a in arrays]), axis)
    return tuple((running[b:e].reshape(a.shape) for a, b, e in zip(arrays, ends, ends[1:])))


def gelu_tanh(value):
    return jax.nn.gelu(value, approximate=True)


def combine(earlier, later):
    return (earlier[0] * later[0], later[0] * earlier[1] + later[1])


def shift_rows(values, steps):
    if steps == 0:
        return values
    filler = jnp.zeros((steps,) + values.shape[1:], values.dtype)
    return jnp.concatenate([filler, values[: values.shape[0] - steps]], axis=0)


def lift_rows(values, steps):
    if steps == 0:
        return values
    filler = jnp.zeros((steps,) + values.shape[1:], values.dtype)
    return jnp.concatenate([values[steps:], filler], axis=0)


def tap_mask(segment, steps):
    filler = jnp.full((steps,), -1, jnp.int32)
    before = jnp.concatenate([filler, segment[: segment.shape[0] - steps]], axis=0)
    return (before == segment).astype(jnp.float32)[:, None]


def layout_of(seq_len, seq_owner, group_pos, capacity):
    seq_index = jnp.arange(seq_len.shape[0], dtype=jnp.int32)
    same_group = seq_owner[:, None] == seq_owner[None, :]
    earlier = same_group & (seq_index[None, :] < seq_index[:, None])
    offset = jnp.sum(jnp.where(earlier, seq_len[None, :], 0), axis=1)
    owned_here = seq_owner == group_pos
    total = jnp.sum(jnp.where(owned_here, seq_len, 0))
    places = jnp.arange(capacity, dtype=jnp.int32)
    start = jnp.any(owned_here[:, None] & (offset[:, None] == places[None, :]), axis=0).astype(
        jnp.int32
    )
    valid = (places < total).astype(jnp.float32)
    return (start, valid)


def body(
    tokens,
    seq_len,
    seq_owner,
    gain_1,
    gain_2,
    w_xy,
    conv_w,
    conv_b,
    gate_w,
    gate_b,
    a_param,
    w_out,
    w_in,
    w_down,
    cotangent,
):
    group_pos = lax.axis_index("rep")
    fsdp_pos = lax.axis_index("fsdp")
    capacity = tokens.shape[0]
    width_own = tokens.shape[1]
    width = width_own * lax.axis_size("fsdp")
    heads = w_xy.shape[2]
    block_own = w_xy.shape[3]
    channels = heads * block_own
    tap_count = conv_w.shape[0]
    start, valid = layout_of(seq_len, seq_owner, group_pos, capacity)
    segment = jnp.cumsum(start)
    keep = (1 - start).astype(jnp.float32)[:, None]
    is_start = (start == 1)[:, None]
    live = valid[:, None]
    rows, gain_one, gain_two = gather_turned((tokens, gain_1, gain_2), "fsdp", (1, 0, 0))
    rows_f = rows.astype(jnp.float32)
    gain_one_f = gain_one.astype(jnp.float32)
    gain_two_f = gain_two.astype(jnp.float32)
    r_one = lax.rsqrt(jnp.mean(rows_f * rows_f, axis=-1, keepdims=True) + EPSILON)
    n_one = (rows_f * r_one * gain_one_f).astype(jnp.bfloat16)
    w_pair = w_xy.reshape(2, width, channels)
    proj = jnp.einsum("td,kdc->ktc", n_one, w_pair, preferred_element_type=jnp.float32)
    x_branch = proj[0]
    y_branch = proj[1]
    y_gelu = gelu_tanh(y_branch)
    taps_w = conv_w.astype(jnp.float32).reshape(tap_count, channels)
    masks = [tap_mask(segment, tap) for tap in range(tap_count)]
    conv_f = conv_b.astype(jnp.float32).reshape(channels)[None, :] + jnp.zeros_like(x_branch)
    for tap in range(tap_count):
        conv_f = conv_f + taps_w[tap][None, :] * shift_rows(x_branch, tap) * masks[tap]
    conv_low = conv_f.astype(jnp.bfloat16)
    conv_full = gather_directly(conv_low.reshape(capacity, heads, block_own), "fsdp", 2)
    pre = jnp.einsum("thb,khbm->kthm", conv_full, gate_w, preferred_element_type=jnp.float32)
    pre = pre + gate_b.astype(jnp.float32)[:, None]
    gate_x = jax.nn.sigmoid(pre[0].reshape(capacity, channels))
    gate_a = jax.nn.sigmoid(pre[1].reshape(capacity, channels))
    decay_raw = a_param.reshape(channels)
    soft_decay = jax.nn.softplus(decay_raw)[None, :]
    decay = jnp.exp(-8.0 * gate_a * soft_decay)
    spread = 1.0 - decay * decay
    mult = jnp.where(is_start, 1.0, jnp.sqrt(jnp.maximum(spread, 0.01)))
    conv_v = conv_low.astype(jnp.float32)
    inflow = mult * gate_x * conv_v
    coeffs = decay * keep
    states = lax.associative_scan(combine, (coeffs, inflow), axis=0)[1]
    mixed = (states * y_gelu).astype(jnp.bfloat16)
    w_out_flat = w_out.reshape(channels, width)
    rec = sum_in_two_steps(jnp.dot(mixed, w_out_flat, preferred_element_type=jnp.float32), "fsdp")
    h_one = rows_f + rec
    r_two = lax.rsqrt(jnp.mean(h_one * h_one, axis=-1, keepdims=True) + EPSILON)
    n_two = (h_one * r_two * gain_two_f).astype(jnp.bfloat16)
    grad_rows = gather_directly(cotangent, "fsdp", 1)
    d_top = grad_rows.astype(jnp.float32) * live
    d_top_low = d_top.astype(jnp.bfloat16)
    hid_t, dg_t, du_t, mlp_low, dn2_low = ffn(n_two, d_top_low, w_in, w_down)
    mlp = sum_at_owner(mlp_low, "fsdp", 1)
    d_n_two = lax.psum(dn2_low.astype(jnp.float32), "fsdp")
    h_own = lax.dynamic_slice_in_dim(h_one, fsdp_pos * width_own, width_own, 1)
    block_out = (live * (h_own + mlp)).astype(jnp.bfloat16)
    d_gain_two_all = jnp.sum(d_n_two * h_one * r_two, axis=0)
    v_two = d_n_two * gain_two_f
    d_h_one = (
        d_top + r_two * v_two - h_one * r_two**3 * jnp.mean(v_two * h_one, axis=-1, keepdims=True)
    )
    d_rec = d_h_one.astype(jnp.bfloat16)
    d_mixed = jnp.einsum("td,cd->tc", d_rec, w_out_flat, preferred_element_type=jnp.float32)
    d_states = d_mixed * y_gelu
    _, ygelu_pull = jax.vjp(gelu_tanh, y_branch)
    d_y_branch = ygelu_pull(d_mixed * states)[0]
    coeff_next = lift_rows(coeffs, 1)
    flipped = lax.associative_scan(
        combine, (jnp.flip(coeff_next, 0), jnp.flip(d_states, 0)), axis=0
    )[1]
    d_inflow = jnp.flip(flipped, 0)
    states_prev = shift_rows(states, 1)
    mult_slope = jnp.where(is_start | (spread <= 0.01), 0.0, -decay / mult)
    d_decay = d_inflow * states_prev * keep + d_inflow * gate_x * conv_v * mult_slope
    d_gate_x = d_inflow * mult * conv_v
    d_conv = d_inflow * mult * gate_x
    d_log = d_decay * decay
    d_decay_param = jnp.sum(d_log * (-8.0 * gate_a), axis=0) * jax.nn.sigmoid(decay_raw)
    d_pre_x = d_gate_x * gate_x * (1.0 - gate_x)
    d_pre_a = -8.0 * d_log * soft_decay * gate_a * (1.0 - gate_a)
    d_pre = (
        jnp.stack([d_pre_x, d_pre_a]).reshape(2, capacity, heads, block_own).astype(jnp.bfloat16)
    )
    d_gate_b = jnp.sum(d_pre.astype(jnp.float32), axis=1)
    d_gate_w = jnp.einsum("thb,kthm->khbm", conv_full, d_pre, preferred_element_type=jnp.float32)
    d_blocks = jnp.einsum("kthm,khbm->thb", d_pre, gate_w, preferred_element_type=jnp.float32)
    d_conv = d_conv + sum_at_owner(d_blocks.astype(jnp.bfloat16), "fsdp", 2).reshape(
        capacity, channels
    )
    d_conv_b = jnp.sum(d_conv, axis=0)
    d_conv_taps = []
    d_x_branch = jnp.zeros_like(x_branch)
    for tap in range(tap_count):
        masked = d_conv * masks[tap]
        d_conv_taps.append(jnp.sum(masked * shift_rows(x_branch, tap), axis=0))
        d_x_branch = d_x_branch + taps_w[tap][None, :] * lift_rows(masked, tap)
    d_conv_w = jnp.stack(d_conv_taps)
    d_pair = jnp.stack([d_x_branch, d_y_branch]).astype(jnp.bfloat16)
    d_n_one_part = jnp.einsum("ktc,kdc->td", d_pair, w_pair, preferred_element_type=jnp.float32)
    gain_one_own = lax.dynamic_slice_in_dim(gain_one_f, fsdp_pos * width_own, width_own, 0)
    rows_own = lax.dynamic_slice_in_dim(rows_f, fsdp_pos * width_own, width_own, 1)
    d_h_own = lax.dynamic_slice_in_dim(d_h_one, fsdp_pos * width_own, width_own, 1)
    d_n_one = sum_at_owner(d_n_one_part.astype(jnp.bfloat16), "fsdp", 1)
    v_one = d_n_one * gain_one_own
    row_stat = taken_together(jnp.sum(v_one * rows_own, axis=-1, keepdims=True), "fsdp")
    d_tokens = d_h_own + r_one * v_one - rows_own * r_one**3 * row_stat / width
    d_gain_one = jnp.sum(d_n_one * rows_own * r_one, axis=0)
    d_gain_two = lax.dynamic_slice_in_dim(d_gain_two_all, fsdp_pos * width_own, width_own, 0)
    turned = lambda v: v.T.reshape(4, 4, 160, 256)
    red = grads(
        turned(n_two), turned(d_top_low), turned(n_one), turned(d_rec), dg_t, du_t, hid_t, d_pair, mixed
    )
    cols = lambda v: jnp.moveaxis(v, 0, 1).reshape(80, -1)
    red_w_in = jnp.stack([cols(red[0:3]), cols(red[3:6])])
    red_w_down = cols(red[6:9]).T
    red_w_xy = red[9:11].reshape(2, 80, heads, block_own)
    red_w_out = red[11].T.reshape(heads, block_own, 80)
    gate_lines = jnp.moveaxis(d_gate_w, 2, 0).reshape(256, -1).astype(jnp.bfloat16)
    gate_own = lax.psum_scatter(gate_lines, "rep", scatter_dimension=0, tiled=True)
    red_gate_w = jnp.moveaxis(gate_own.astype(jnp.float32).reshape(8, 2, heads, block_own), 0, 2)
    sum_g1, sum_g2, sum_conv_w, sum_conv_b, sum_gate_b, sum_decay = in_one(
        (
            d_gain_one,
            d_gain_two,
            d_conv_w.reshape(tap_count, heads, block_own),
            d_conv_b.reshape(heads, block_own),
            d_gate_b,
            d_decay_param.reshape(heads, block_own),
        ),
        "rep",
    )
    return (
        block_out,
        d_tokens,
        sum_g1,
        sum_g2,
        red_w_xy,
        sum_conv_w,
        sum_conv_b,
        red_gate_w,
        sum_gate_b,
        sum_decay,
        red_w_out,
        red_w_in,
        red_w_down,
    )


def solution(mesh):
    return jax.shard_map(
        body,
        mesh=mesh,
        in_specs=(
            P("rep", "fsdp"),
            P(),
            P(),
            P("fsdp"),
            P("fsdp"),
            P(None, None, None, "fsdp"),
            P(None, None, "fsdp"),
            P(None, "fsdp"),
            P(None, None, None, "fsdp"),
            P(None, None, "fsdp"),
            P(None, "fsdp"),
            P(None, "fsdp", None),
            P(None, None, "fsdp"),
            P("fsdp", None),
            P("rep", "fsdp"),
        ),
        out_specs=(
            P("rep", "fsdp"),
            P("rep", "fsdp"),
            P("fsdp"),
            P("fsdp"),
            P(None, "rep", None, "fsdp"),
            P(None, None, "fsdp"),
            P(None, "fsdp"),
            P(None, None, "rep", "fsdp"),
            P(None, None, "fsdp"),
            P(None, "fsdp"),
            P(None, "fsdp", "rep"),
            P(None, "rep", "fsdp"),
            P("fsdp", "rep"),
        ),
        check_vma=False,
    )
```

```python
import functools

import jax
import jax.numpy as jnp
from jax import lax
from jax.experimental import pallas as pl
from jax.experimental.pallas import tpu as pltpu
from jax.sharding import PartitionSpec as P

MESH = pl.DeviceIdType.MESH
VM = 60 * 2**20
GC = 0.7978845608028654

def gelu_parts(v):
    v2 = v * v
    t = jnp.tanh(GC * v * (1.0 + 0.044715 * v2))
    half = 0.5 * (1.0 + t)
    g = v * half
    dg = half + 0.5 * v * (1.0 - t * t) * (GC * (1.0 + 3 * 0.044715 * v2))
    return g, dg

def dot(a, b):
    return jnp.dot(a, b, preferred_element_type=jnp.float32)

def dot_nt(a, b):
    return lax.dot_general(a, b, (((1,), (1,)), ((), ())), preferred_element_type=jnp.float32)

def ffn_kernel(n2, dt, w_in, w_dn, hid, dg, du, mlp, dn2, n2t, dtt, am, ad):
    i = pl.program_id(0)
    @pl.when(i == 1)
    def _():
        for c in range(4):
            n2t[c] = n2[:, c * 640:c * 640 + 640].T.reshape(4, 160, 256)
            dtt[c] = dt[:, c * 640:c * 640 + 640].T.reshape(4, 160, 256)
    @pl.when(i == 0)
    def _():
        am[...] = jnp.zeros_like(am)
        ad[...] = jnp.zeros_like(ad)
    gate = dot(n2[...], w_in[0])
    up = dot(n2[...], w_in[1])
    g, dgl = gelu_parts(gate)
    h = (g * up).astype(jnp.bfloat16)
    hid[0] = h
    dh = dot_nt(dt[...], w_dn[...])
    a = (dh * up * dgl).astype(jnp.bfloat16)
    b = (dh * g).astype(jnp.bfloat16)
    dg[0] = a
    du[0] = b
    am[...] += dot(h, w_dn[...])
    ad[...] += dot_nt(a, w_in[0])
    ad[...] += dot_nt(b, w_in[1])
    @pl.when(i == 2)
    def _():
        for c in range(4):
            mlp[c] = am[:, c * 640:c * 640 + 640].astype(jnp.bfloat16).reshape(4, 64, 640)
            dn2[c] = ad[:, c * 640:c * 640 + 640].astype(jnp.bfloat16).reshape(4, 64, 640)

def ffn(n2, dt, w_in, w_dn):
    R, D = n2.shape
    T = 640
    nt = w_dn.shape[0] // T
    full = pl.BlockSpec((R, D), lambda i: (0, 0))
    tile = pl.BlockSpec((1, R, T), lambda i: (i, 0, 0))
    ch = jax.ShapeDtypeStruct((nt, R, T), jnp.bfloat16)
    rd = jax.ShapeDtypeStruct((4, 4, 64, 640), jnp.bfloat16)
    td = jax.ShapeDtypeStruct((4, 4, 160, 256), jnp.bfloat16)
    part = pl.BlockSpec((4, 4, 64, 640), lambda i: (0, 0, 0, 0))
    turned = pl.BlockSpec((4, 4, 160, 256), lambda i: (0, 0, 0, 0))
    return pl.pallas_call(
        ffn_kernel, grid=(nt,),
        in_specs=[full, full, pl.BlockSpec((2, D, T), lambda i: (0, 0, i)), pl.BlockSpec((T, D), lambda i: (i, 0))],
        out_specs=[tile, tile, tile, part, part, turned, turned],
        out_shape=[ch, ch, ch, rd, rd, td, td],
        scratch_shapes=[pltpu.VMEM((R, D), jnp.float32)] * 2,
        compiler_params=pltpu.CompilerParams(vmem_limit_bytes=VM),
        name="ffn",
    )(n2, dt, w_in, w_dn)

def coords():
    r = lax.axis_index("rep")
    f = lax.axis_index("fsdp")
    return r // 8, (r // 2) % 4, r % 2, f

def peer(axis, d):
    x, z, y, f = coords()
    if axis == "x":
        x = (x + d) % 4
    elif axis == "z":
        z = (z + d) % 4
    elif axis == "y":
        y = 1 - y
    else:
        f = (f + d) % 4
    return ((x * 4 + z) * 2 + y, f)

class Grads:
    def __init__(self, plan, fplan):
        self.plan = plan
        self.fplan = fplan
    def scratch(self):
        n, m = len(self.plan), len(self.fplan)
        b = jnp.bfloat16
        return [
            pltpu.VMEM((n, 4, 256, 640), b),
            pltpu.VMEM((m, 4, 160, 1024), b),
            pltpu.VMEM((n, 4, 160, 640), b),
            pltpu.VMEM((n, 3, 160, 640), b),
            pltpu.VMEM((n, 2, 80, 640), b),
            pltpu.VMEM((n, 80, 640), b),
            pltpu.SemaphoreType.DMA((n, 3)), pltpu.SemaphoreType.DMA((n, 3)),
            pltpu.SemaphoreType.DMA((m, 3)), pltpu.SemaphoreType.DMA((m, 3)),
            pltpu.SemaphoreType.DMA((n, 3)), pltpu.SemaphoreType.DMA((n, 3)),
            pltpu.SemaphoreType.DMA((n,)), pltpu.SemaphoreType.DMA((n,)),
            pltpu.SemaphoreType.DMA((n,)), pltpu.SemaphoreType.DMA((m,)),
        ]
    def bind(self, refs, usrc, fsrc, out):
        (self.ub, self.ft, self.st, self.rr, self.tt, self.yr, self.us, self.ur, self.fs, self.fr,
         self.rq, self.rv, self.ys, self.yv, self.lu, self.lf) = refs
        self.usrc, self.fsrc, self.out = usrc, fsrc, out
    def rc(self, src, dst, s, r, axis, d):
        return pltpu.make_async_remote_copy(src_ref=src, dst_ref=dst, send_sem=s, recv_sem=r, device_id=peer(axis, d), device_id_type=MESH)
    def fcopies(self, k):
        i, axis = self.fplan[k]
        x, z, y, f = coords()
        src = self.fsrc[i]
        me = x if axis == "x" else z
        pick = (lambda t: src.at[t]) if axis == "x" else (lambda t: src.at[:, t])
        loc = pltpu.make_async_copy(pick(me), self.ft.at[k, :, :, pl.ds(0, 256)], self.lf.at[k])
        rem = [self.rc(pick((me + d) % 4), self.ft.at[k, :, :, pl.ds(d * 256, 256)], self.fs.at[k, d - 1], self.fr.at[k, d - 1], axis, d) for d in (1, 3, 2)]
        return loc, rem
    def ucopies(self, c):
        k, axis = self.plan[c]
        src = self.usrc(c)
        loc = pltpu.make_async_copy(src, self.ub.at[c, 0], self.lu.at[c])
        rem = [self.rc(src, self.ub.at[c, d], self.us.at[c, d - 1], self.ur.at[c, d - 1], axis, d) for d in (1, 3, 2)]
        return loc, rem
    def rscopies(self, c):
        k, axis = self.plan[c]
        ra = "z" if axis == "x" else "x"
        x, z, y, f = coords()
        me = z if axis == "x" else x
        return me, [self.rc(self.st.at[c, (me + d) % 4], self.rr.at[c, d - 1], self.rq.at[c, d - 1], self.rv.at[c, d - 1], ra, d) for d in (1, 3, 2)]
    def ycopy(self, c):
        x, z, y, f = coords()
        return self.rc(self.tt.at[c, 1 - y], self.yr.at[c], self.ys.at[c], self.yv.at[c], "y", 0)
    def send_f(self, k):
        loc, rem = self.fcopies(k)
        loc.start()
        for r in rem: r.start()
    def send_u(self, c):
        loc, rem = self.ucopies(c)
        loc.start()
        for r in rem: r.start()
    def mm(self, c):
        k, axis = self.plan[c]
        loc, rem = self.ucopies(c)
        loc.wait()
        for r in rem: r.wait()
        if not self.fdone[k]:
            loc, rem = self.fcopies(k)
            loc.wait()
            for r in rem: r.wait()
            self.fdone[k] = True
        self.st[c] = dot(self.ft[k].reshape(640, 1024), self.ub[c].reshape(1024, 640)).astype(jnp.bfloat16).reshape(4, 160, 640)
        me, cps = self.rscopies(c)
        for r in cps: r.start()
    def rs(self, c):
        me, cps = self.rscopies(c)
        for r in cps: r.wait()
        f = jnp.float32
        t = (self.st[c, me].astype(f) + self.rr[c, 0].astype(f)) + (self.rr[c, 1].astype(f) + self.rr[c, 2].astype(f))
        self.tt[c] = t.astype(jnp.bfloat16).reshape(2, 80, 640)
        self.ycopy(c).start()
    def fin(self, c):
        x, z, y, f = coords()
        self.ycopy(c).wait()
        self.out[c] = self.tt[c, y].astype(jnp.float32) + self.yr[c].astype(jnp.float32)

def entry_barrier(peers):
    b = pltpu.get_barrier_semaphore()
    for axis, d in peers:
        pl.semaphore_signal(b, inc=1, device_id=peer(axis, d), device_id_type=MESH)
    pl.semaphore_wait(b, len(peers))

REP = [("x", 1), ("x", 2), ("x", 3), ("z", 1), ("z", 2), ("z", 3), ("y", 1)]

PLAN = [(0, "x")] * 6 + [(1, "z")] * 3 + [(2, "x"), (3, "z"), (4, "z")]
FPLAN = [(0, "x"), (1, "z"), (2, "x"), (2, "z"), (3, "z")]

def grads_kernel(g, n2t, dtt, n1t, drt, dgs, dus, hids, dxs, zs, out, *refs):
    def usrc(c):
        if c < 3: return dgs.at[c]
        if c < 6: return dus.at[c - 3]
        if c < 9: return hids.at[c - 6]
        if c < 11: return dxs.at[c - 9]
        return zs
    g.bind(refs, usrc, [n2t, dtt, n1t, drt], out)
    g.fdone = [False] * len(g.fplan)
    entry_barrier(REP)
    g.send_f(0); g.send_f(1)
    order = [0, 6, 1, 3, 7, 2, 4, 8, 5, 9, 10, 11]
    for j, c in enumerate(order):
        if j == 6:
            for k in (2, 3, 4): g.send_f(k)
        g.send_u(c)
    n = len(order)
    for j in range(n + 4):
        if j < n: g.mm(order[j])
        if 0 <= j - 2 < n: g.rs(order[j - 2])
        if 0 <= j - 4 < n: g.fin(order[j - 4])

def grads(n2t, dtt, n1t, drt, dgs, dus, hids, dxs, zs):
    g = Grads(PLAN, FPLAN)
    return pl.pallas_call(
        functools.partial(grads_kernel, g),
        out_shape=jax.ShapeDtypeStruct((12, 80, 640), jnp.float32),
        in_specs=[pl.BlockSpec(memory_space=pl.ANY)] * 9,
        out_specs=pl.BlockSpec(memory_space=pltpu.VMEM),
        scratch_shapes=g.scratch(),
        compiler_params=pltpu.CompilerParams(collective_id=7, has_side_effects=True, vmem_limit_bytes=VM),
        name="grads",
    )(n2t, dtt, n1t, drt, dgs, dus, hids, dxs, zs)

F32 = jnp.float32
BF = jnp.bfloat16
EPS = 1e-06
ANY = pl.BlockSpec(memory_space=pl.ANY)
VMEM = pl.BlockSpec(memory_space=pltpu.VMEM)

def fpeer(d):
    r = lax.axis_index("rep")
    f = lax.axis_index("fsdp")
    h, c = f // 2, f % 2
    if d % 2:
        c = 1 - c
    if d // 2:
        h = 1 - h
    return r, h * 2 + c

class Comm:
    def __init__(self, ssem, rsem, lsem):
        self.ssem, self.rsem, self.lsem = ssem, rsem, lsem
        self.n = self.m = 0
        self.open = []
    def remote(self, src, dst, dev):
        k = self.n
        self.n += 1
        c = pltpu.make_async_remote_copy(src_ref=src, dst_ref=dst, send_sem=self.ssem.at[k], recv_sem=self.rsem.at[k], device_id=dev, device_id_type=MESH)
        c.start()
        self.open.append(c)
        return c
    def local(self, src, dst):
        k = self.m
        self.m += 1
        c = pltpu.make_async_copy(src, dst, self.lsem.at[k])
        c.start()
        return c
    def drain(self):
        for c in self.open:
            c.wait_send()
        self.open = []

class Gather:
    def __init__(self, comm, buf, own=None, parts=None):
        self.comm, self.buf = comm, buf
        self.f = lax.axis_index("fsdp")
        self.parts = parts or [()]
        self.own = own
        self.far, self.near = [], []
    def start(self):
        f, cm = self.f, self.comm
        for p in self.parts:
            dst = self.buf.at[(f, *p)]
            src = self.own.at[p] if self.own is not None else dst
            self.far.append(cm.remote(src, dst, fpeer(2)))
            self.near.append(cm.remote(src, dst, fpeer(1)))
    def relay(self):
        _, o = fpeer(2)
        self.late = []
        for p, c in zip(self.parts, self.far):
            c.wait_recv()
            dst = self.buf.at[(o, *p)]
            self.late.append(self.comm.remote(dst, dst, fpeer(1)))
    def finish(self):
        for c in self.near + self.late:
            c.wait_recv()

class Reduce:
    def __init__(self, comm, part, r1, s2, r2):
        self.comm, self.part, self.r1, self.s2, self.r2 = comm, part, r1, s2, r2
        self.f = lax.axis_index("fsdp")
        self.a, self.b, self.c = {}, {}, {}
    def send(self, c):
        _, o1 = fpeer(1)
        _, o3 = fpeer(3)
        self.a[c] = self.comm.remote(self.part.at[c, o3], self.r1.at[c, 1], fpeer(1))
        self.b[c] = self.comm.remote(self.part.at[c, o1], self.r1.at[c, 0], fpeer(1))
    def mid(self, c):
        _, o2 = fpeer(2)
        self.a[c].wait_recv()
        self.s2[c] = (self.part[c, o2].astype(F32) + self.r1[c, 1].astype(F32)).astype(BF)
        self.c[c] = self.comm.remote(self.s2.at[c], self.r2.at[c], fpeer(2))
    def fin(self, c):
        self.b[c].wait_recv()
        self.c[c].wait_recv()
        return self.part[c, self.f].astype(F32) + self.r1[c, 0].astype(F32) + self.r2[c].astype(F32)

def group_barrier(ds):
    b = pltpu.get_barrier_semaphore()
    for d in ds:
        pl.semaphore_signal(b, inc=1, device_id=fpeer(d), device_id_type=MESH)
    pl.semaphore_wait(b, len(ds))

def lanes(q):
    return slice(q * 128, q * 128 + 128)

def row_masks(lenc, ownc, ownr, msk):
    me = lax.axis_index("rep")
    ln = lenc[...]
    own = ownc[...] == me
    mine = jnp.where(own, ln, 0)
    j = lax.broadcasted_iota(jnp.int32, (128, 128), 0)
    i = lax.broadcasted_iota(jnp.int32, (128, 128), 1)
    offset = jnp.sum(jnp.where(j < i, mine, 0), axis=0, keepdims=True)
    total = jnp.sum(mine, axis=0, keepdims=True)
    place = lax.broadcasted_iota(jnp.int32, (256, 128), 0)
    hit = jnp.where((ownr[...] == me) & (offset == place), 1.0, 0.0)
    start = jnp.broadcast_to(jnp.max(hit, axis=1, keepdims=True), (256, 128))
    msk[0] = start
    run = start
    for k in (1, 2, 3):
        msk[k] = jnp.where((run == 0.0) & (place >= k), 1.0, 0.0)
        run = jnp.maximum(run, jnp.where(place >= k, pltpu.roll(start, k, axis=0), 0.0))
    msk[4] = jnp.where(place < total, 1.0, 0.0)

def wide_gates(gw, wg):
    row = lax.broadcasted_iota(jnp.int32, (128, 128), 0) // 64
    col = lax.broadcasted_iota(jnp.int32, (128, 128), 1) // 64
    for q in range(5):
        for k in range(2):
            for g in range(2):
                v = gw[k, q * 128:q * 128 + 128, g * 128:g * 128 + 128].astype(F32)
                r = pltpu.roll(v, 64, axis=1)
                for e in range(2):
                    twice = jnp.where(col == e, v, r)
                    p = 2 * g + e
                    wg[q, k * 128:k * 128 + 128, p * 128:p * 128 + 128] = jnp.where(row == col, twice, 0.0).astype(BF)

def softplus(v):
    return jnp.maximum(v, 0.0) + jnp.log(1.0 + jnp.exp(-jnp.abs(v)))

def sigmoid(v):
    return 1.0 / (1.0 + jnp.exp(-v))

def scan_rows(a_ref, u_ref, h_ref, back):
    rows = lax.broadcasted_iota(jnp.int32, (8, 640), 0)
    carry = jnp.zeros((1, 640), F32)
    order = range(31, -1, -1) if back else range(32)
    for i in order:
        a = a_ref[i * 8:i * 8 + 8, :]
        u = u_ref[i * 8:i * 8 + 8, :]
        for s in (1, 2, 4):
            if back:
                ok = rows < 8 - s
                a2 = jnp.where(ok, pltpu.roll(a, 8 - s, axis=0), 1.0)
                u2 = jnp.where(ok, pltpu.roll(u, 8 - s, axis=0), 0.0)
            else:
                ok = rows >= s
                a2 = jnp.where(ok, pltpu.roll(a, s, axis=0), 1.0)
                u2 = jnp.where(ok, pltpu.roll(u, s, axis=0), 0.0)
            u = u + a * u2
            a = a * a2
        h = u + a * carry
        h_ref[i * 8:i * 8 + 8, :] = h
        carry = h[0:1, :] if back else h[7:8, :]

def gate_values(q, pre, par, start):
    gx = sigmoid(pre[:, 0:128] + par[5:6, lanes(q)])
    ga = sigmoid(pre[:, 128:256] + par[6:7, lanes(q)])
    return gx, ga

def decay_of(q, ga, par, start):
    sp = softplus(par[7:8, lanes(q)])
    a = jnp.exp(-8.0 * ga * sp)
    spread = 1.0 - a * a
    mult = jnp.where(start == 1.0, 1.0, jnp.sqrt(jnp.maximum(spread, 0.01)))
    return sp, a, spread, mult

def forward_kernel(lenc, ownc, ownr, par, gn, tok, cot, w_t, gw_h, wo_h,
                   n1_o, cv_o, xb_o, yb_o, gx_o, ga_o, hs_o, z_o, n2_o, dt_o, h1_o, msk_o, r_o, g_o, wg_o, tk_o, n1t_o,
                   tkb, ctb, gnb, wv, gw, wo, wg, n1, dt, cvb, xb, yb, gx, ga, aa, uu, hs, z, msk, pt, r1, s2, r2, h1, n2b, rs1, rs2, n1t,
                   ssem, rsem, lsem):
    cm = Comm(ssem, rsem, lsem)
    f = lax.axis_index("fsdp")
    lw = [cm.local(w_t.at[0], wv.at[0]), cm.local(gw_h, gw), cm.local(w_t.at[1], wv.at[1]), cm.local(wo_h, wo)]
    lt = [cm.local(tok, tkb.at[f]), cm.local(gn, gnb.at[f]), cm.local(cot, ctb.at[f])]
    group_barrier((1, 2))
    halves = [(pl.ds(0, 128),), (pl.ds(128, 128),)]
    gtk = Gather(cm, tkb, tok, halves)
    ggn = Gather(cm, gnb, gn)
    gct = Gather(cm, ctb, cot)
    ggn.start()
    gtk.start()
    gct.start()
    row_masks(lenc, ownc, ownr, msk)
    lw[1].wait()
    wide_gates(gw, wg)
    outs = [cm.local(msk, msk_o), cm.local(wg, wg_o)]
    ggn.relay()
    gtk.relay()
    for c in lt:
        c.wait()
    ggn.finish()
    gtk.finish()
    @pl.loop(0, 16)
    def _(i):
        rows = pl.ds(pl.multiple_of(i * 16, 16), 16)
        xs = [tkb[p, rows, :].astype(F32) for p in range(4)]
        ss = sum(jnp.sum(x * x, axis=-1, keepdims=True) for x in xs)
        r = lax.rsqrt(ss * (1.0 / 2560) + EPS)
        rs1[rows, :] = jnp.broadcast_to(r, (16, 128))
        for p in range(4):
            n1[rows, p * 640:p * 640 + 640] = (xs[p] * r * gnb[p, 0:1, :]).astype(BF)
    outs += [cm.local(n1, n1_o), cm.local(gnb, g_o), cm.local(tkb, tk_o)]
    lw[0].wait()
    xb[...] = dot_nt(n1[...], wv[0])
    outs.append(cm.local(xb, xb_o))
    for q in range(5):
        x = xb[:, lanes(q)]
        acc = par[4:5, lanes(q)] + par[0:1, lanes(q)] * x
        for k in (1, 2, 3):
            acc = acc + par[k:k + 1, lanes(q)] * pltpu.roll(x, k, axis=0) * msk[k]
        cvb[f, :, lanes(q)] = acc.astype(BF)
    gcv = Gather(cm, cvb, None, halves)
    gcv.start()
    lw[2].wait()
    yb[...] = dot_nt(n1[...], wv[1])
    outs.append(cm.local(yb, yb_o))
    gct.relay()
    gcv.relay()
    for c in range(4):
        n1t[c] = n1[:, c * 640:c * 640 + 640].T.reshape(4, 160, 256)
    outs.append(cm.local(n1t, n1t_o))
    gcv.finish()
    outs.append(cm.local(cvb, cv_o))
    for q in range(5):
        lhs = jnp.concatenate([cvb[p, :, lanes(q)] for p in range(4)], axis=1)
        pre = dot_nt(lhs, wg[q])
        gxq, gaq = gate_values(q, pre, par, msk[0])
        sp, a, spread, mult = decay_of(q, gaq, par, msk[0])
        gx[:, lanes(q)] = gxq
        ga[:, lanes(q)] = gaq
        aa[:, lanes(q)] = jnp.where(msk[0] == 1.0, 0.0, a)
        uu[:, lanes(q)] = mult * gxq * cvb[f, :, lanes(q)].astype(F32)
    outs += [cm.local(gx, gx_o), cm.local(ga, ga_o)]
    scan_rows(aa, uu, hs, False)
    for q in range(5):
        yg, _ = gelu_parts(yb[:, lanes(q)])
        z[:, lanes(q)] = (hs[:, lanes(q)] * yg).astype(BF)
    outs += [cm.local(hs, hs_o), cm.local(z, z_o)]
    lw[3].wait()
    red = Reduce(cm, pt, r1, s2, r2)
    for c in range(4):
        pt[c] = dot(z[...], wo[:, c * 640:c * 640 + 640]).astype(BF).reshape(4, 64, 640)
        red.send(c)
        if c: red.mid(c - 1)
    red.mid(3)
    gct.finish()
    @pl.loop(0, 16)
    def _(i):
        rows = pl.ds(pl.multiple_of(i * 16, 16), 16)
        live = jnp.broadcast_to(msk[4, rows, 0:1], (16, 640))
        for p in range(4):
            dt[rows, p * 640:p * 640 + 640] = (ctb[p, rows, :].astype(F32) * live).astype(BF)
    outs.append(cm.local(dt, dt_o))
    own = pl.ds(pl.multiple_of(f * 64, 64), 64)
    ss = jnp.zeros((64, 1), F32)
    for c in range(4):
        h = tkb[c, own, :].astype(F32) + red.fin(c)
        h1[:, c * 640:c * 640 + 640] = h
        ss = ss + jnp.sum(h * h, axis=-1, keepdims=True)
    r = lax.rsqrt(ss * (1.0 / 2560) + EPS)
    rs2[...] = jnp.broadcast_to(r, (64, 128))
    for c in range(4):
        cs = slice(c * 640, c * 640 + 640)
        n2b[f, :, cs] = (h1[:, cs] * r * gnb[c, 1:2, :]).astype(BF)
    gn2 = Gather(cm, n2b, None, [(pl.ds(0, 32),), (pl.ds(32, 32),)])
    gn2.start()
    outs += [cm.local(h1, h1_o), cm.local(rs1, r_o.at[pl.ds(0, 256)]), cm.local(rs2, r_o.at[pl.ds(256, 64)])]
    gn2.relay()
    gn2.finish()
    outs.append(cm.local(n2b, n2_o))
    for c in outs:
        c.wait()
    cm.drain()

def forward(lenc, ownc, ownr, par, gn, tok, cot, w_t, gw_t, wo):
    s = jax.ShapeDtypeStruct
    R = 256
    fw = s((R, 640), F32)
    out_shape = [s((R, 2560), BF), s((4, R, 640), BF), fw, fw, fw, fw, fw, s((R, 640), BF), s((4, 64, 2560), BF), s((R, 2560), BF),
                 s((64, 2560), F32), s((5, R, 128), F32), s((320, 128), F32), s((4, 8, 640), F32), s((5, 256, 512), BF), s((4, R, 640), BF), s((4, 4, 160, 256), BF)]
    V = pltpu.VMEM
    f640 = V((R, 640), F32)
    scratch = [V((4, R, 640), BF), V((4, R, 640), BF), V((4, 8, 640), F32), V((2, 640, 2560), BF), V((2, 640, 256), BF), V((640, 2560), BF),
               V((5, 256, 512), BF), V((R, 2560), BF), V((R, 2560), BF), V((4, R, 640), BF), f640, f640, f640, f640, f640, f640, f640,
               V((R, 640), BF), V((5, R, 128), F32), V((4, 4, 64, 640), BF), V((4, 2, 64, 640), BF), V((4, 64, 640), BF), V((4, 64, 640), BF),
               V((64, 2560), F32), V((4, 64, 2560), BF), V((R, 128), F32), V((64, 128), F32), V((4, 4, 160, 256), BF),
               pltpu.SemaphoreType.DMA((48,)), pltpu.SemaphoreType.DMA((48,)), pltpu.SemaphoreType.DMA((32,))]
    return pl.pallas_call(
        forward_kernel, out_shape=out_shape,
        in_specs=[VMEM] * 5 + [ANY] * 5,
        out_specs=[ANY] * len(out_shape),
        scratch_shapes=scratch,
        compiler_params=pltpu.CompilerParams(collective_id=3, has_side_effects=True, vmem_limit_bytes=VM),
        name="forward",
    )(lenc, ownc, ownr, par, gn, tok, cot, w_t, gw_t, wo)

def prep(seq_len, seq_owner, gain_1, gain_2, w_xy, conv_w, conv_b, gate_w, gate_b, a_param, w_out):
    lenc = seq_len.reshape(128, 1)
    ownc = seq_owner.reshape(128, 1)
    ownr = seq_owner.reshape(1, 128)
    fl = lambda v: v.astype(F32).reshape(-1, 640)
    par = jnp.concatenate([fl(conv_w), fl(conv_b), fl(gate_b), fl(a_param)], axis=0)
    gn = jnp.pad(jnp.stack([gain_1, gain_2]).astype(F32), ((0, 6), (0, 0)))
    w_t = jnp.transpose(w_xy, (0, 2, 3, 1)).reshape(2, 640, 2560)
    gw_t = jnp.swapaxes(gate_w, 2, 3).reshape(2, 640, 256)
    return lenc, ownc, ownr, par, gn, w_t, gw_t, w_out.reshape(640, 2560)

def dot_tn(a, b):
    return lax.dot_general(a, b, (((0,), (0,)), ((), ())), preferred_element_type=jnp.float32)

class Swap:
    def __init__(self, comm, src, dst):
        f = lax.axis_index("fsdp")
        self.cps = []
        for d in (3, 2, 1):
            _, t = fpeer(d)
            self.cps.append(comm.remote(src.at[t], dst.at[f], fpeer(d)))
        self.own = comm.local(src.at[f], dst.at[f])
    def finish(self):
        self.own.wait()
        for c in self.cps:
            c.wait_recv()

def backward_kernel(par, mlp_h, dn2_h, cv_h, xb_h, yb_h, gx_h, ga_h, hs_h, msk_h, r_h, g_h, wg_h, tk_h, dt_h, h1_h, w_t, wo_h,
                    bo_o, dtok_o, dxy_o, dr_o, drt_o, sg_o, sm_o,
                    pm, pd, cv, xb, yb, gx, ga, hs, msk, rb, gnb, wg, tk, dtb, h1, wv, wo,
                    aa, uu, gg, dc1, dr, pb, dp, dxy, dna, dnp, dh1, bo, bob, dto, dtr, gs, gr, sm, sg, dob,
                    m1, m2, m3, d1, d2, d3, e1, e2, e3, f1, f2, f3,
                    ssem, rsem, lsem):
    cm = Comm(ssem, rsem, lsem)
    f = lax.axis_index("fsdp")
    own = pl.ds(pl.multiple_of(f * 64, 64), 64)
    ld = [cm.local(dn2_h.at[c], pd.at[c]) for c in range(4)]
    lh = [cm.local(h1_h, h1), cm.local(g_h, gnb), cm.local(r_h, rb), cm.local(dt_h.at[own], dtb), cm.local(msk_h, msk)]
    lm = [cm.local(mlp_h.at[c], pm.at[c]) for c in range(4)]
    lb = [cm.local(wo_h, wo), cm.local(yb_h, yb), cm.local(hs_h, hs), cm.local(ga_h, ga), cm.local(gx_h, gx), cm.local(cv_h, cv),
          cm.local(wg_h, wg), cm.local(xb_h, xb), cm.local(w_t, wv), cm.local(tk_h.at[:, own], tk)]
    group_barrier((1, 2, 3))
    rd = Reduce(cm, pd, d1, d2, d3)
    rm = Reduce(cm, pm, m1, m2, m3)
    for c in range(4):
        ld[c].wait()
        rd.send(c)
    for c in range(4):
        rd.mid(c)
    for c in range(4):
        lm[c].wait()
        rm.send(c)
    for c in lh:
        c.wait()
    gs[...] = jnp.zeros_like(gs)
    r2 = rb[256:320, 0:1]
    acc = jnp.zeros((64, 1), F32)
    for c in range(4):
        cs = slice(c * 640, c * 640 + 640)
        dn = rd.fin(c)
        h = h1[:, cs]
        gs[c, 1:2, :] = jnp.sum(dn * h * r2, axis=0, keepdims=True)
        v = dn * gnb[c, 1:2, :]
        dh1[:, cs] = v
        acc = acc + jnp.sum(v * h, axis=-1, keepdims=True)
    acc = acc * (1.0 / 2560) * (r2 * r2 * r2)
    for c in range(4):
        cs = slice(c * 640, c * 640 + 640)
        d = dtb[:, cs].astype(F32) + r2 * dh1[:, cs] - h1[:, cs] * acc
        dh1[:, cs] = d
        dr[f, :, cs] = d.astype(BF)
    gdr = Gather(cm, dr, None, [(pl.ds(0, 32),), (pl.ds(32, 32),)])
    gdr.start()
    for c in range(4):
        rm.mid(c)
    for c in lb:
        c.wait()
    gdr.relay()
    for q in range(5):
        sp, a, spread, mult = decay_of(q, ga[:, lanes(q)], par, msk[0])
        up = pltpu.roll(jnp.where(msk[0] == 1.0, 0.0, a), 255, axis=0)
        rows = lax.broadcasted_iota(jnp.int32, (256, 128), 0)
        aa[:, lanes(q)] = jnp.where(rows == 255, 0.0, up)
    gdr.finish()
    uu[...] = dot_nt(dr[...].reshape(256, 2560), wo[...])
    outs = [cm.local(dr, dr_o)]
    for q in range(5):
        yg, dgl = gelu_parts(yb[:, lanes(q)])
        dz = uu[:, lanes(q)]
        dxy[1, :, lanes(q)] = (dz * hs[:, lanes(q)] * dgl).astype(BF)
        uu[:, lanes(q)] = dz * yg
    scan_rows(aa, uu, gg, True)
    re = Reduce(cm, pb, e1, e2, e3)
    for q in range(5):
        ls = lanes(q)
        start = msk[0]
        gxq, gaq, g = gx[:, ls], ga[:, ls], gg[:, ls]
        sp, a, spread, mult = decay_of(q, gaq, par, start)
        cvq = cv[f, :, ls].astype(F32)
        prev = jnp.where(start == 1.0, 0.0, pltpu.roll(hs[:, ls], 1, axis=0))
        slope = jnp.where((start == 1.0) | (spread <= 0.01), 0.0, -a / mult)
        da = g * prev + g * gxq * cvq * slope
        dc1[:, ls] = g * mult * gxq
        dlog = da * a
        da_p = jnp.sum(dlog * (-8.0 * gaq), axis=0, keepdims=True) * sigmoid(par[7:8, ls])
        px = (g * mult * cvq * gxq * (1.0 - gxq)).astype(BF)
        pa = (-8.0 * dlog * sp * gaq * (1.0 - gaq)).astype(BF)
        dp[q, :, 0:128] = px
        dp[q, :, 128:256] = pa
        sm[7:8, ls] = jnp.sum(px.astype(F32), axis=0, keepdims=True)
        sm[8:9, ls] = jnp.sum(pa.astype(F32), axis=0, keepdims=True)
        sm[9:10, ls] = da_p
        db = dot(dp[q], wg[q]).astype(BF)
        for p in range(4):
            pb[q, p] = db[:, lanes(p)]
        re.send(q)
        if q: re.mid(q - 1)
    re.mid(4)
    for c in range(4):
        cs = slice(c * 640, c * 640 + 640)
        dna[c] = dot(dxy[1], wv[1, :, cs])
    low = lax.broadcasted_iota(jnp.int32, (64, 128), 1) < 64
    for q in range(5):
        lhs = jnp.concatenate([cv[p, :, lanes(q)] for p in range(4)], axis=1)
        gwt = dot_tn(lhs, dp[q])
        for p in range(4):
            for k in range(2):
                blk = gwt[p * 128:p * 128 + 128, k * 128:k * 128 + 128]
                sg[k, q, p] = jnp.where(low, blk[0:64], blk[64:128]).astype(BF)
    outs.append(cm.local(sg, sg_o))
    live = msk[4, own, 0:1]
    for c in range(4):
        bo[c] = (live * (h1[:, c * 640:c * 640 + 640] + rm.fin(c))).astype(BF)
    sbo = Swap(cm, bo, bob)
    for q in range(5):
        ls = lanes(q)
        d = dc1[:, ls] + re.fin(q)
        x = xb[:, ls]
        sm[6:7, ls] = jnp.sum(d, axis=0, keepdims=True)
        sm[2:3, ls] = jnp.sum(d * x, axis=0, keepdims=True)
        dx = par[0:1, ls] * d
        for k in (1, 2, 3):
            m = d * msk[k]
            sm[2 + k:3 + k, ls] = jnp.sum(m * pltpu.roll(x, k, axis=0), axis=0, keepdims=True)
            dx = dx + par[k:k + 1, ls] * pltpu.roll(m, 256 - k, axis=0)
        dxy[0, :, ls] = dx.astype(BF)
    outs.append(cm.local(dxy, dxy_o))
    rf = Reduce(cm, dnp, f1, f2, f3)
    for c in range(4):
        cs = slice(c * 640, c * 640 + 640)
        dnp[c] = (dna[c] + dot(dxy[0], wv[0, :, cs])).astype(BF).reshape(4, 64, 640)
        rf.send(c)
        if c: rf.mid(c - 1)
    rf.mid(3)
    for p in range(4):
        for o in range(4):
            pass
    drt = dr[...].reshape(256, 2560)
    for c in range(4):
        dtr[c] = drt[:, c * 640:c * 640 + 640].T.reshape(4, 160, 256)
    outs.append(cm.local(dtr, drt_o))
    r1 = rb[own, 0:1]
    acc = jnp.zeros((64, 1), F32)
    for c in range(4):
        dn = rf.fin(c)
        x = tk[c].astype(F32)
        gs[c, 0:1, :] = jnp.sum(dn * x * r1, axis=0, keepdims=True)
        v = dn * gnb[c, 0:1, :]
        dna[c, 0:64, :] = v
        acc = acc + jnp.sum(v * x, axis=-1, keepdims=True)
    acc = acc * (1.0 / 2560) * (r1 * r1 * r1)
    for c in range(4):
        dob[c] = (dh1[:, c * 640:c * 640 + 640] + r1 * dna[c, 0:64, :] - tk[c].astype(F32) * acc).astype(BF)
    sdt = Swap(cm, dob, dto)
    gcp = []
    for d in (3, 2, 1):
        _, t = fpeer(d)
        gcp.append(cm.remote(gs.at[t], gr.at[d - 1], fpeer(d)))
    sbo.finish()
    outs.append(cm.local(bob, bo_o))
    for c in gcp:
        c.wait_recv()
    sm[0:2, :] = (gs[f, 0:2, :] + gr[0, 0:2, :]) + (gr[1, 0:2, :] + gr[2, 0:2, :])
    sm[10:16, :] = jnp.zeros((6, 640), F32)
    outs.append(cm.local(sm, sm_o))
    sdt.finish()
    uu[...] = dto[...].astype(F32).reshape(256, 640)
    outs.append(cm.local(uu, dtok_o))
    for c in outs:
        c.wait()
    cm.drain()

def backward(par, mlp, dn2, cv, xb, yb, gx, ga, hs, msk, r, g, wg, tk, dt, h1, w_t, wo):
    s = jax.ShapeDtypeStruct
    R = 256
    V = pltpu.VMEM
    out_shape = [s((4, 64, 640), BF), s((R, 640), F32), s((2, R, 640), BF), s((4, 64, 2560), BF), s((4, 4, 160, 256), BF), s((2, 5, 4, 64, 128), BF), s((16, 640), F32)]
    w = V((R, 640), F32)
    blk = V((4, 4, 64, 640), BF)
    red = [V((4, 2, 64, 640), BF), V((4, 64, 640), BF), V((4, 64, 640), BF)]
    red5 = [V((5, 2, R, 128), BF), V((5, R, 128), BF), V((5, R, 128), BF)]
    scratch = [blk, blk, V((4, R, 640), BF), w, w, w, w, w, V((5, R, 128), F32), V((320, 128), F32), V((4, 8, 640), F32), V((5, 256, 512), BF),
               V((4, 64, 640), BF), V((64, 2560), BF), V((64, 2560), F32), V((2, 640, 2560), BF), V((640, 2560), BF),
               w, w, w, w, V((4, 64, 2560), BF), V((5, 4, R, 128), BF), V((5, R, 256), BF), V((2, R, 640), BF), V((4, R, 640), F32), blk, V((64, 2560), F32),
               V((4, 64, 640), BF), V((4, 64, 640), BF), V((4, 64, 640), BF), V((4, 4, 160, 256), BF), V((4, 8, 640), F32), V((3, 8, 640), F32), V((16, 640), F32),
               V((2, 5, 4, 64, 128), BF), V((4, 64, 640), BF)] + red + red + red5 + red + [
               pltpu.SemaphoreType.DMA((80,)), pltpu.SemaphoreType.DMA((80,)), pltpu.SemaphoreType.DMA((40,))]
    return pl.pallas_call(
        backward_kernel, out_shape=out_shape,
        in_specs=[VMEM] + [ANY] * 17,
        out_specs=[ANY] * len(out_shape),
        scratch_shapes=scratch,
        compiler_params=pltpu.CompilerParams(collective_id=4, has_side_effects=True, vmem_limit_bytes=VM),
        name="backward",
    )(par, mlp, dn2, cv, xb, yb, gx, ga, hs, msk, r, g, wg, tk, dt, h1, w_t, wo)

def exchange(g, send, slots, ss, rs, axis):
    cps = [g.rc(send(d), slots.at[d - 1], ss.at[d - 1], rs.at[d - 1], axis, d) for d in (1, 3, 2)]
    for c in cps: c.start()
    return cps

def grads3_kernel(g, n2t, dtt, n1t, drt, dgs, dus, hids, dxy, zs, sg_h, sm_h, in_o, dn_o, xy_o, wout_o, gate_o, sm_o, red, sg, sgr, sgt, sgr2, sgy, sma, smr, smy, sems, semr, seml, *refs):
    def usrc(c):
        if c < 3: return dgs.at[c]
        if c < 6: return dus.at[c - 3]
        if c < 9: return hids.at[c - 6]
        if c < 11: return dxy.at[c - 9]
        return zs
    g.bind(refs, usrc, [n2t, dtt, n1t, drt], red)
    g.fdone = [False] * len(g.fplan)
    x, z, y, f = coords()
    lsg = pltpu.make_async_copy(sg_h, sg, seml.at[0]); lsg.start()
    lsm = pltpu.make_async_copy(sm_h, sma.at[0], seml.at[1]); lsm.start()
    entry_barrier(REP)
    lsm.wait()
    e1 = exchange(g, lambda d: sma.at[0], smr.at[0], sems.at[0], semr.at[0], "x")
    lsg.wait()
    e2 = exchange(g, lambda d: sg.at[(x + d) % 4], sgr, sems.at[1], semr.at[1], "x")
    g.send_f(0); g.send_f(1)
    order = [0, 6, 1, 3, 7, 2, 4, 8, 5, 9, 10, 11]
    for j, c in enumerate(order):
        if j == 6:
            for k in (2, 3, 4): g.send_f(k)
        g.send_u(c)
    n = len(order)
    for j in range(n + 4):
        if j < n: g.mm(order[j])
        if 0 <= j - 2 < n: g.rs(order[j - 2])
        if 0 <= j - 4 < n: g.fin(order[j - 4])
        if j == 0:
            for c in e1: c.wait()
            sma[1] = (sma[0] + smr[0, 0]) + (smr[0, 1] + smr[0, 2])
            e3 = exchange(g, lambda d: sma.at[1], smr.at[1], sems.at[2], semr.at[2], "z")
            for c in e2: c.wait()
            t = (sg[x].astype(F32) + sgr[0].astype(F32)) + (sgr[1].astype(F32) + sgr[2].astype(F32))
            sgt[...] = t.astype(BF)
            e4 = exchange(g, lambda d: sgt.at[:, :, pl.ds(pl.multiple_of((z + d) % 4 * 16, 16), 16)], sgr2, sems.at[3], semr.at[3], "z")
        if j == 2:
            for c in e3: c.wait()
            sma[2] = (sma[1] + smr[1, 0]) + (smr[1, 1] + smr[1, 2])
            e5 = g.rc(sma.at[2], smy, sems.at[4, 0], semr.at[4, 0], "y", 0); e5.start()
            for c in e4: c.wait()
            t = sgt[:, :, pl.ds(pl.multiple_of(z * 16, 16), 16), :].astype(F32) + sgr2[0].astype(F32) + sgr2[1].astype(F32) + sgr2[2].astype(F32)
            sgy[0] = t
            e6 = g.rc(sgy.at[0], sgy.at[1], sems.at[4, 1], semr.at[4, 1], "y", 0); e6.start()
        if j == 4:
            e5.wait()
            sm_o[...] = sma[2] + smy[...]
            e6.wait()
            half = pl.ds(pl.multiple_of(y * 8, 8), 8)
            gate_o[...] = sgy[0, :, :, half, :] + sgy[1, :, :, half, :]
    for k in range(2):
        for i in range(3):
            in_o[k, :, i * 640:i * 640 + 640] = red[3 * k + i]
        xy_o[k] = red[9 + k].T
    for i in range(3):
        dn_o[:, i * 640:i * 640 + 640] = red[6 + i]
    wout_o[...] = red[11].T

def grads3(n2t, dtt, n1t, drt, dgs, dus, hids, dxy, zs, sg, sm):
    g = Grads(PLAN, FPLAN)
    s = jax.ShapeDtypeStruct
    V = pltpu.VMEM
    return pl.pallas_call(
        functools.partial(grads3_kernel, g),
        out_shape=[s((2, 80, 1920), F32), s((80, 1920), F32), s((2, 640, 80), F32), s((640, 80), F32), s((2, 5, 8, 128), F32), s((16, 640), F32)],
        in_specs=[ANY] * 11,
        out_specs=[VMEM] * 6,
        scratch_shapes=[V((12, 80, 640), F32), V((4, 2, 5, 64, 128), BF), V((3, 2, 5, 64, 128), BF), V((2, 5, 64, 128), BF), V((3, 2, 5, 16, 128), BF), V((2, 2, 5, 16, 128), F32),
                        V((3, 16, 640), F32), V((2, 3, 16, 640), F32), V((16, 640), F32),
                        pltpu.SemaphoreType.DMA((5, 3)), pltpu.SemaphoreType.DMA((5, 3)), pltpu.SemaphoreType.DMA((2,))] + g.scratch(),
        compiler_params=pltpu.CompilerParams(collective_id=7, has_side_effects=True, vmem_limit_bytes=VM),
        name="grads",
    )(n2t, dtt, n1t, drt, dgs, dus, hids, dxy, zs, sg, sm)

def body(tokens, seq_len, seq_owner, gain_1, gain_2, w_xy, conv_w, conv_b, gate_w, gate_b, a_param, w_out, w_in, w_down, cotangent):
    lenc, ownc, ownr, par, gn, w_t, gw_t, wo = prep(seq_len, seq_owner, gain_1, gain_2, w_xy, conv_w, conv_b, gate_w, gate_b, a_param, w_out)
    (n1, cv, xb, yb, gx, ga, hs, z, n2, dt, h1, msk, r, g, wg, tk, n1t) = forward(lenc, ownc, ownr, par, gn, tokens, cotangent, w_t, gw_t, wo)
    hid, dg, du, mlp, dn2, n2t, dtt = ffn(n2.reshape(256, 2560), dt, w_in, w_down)
    bo, dtok, dxy, dr, drt, sg, sm = backward(par, mlp, dn2, cv, xb, yb, gx, ga, hs, msk, r, g, wg, tk, dt, h1, w_t, wo)
    r_in, r_dn, r_xy, r_wo, r_gate, r_sm = grads3(n2t, dtt, n1t, drt, dg, du, hid, dxy, z, jnp.moveaxis(sg, 2, 0), sm)
    red_xy = jnp.transpose(r_xy.reshape(2, 10, 64, 80), (0, 3, 1, 2))
    red_gate = jnp.transpose(r_gate.reshape(2, 5, 8, 2, 64), (0, 1, 3, 2, 4)).reshape(2, 10, 8, 64)
    return (bo.reshape(256, 640), dtok, r_sm[0], r_sm[1], red_xy, r_sm[2:6].reshape(4, 10, 64), r_sm[6].reshape(10, 64),
            red_gate, r_sm[7:9].reshape(2, 10, 64), r_sm[9].reshape(10, 64), r_wo.reshape(10, 64, 80), r_in, r_dn.T)


def solution(mesh):
    return jax.shard_map(
        body,
        mesh=mesh,
        in_specs=(
            P("rep", "fsdp"), P(), P(), P("fsdp"), P("fsdp"), P(None, None, None, "fsdp"), P(None, None, "fsdp"), P(None, "fsdp"),
            P(None, None, None, "fsdp"), P(None, None, "fsdp"), P(None, "fsdp"), P(None, "fsdp", None), P(None, None, "fsdp"), P("fsdp", None), P("rep", "fsdp"),
        ),
        out_specs=(
            P("rep", "fsdp"), P("rep", "fsdp"), P("fsdp"), P("fsdp"), P(None, "rep", None, "fsdp"), P(None, None, "fsdp"), P(None, "fsdp"),
            P(None, None, "rep", "fsdp"), P(None, None, "fsdp"), P(None, "fsdp"), P(None, "fsdp", "rep"), P(None, "rep", "fsdp"), P("fsdp", "rep"),
        ),
        check_vma=False,
    )
```

```python
import functools

import jax
import jax.numpy as jnp
from jax import lax
from jax.experimental import pallas as pl
from jax.experimental.pallas import tpu as pltpu
from jax.sharding import PartitionSpec as P

MESH = pl.DeviceIdType.MESH
VM = 63 * 2**20
GC = 0.7978845608028654

def gelu_parts(v):
    v2 = v * v
    t = jnp.tanh(GC * v * (1.0 + 0.044715 * v2))
    half = 0.5 * (1.0 + t)
    g = v * half
    dg = half + 0.5 * v * (1.0 - t * t) * (GC * (1.0 + 3 * 0.044715 * v2))
    return g, dg

def dot(a, b):
    return jnp.dot(a, b, preferred_element_type=jnp.float32)

def dot_nt(a, b):
    return lax.dot_general(a, b, (((1,), (1,)), ((), ())), preferred_element_type=jnp.float32)

def ffn_kernel(n2, dt, w_in, w_dn, hid, dg, du, mlp, dn2, n2t, dtt, am, ad):
    i = pl.program_id(0)
    @pl.when(i == 1)
    def _():
        for c in range(4):
            n2t[c] = n2[:, c * 640:c * 640 + 640].T.reshape(4, 160, 256)
            dtt[c] = dt[:, c * 640:c * 640 + 640].T.reshape(4, 160, 256)
    @pl.when(i == 0)
    def _():
        am[...] = jnp.zeros_like(am)
        ad[...] = jnp.zeros_like(ad)
    gate = dot(n2[...], w_in[0])
    up = dot(n2[...], w_in[1])
    g, dgl = gelu_parts(gate)
    h = (g * up).astype(jnp.bfloat16)
    hid[0] = h
    dh = dot_nt(dt[...], w_dn[...])
    a = (dh * up * dgl).astype(jnp.bfloat16)
    b = (dh * g).astype(jnp.bfloat16)
    dg[0] = a
    du[0] = b
    am[...] += dot(h, w_dn[...])
    ad[...] += dot_nt(a, w_in[0])
    ad[...] += dot_nt(b, w_in[1])
    @pl.when(i == 2)
    def _():
        for c in range(4):
            mlp[c] = am[:, c * 640:c * 640 + 640].astype(jnp.bfloat16).reshape(4, 64, 640)
            dn2[c] = ad[:, c * 640:c * 640 + 640].astype(jnp.bfloat16).reshape(4, 64, 640)

def ffn(n2, dt, w_in, w_dn):
    R, D = n2.shape
    T = 640
    nt = w_dn.shape[0] // T
    full = pl.BlockSpec((R, D), lambda i: (0, 0))
    tile = pl.BlockSpec((1, R, T), lambda i: (i, 0, 0))
    ch = jax.ShapeDtypeStruct((nt, R, T), jnp.bfloat16)
    rd = jax.ShapeDtypeStruct((4, 4, 64, 640), jnp.bfloat16)
    td = jax.ShapeDtypeStruct((4, 4, 160, 256), jnp.bfloat16)
    part = pl.BlockSpec((4, 4, 64, 640), lambda i: (0, 0, 0, 0))
    turned = pl.BlockSpec((4, 4, 160, 256), lambda i: (0, 0, 0, 0))
    return pl.pallas_call(
        ffn_kernel, grid=(nt,),
        in_specs=[full, full, pl.BlockSpec((2, D, T), lambda i: (0, 0, i)), pl.BlockSpec((T, D), lambda i: (i, 0))],
        out_specs=[tile, tile, tile, part, part, turned, turned],
        out_shape=[ch, ch, ch, rd, rd, td, td],
        scratch_shapes=[pltpu.VMEM((R, D), jnp.float32)] * 2,
        compiler_params=pltpu.CompilerParams(vmem_limit_bytes=VM),
        name="ffn",
    )(n2, dt, w_in, w_dn)

def coords():
    r = lax.axis_index("rep")
    f = lax.axis_index("fsdp")
    return r // 8, (r // 2) % 4, r % 2, f

def peer(axis, d):
    x, z, y, f = coords()
    if axis == "x":
        x = (x + d) % 4
    elif axis == "z":
        z = (z + d) % 4
    elif axis == "y":
        y = 1 - y
    else:
        f = (f + d) % 4
    return ((x * 4 + z) * 2 + y, f)

class Grads:
    def __init__(self, plan, fplan):
        self.plan = plan
        self.fplan = fplan
    def scratch(self):
        n, m = len(self.plan), len(self.fplan)
        b = jnp.bfloat16
        return [
            pltpu.VMEM((n, 4, 256, 640), b),
            pltpu.VMEM((m, 4, 160, 1024), b),
            pltpu.VMEM((n, 4, 160, 640), b),
            pltpu.VMEM((n, 3, 160, 640), b),
            pltpu.VMEM((n, 2, 80, 640), b),
            pltpu.VMEM((n, 80, 640), b),
            pltpu.SemaphoreType.DMA((n, 3)), pltpu.SemaphoreType.DMA((n, 3)),
            pltpu.SemaphoreType.DMA((m, 3)), pltpu.SemaphoreType.DMA((m, 3)),
            pltpu.SemaphoreType.DMA((n, 3)), pltpu.SemaphoreType.DMA((n, 3)),
            pltpu.SemaphoreType.DMA((n,)), pltpu.SemaphoreType.DMA((n,)),
            pltpu.SemaphoreType.DMA((n,)), pltpu.SemaphoreType.DMA((m,)),
        ]
    def bind(self, refs, usrc, fsrc, out):
        (self.ub, self.ft, self.st, self.rr, self.tt, self.yr, self.us, self.ur, self.fs, self.fr,
         self.rq, self.rv, self.ys, self.yv, self.lu, self.lf) = refs
        self.usrc, self.fsrc, self.out = usrc, fsrc, out
    def rc(self, src, dst, s, r, axis, d):
        return pltpu.make_async_remote_copy(src_ref=src, dst_ref=dst, send_sem=s, recv_sem=r, device_id=peer(axis, d), device_id_type=MESH)
    def fcopies(self, k):
        i, axis = self.fplan[k]
        x, z, y, f = coords()
        src = self.fsrc[i]
        me = x if axis == "x" else z
        pick = (lambda t: src.at[t]) if axis == "x" else (lambda t: src.at[:, t])
        loc = pltpu.make_async_copy(pick(me), self.ft.at[k, :, :, pl.ds(0, 256)], self.lf.at[k])
        rem = [self.rc(pick((me + d) % 4), self.ft.at[k, :, :, pl.ds(d * 256, 256)], self.fs.at[k, d - 1], self.fr.at[k, d - 1], axis, d) for d in (1, 3, 2)]
        return loc, rem
    def ucopies(self, c):
        k, axis = self.plan[c]
        src = self.usrc(c)
        loc = pltpu.make_async_copy(src, self.ub.at[c, 0], self.lu.at[c])
        rem = [self.rc(src, self.ub.at[c, d], self.us.at[c, d - 1], self.ur.at[c, d - 1], axis, d) for d in (1, 3, 2)]
        return loc, rem
    def rscopies(self, c):
        k, axis = self.plan[c]
        ra = "z" if axis == "x" else "x"
        x, z, y, f = coords()
        me = z if axis == "x" else x
        return me, [self.rc(self.st.at[c, (me + d) % 4], self.rr.at[c, d - 1], self.rq.at[c, d - 1], self.rv.at[c, d - 1], ra, d) for d in (1, 3, 2)]
    def ycopy(self, c):
        x, z, y, f = coords()
        return self.rc(self.tt.at[c, 1 - y], self.yr.at[c], self.ys.at[c], self.yv.at[c], "y", 0)
    def send_f(self, k):
        loc, rem = self.fcopies(k)
        loc.start()
        for r in rem: r.start()
    def send_u(self, c):
        loc, rem = self.ucopies(c)
        loc.start()
        for r in rem: r.start()
    def mm(self, c):
        k, axis = self.plan[c]
        loc, rem = self.ucopies(c)
        loc.wait()
        for r in rem: r.wait()
        if not self.fdone[k]:
            loc, rem = self.fcopies(k)
            loc.wait()
            for r in rem: r.wait()
            self.fdone[k] = True
        self.st[c] = dot(self.ft[k].reshape(640, 1024), self.ub[c].reshape(1024, 640)).astype(jnp.bfloat16).reshape(4, 160, 640)
        me, cps = self.rscopies(c)
        for r in cps: r.start()
    def rs(self, c):
        me, cps = self.rscopies(c)
        for r in cps: r.wait()
        f = jnp.float32
        t = (self.st[c, me].astype(f) + self.rr[c, 0].astype(f)) + (self.rr[c, 1].astype(f) + self.rr[c, 2].astype(f))
        self.tt[c] = t.astype(jnp.bfloat16).reshape(2, 80, 640)
        self.ycopy(c).start()
    def fin(self, c):
        x, z, y, f = coords()
        self.ycopy(c).wait()
        self.out[c] = self.tt[c, y].astype(jnp.float32) + self.yr[c].astype(jnp.float32)

def entry_barrier(peers):
    b = pltpu.get_barrier_semaphore()
    for axis, d in peers:
        pl.semaphore_signal(b, inc=1, device_id=peer(axis, d), device_id_type=MESH)
    pl.semaphore_wait(b, len(peers))

REP = [("x", 1), ("x", 2), ("x", 3), ("z", 1), ("z", 2), ("z", 3), ("y", 1)]

PLAN = [(0, "x")] * 6 + [(1, "z")] * 3 + [(2, "x"), (3, "z"), (4, "z")]
FPLAN = [(0, "x"), (1, "z"), (2, "x"), (2, "z"), (3, "z")]

def grads_kernel(g, n2t, dtt, n1t, drt, dgs, dus, hids, dxs, zs, out, *refs):
    def usrc(c):
        if c < 3: return dgs.at[c]
        if c < 6: return dus.at[c - 3]
        if c < 9: return hids.at[c - 6]
        if c < 11: return dxs.at[c - 9]
        return zs
    g.bind(refs, usrc, [n2t, dtt, n1t, drt], out)
    g.fdone = [False] * len(g.fplan)
    entry_barrier(REP)
    g.send_f(0); g.send_f(1)
    order = [0, 6, 1, 3, 7, 2, 4, 8, 5, 9, 10, 11]
    for j, c in enumerate(order):
        if j == 6:
            for k in (2, 3, 4): g.send_f(k)
        g.send_u(c)
    n = len(order)
    for j in range(n + 4):
        if j < n: g.mm(order[j])
        if 0 <= j - 2 < n: g.rs(order[j - 2])
        if 0 <= j - 4 < n: g.fin(order[j - 4])

def grads(n2t, dtt, n1t, drt, dgs, dus, hids, dxs, zs):
    g = Grads(PLAN, FPLAN)
    return pl.pallas_call(
        functools.partial(grads_kernel, g),
        out_shape=jax.ShapeDtypeStruct((12, 80, 640), jnp.float32),
        in_specs=[pl.BlockSpec(memory_space=pl.ANY)] * 9,
        out_specs=pl.BlockSpec(memory_space=pltpu.VMEM),
        scratch_shapes=g.scratch(),
        compiler_params=pltpu.CompilerParams(collective_id=7, has_side_effects=True, vmem_limit_bytes=VM),
        name="grads",
    )(n2t, dtt, n1t, drt, dgs, dus, hids, dxs, zs)

F32 = jnp.float32
BF = jnp.bfloat16
EPS = 1e-06
ANY = pl.BlockSpec(memory_space=pl.ANY)
VMEM = pl.BlockSpec(memory_space=pltpu.VMEM)

def fpeer(d):
    r = lax.axis_index("rep")
    f = lax.axis_index("fsdp")
    h, c = f // 2, f % 2
    if d % 2:
        c = 1 - c
    if d // 2:
        h = 1 - h
    return r, h * 2 + c

def device(to):
    axis, d = to
    return fpeer(d) if axis == "f" else peer(axis, d)

class Sent:
    def __init__(self, src, dst, to, ssem, rsem):
        self.src, self.dst, self.to, self.ssem, self.rsem = src, dst, to, ssem, rsem
    def make(self):
        return pltpu.make_async_remote_copy(
            src_ref=self.src(), dst_ref=self.dst(), send_sem=self.ssem(), recv_sem=self.rsem(), device_id=device(self.to), device_id_type=MESH)
    def wait_recv(self):
        self.make().wait_recv()
    def wait_send(self):
        self.make().wait_send()

class Comm:
    def __init__(self, ssem, rsem, lsem):
        self.ssem, self.rsem, self.lsem = ssem, rsem, lsem
        self.n = self.m = 0
        self.open = []
    def remote(self, src, dst, to):
        k = self.n
        self.n += 1
        c = Sent(src if callable(src) else lambda: src, dst if callable(dst) else lambda: dst, to, lambda: self.ssem.at[k], lambda: self.rsem.at[k])
        c.make().start()
        self.open.append(c)
        return c
    def local(self, src, dst):
        k = self.m
        self.m += 1
        c = pltpu.make_async_copy(src, dst, self.lsem.at[k])
        c.start()
        return c
    def sent(self, c):
        c.wait_send()
        self.open = [o for o in self.open if o is not c]
    def drain(self):
        for c in self.open:
            c.wait_send()
        self.open = []

class Gather:
    def __init__(self, comm, buf, own=None, parts=None):
        self.comm, self.buf = comm, buf
        self.f = lax.axis_index("fsdp")
        self.parts = parts or [()]
        self.own = own
        self.far, self.near = [], []
    def start(self):
        f, cm = self.f, self.comm
        for p in self.parts:
            dst = self.buf.at[(f, *p)]
            src = self.own.at[p] if self.own is not None else dst
            self.far.append(cm.remote(src, dst, ("f", 2)))
            self.near.append(cm.remote(src, dst, ("f", 1)))
    def relay(self):
        _, o = fpeer(2)
        self.late = []
        for p, c in zip(self.parts, self.far):
            c.wait_recv()
            dst = self.buf.at[(o, *p)]
            self.late.append(self.comm.remote(dst, dst, ("f", 1)))
    def finish(self):
        for c in self.near + self.late:
            c.wait_recv()

class Reduce:
    def __init__(self, comm, part, r1, s2, r2):
        self.comm, self.part, self.r1, self.s2, self.r2 = comm, part, r1, s2, r2
        self.f = lax.axis_index("fsdp")
        self.a, self.b, self.c = {}, {}, {}
    def send(self, c):
        self.a[c] = self.comm.remote(lambda: self.part.at[c, fpeer(3)[1]], lambda: self.r1.at[c, 1], ("f", 1))
        self.b[c] = self.comm.remote(lambda: self.part.at[c, fpeer(1)[1]], lambda: self.r1.at[c, 0], ("f", 1))
    def mid(self, c):
        _, o2 = fpeer(2)
        self.a[c].wait_recv()
        self.s2[c] = (self.part[c, o2].astype(F32) + self.r1[c, 1].astype(F32)).astype(BF)
        self.c[c] = self.comm.remote(lambda: self.s2.at[c], lambda: self.r2.at[c], ("f", 2))
    def fin(self, c):
        self.b[c].wait_recv()
        self.c[c].wait_recv()
        return self.part[c, self.f].astype(F32) + self.r1[c, 0].astype(F32) + self.r2[c].astype(F32)

def group_barrier(ds):
    b = pltpu.get_barrier_semaphore()
    for d in ds:
        pl.semaphore_signal(b, inc=1, device_id=fpeer(d), device_id_type=MESH)
    pl.semaphore_wait(b, len(ds))

def lanes(q):
    return slice(q * 128, q * 128 + 128)

def row_masks(lenc, ownc, ownr, msk):
    me = lax.axis_index("rep")
    ln = lenc[...]
    own = ownc[...] == me
    mine = jnp.where(own, ln, 0)
    j = lax.broadcasted_iota(jnp.int32, (128, 128), 0)
    i = lax.broadcasted_iota(jnp.int32, (128, 128), 1)
    offset = jnp.sum(jnp.where(j < i, mine, 0), axis=0, keepdims=True)
    total = jnp.sum(mine, axis=0, keepdims=True)
    place = lax.broadcasted_iota(jnp.int32, (256, 128), 0)
    hit = jnp.where((ownr[...] == me) & (offset == place), 1.0, 0.0)
    start = jnp.broadcast_to(jnp.max(hit, axis=1, keepdims=True), (256, 128))
    msk[0] = start
    run = start
    for k in (1, 2, 3):
        msk[k] = jnp.where((run == 0.0) & (place >= k), 1.0, 0.0)
        run = jnp.maximum(run, jnp.where(place >= k, pltpu.roll(start, k, axis=0), 0.0))
    msk[4] = jnp.where(place < total, 1.0, 0.0)

def wide_gates(gw, wg):
    row = lax.broadcasted_iota(jnp.int32, (128, 128), 0) // 64
    col = lax.broadcasted_iota(jnp.int32, (128, 128), 1) // 64
    for q in range(5):
        for k in range(2):
            for g in range(2):
                v = gw[k, q * 128:q * 128 + 128, g * 128:g * 128 + 128].astype(F32)
                r = pltpu.roll(v, 64, axis=1)
                for e in range(2):
                    twice = jnp.where(col == e, v, r)
                    p = 2 * g + e
                    wg[q, k * 128:k * 128 + 128, p * 128:p * 128 + 128] = jnp.where(row == col, twice, 0.0).astype(BF)

def softplus(v):
    return jnp.maximum(v, 0.0) + jnp.log1p(jnp.exp(-jnp.abs(v)))

def sigmoid(v):
    return 1.0 / (1.0 + jnp.exp(-v))

def scan_rows(a_ref, u_ref, h_ref, back):
    rows = lax.broadcasted_iota(jnp.int32, (8, 640), 0)
    carry = jnp.zeros((1, 640), F32)
    order = range(31, -1, -1) if back else range(32)
    for i in order:
        a = a_ref[i * 8:i * 8 + 8, :]
        u = u_ref[i * 8:i * 8 + 8, :]
        for s in (1, 2, 4):
            if back:
                ok = rows < 8 - s
                a2 = jnp.where(ok, pltpu.roll(a, 8 - s, axis=0), 1.0)
                u2 = jnp.where(ok, pltpu.roll(u, 8 - s, axis=0), 0.0)
            else:
                ok = rows >= s
                a2 = jnp.where(ok, pltpu.roll(a, s, axis=0), 1.0)
                u2 = jnp.where(ok, pltpu.roll(u, s, axis=0), 0.0)
            u = u + a * u2
            a = a * a2
        h = u + a * carry
        h_ref[i * 8:i * 8 + 8, :] = h
        carry = h[0:1, :] if back else h[7:8, :]

def gate_values(q, pre, par, start):
    gx = sigmoid(pre[:, 0:128] + par[5:6, lanes(q)])
    ga = sigmoid(pre[:, 128:256] + par[6:7, lanes(q)])
    return gx, ga

def decay_of(q, ga, par, start):
    sp = softplus(par[7:8, lanes(q)])
    a = jnp.exp(-8.0 * ga * sp)
    spread = 1.0 - a * a
    mult = jnp.where(start == 1.0, 1.0, jnp.sqrt(jnp.maximum(spread, 0.01)))
    return sp, a, spread, mult

def forward_kernel(lenc, ownc, ownr, par, gn, tok, cot, w_t, gw_h, wo_h,
                   n1_o, cv_o, xb_o, yb_o, gx_o, ga_o, hs_o, z_o, n2_o, dt_o, h1_o, msk_o, r_o, g_o, wg_o, tk_o, n1t_o,
                   tkb, ctb, gnb, wv, gw, wo, wg, n1, dt, cvb, xb, yb, gx, ga, aa, uu, hs, z, msk, pt, r1, s2, r2, h1, n2b, rs1, rs2, n1t,
                   ssem, rsem, lsem):
    cm = Comm(ssem, rsem, lsem)
    f = lax.axis_index("fsdp")
    lw = [cm.local(w_t.at[0], wv.at[0]), cm.local(gw_h, gw), cm.local(w_t.at[1], wv.at[1]), cm.local(wo_h, wo)]
    lt = [cm.local(tok, tkb.at[f]), cm.local(gn, gnb.at[f]), cm.local(cot, ctb.at[f])]
    group_barrier((1, 2))
    halves = [(pl.ds(0, 128),), (pl.ds(128, 128),)]
    gtk = Gather(cm, tkb, tok, halves)
    ggn = Gather(cm, gnb, gn)
    gct = Gather(cm, ctb, cot)
    ggn.start()
    gtk.start()
    gct.start()
    row_masks(lenc, ownc, ownr, msk)
    lw[1].wait()
    wide_gates(gw, wg)
    outs = [cm.local(msk, msk_o), cm.local(wg, wg_o)]
    ggn.relay()
    gtk.relay()
    for c in lt:
        c.wait()
    ggn.finish()
    gtk.finish()
    @pl.loop(0, 16)
    def _(i):
        rows = pl.ds(pl.multiple_of(i * 16, 16), 16)
        xs = [tkb[p, rows, :].astype(F32) for p in range(4)]
        ss = sum(jnp.sum(x * x, axis=-1, keepdims=True) for x in xs)
        r = lax.rsqrt(ss * (1.0 / 2560) + EPS)
        rs1[rows, :] = jnp.broadcast_to(r, (16, 128))
        for p in range(4):
            n1[rows, p * 640:p * 640 + 640] = (xs[p] * r * gnb[p, 0:1, :]).astype(BF)
    outs += [cm.local(n1, n1_o), cm.local(gnb, g_o), cm.local(tkb, tk_o)]
    lw[0].wait()
    xb[...] = dot_nt(n1[...], wv[0])
    outs.append(cm.local(xb, xb_o))
    for q in range(5):
        x = xb[:, lanes(q)]
        acc = par[4:5, lanes(q)] + par[0:1, lanes(q)] * x
        for k in (1, 2, 3):
            acc = acc + par[k:k + 1, lanes(q)] * pltpu.roll(x, k, axis=0) * msk[k]
        cvb[f, :, lanes(q)] = acc.astype(BF)
    gcv = Gather(cm, cvb, None, halves)
    gcv.start()
    lw[2].wait()
    yb[...] = dot_nt(n1[...], wv[1])
    outs.append(cm.local(yb, yb_o))
    gct.relay()
    gcv.relay()
    for c in range(4):
        n1t[c] = n1[:, c * 640:c * 640 + 640].T.reshape(4, 160, 256)
    outs.append(cm.local(n1t, n1t_o))
    gcv.finish()
    outs.append(cm.local(cvb, cv_o))
    for q in range(5):
        lhs = jnp.concatenate([cvb[p, :, lanes(q)] for p in range(4)], axis=1)
        pre = dot_nt(lhs, wg[q])
        gxq, gaq = gate_values(q, pre, par, msk[0])
        sp, a, spread, mult = decay_of(q, gaq, par, msk[0])
        gx[:, lanes(q)] = gxq
        ga[:, lanes(q)] = gaq
        aa[:, lanes(q)] = jnp.where(msk[0] == 1.0, 0.0, a)
        uu[:, lanes(q)] = mult * gxq * cvb[f, :, lanes(q)].astype(F32)
    outs += [cm.local(gx, gx_o), cm.local(ga, ga_o)]
    scan_rows(aa, uu, hs, False)
    for q in range(5):
        yg, _ = gelu_parts(yb[:, lanes(q)])
        z[:, lanes(q)] = (hs[:, lanes(q)] * yg).astype(BF)
    outs += [cm.local(hs, hs_o), cm.local(z, z_o)]
    lw[3].wait()
    red = Reduce(cm, pt, r1, s2, r2)
    for c in range(4):
        pt[c] = dot(z[...], wo[:, c * 640:c * 640 + 640]).astype(BF).reshape(4, 64, 640)
        red.send(c)
        if c: red.mid(c - 1)
    red.mid(3)
    gct.finish()
    @pl.loop(0, 16)
    def _(i):
        rows = pl.ds(pl.multiple_of(i * 16, 16), 16)
        live = jnp.broadcast_to(msk[4, rows, 0:1], (16, 640))
        for p in range(4):
            dt[rows, p * 640:p * 640 + 640] = (ctb[p, rows, :].astype(F32) * live).astype(BF)
    outs.append(cm.local(dt, dt_o))
    own = pl.ds(pl.multiple_of(f * 64, 64), 64)
    ss = jnp.zeros((64, 1), F32)
    for c in range(4):
        h = tkb[c, own, :].astype(F32) + red.fin(c)
        h1[:, c * 640:c * 640 + 640] = h
        ss = ss + jnp.sum(h * h, axis=-1, keepdims=True)
    r = lax.rsqrt(ss * (1.0 / 2560) + EPS)
    rs2[...] = jnp.broadcast_to(r, (64, 128))
    for c in range(4):
        cs = slice(c * 640, c * 640 + 640)
        n2b[f, :, cs] = (h1[:, cs] * r * gnb[c, 1:2, :]).astype(BF)
    gn2 = Gather(cm, n2b, None, [(pl.ds(0, 32),), (pl.ds(32, 32),)])
    gn2.start()
    outs += [cm.local(h1, h1_o), cm.local(rs1, r_o.at[pl.ds(0, 256)]), cm.local(rs2, r_o.at[pl.ds(256, 64)])]
    gn2.relay()
    gn2.finish()
    outs.append(cm.local(n2b, n2_o))
    for c in outs:
        c.wait()
    cm.drain()

def forward(lenc, ownc, ownr, par, gn, tok, cot, w_t, gw_t, wo):
    s = jax.ShapeDtypeStruct
    R = 256
    fw = s((R, 640), F32)
    out_shape = [s((R, 2560), BF), s((4, R, 640), BF), fw, fw, fw, fw, fw, s((R, 640), BF), s((4, 64, 2560), BF), s((R, 2560), BF),
                 s((64, 2560), F32), s((5, R, 128), F32), s((320, 128), F32), s((4, 8, 640), F32), s((5, 256, 512), BF), s((4, R, 640), BF), s((4, 4, 160, 256), BF)]
    V = pltpu.VMEM
    f640 = V((R, 640), F32)
    scratch = [V((4, R, 640), BF), V((4, R, 640), BF), V((4, 8, 640), F32), V((2, 640, 2560), BF), V((2, 640, 256), BF), V((640, 2560), BF),
               V((5, 256, 512), BF), V((R, 2560), BF), V((R, 2560), BF), V((4, R, 640), BF), f640, f640, f640, f640, f640, f640, f640,
               V((R, 640), BF), V((5, R, 128), F32), V((4, 4, 64, 640), BF), V((4, 2, 64, 640), BF), V((4, 64, 640), BF), V((4, 64, 640), BF),
               V((64, 2560), F32), V((4, 64, 2560), BF), V((R, 128), F32), V((64, 128), F32), V((4, 4, 160, 256), BF),
               pltpu.SemaphoreType.DMA((48,)), pltpu.SemaphoreType.DMA((48,)), pltpu.SemaphoreType.DMA((32,))]
    return pl.pallas_call(
        forward_kernel, out_shape=out_shape,
        in_specs=[VMEM] * 5 + [ANY] * 5,
        out_specs=[ANY] * len(out_shape),
        scratch_shapes=scratch,
        compiler_params=pltpu.CompilerParams(collective_id=3, has_side_effects=True, vmem_limit_bytes=VM),
        name="forward",
    )(lenc, ownc, ownr, par, gn, tok, cot, w_t, gw_t, wo)

def prep(seq_len, seq_owner, gain_1, gain_2, w_xy, conv_w, conv_b, gate_w, gate_b, a_param, w_out):
    lenc = seq_len.reshape(128, 1)
    ownc = seq_owner.reshape(128, 1)
    ownr = seq_owner.reshape(1, 128)
    fl = lambda v: v.astype(F32).reshape(-1, 640)
    par = jnp.concatenate([fl(conv_w), fl(conv_b), fl(gate_b), fl(a_param)], axis=0)
    gn = jnp.pad(jnp.stack([gain_1, gain_2]).astype(F32), ((0, 6), (0, 0)))
    w_t = jnp.transpose(w_xy, (0, 2, 3, 1)).reshape(2, 640, 2560)
    gw_t = jnp.swapaxes(gate_w, 2, 3).reshape(2, 640, 256)
    return lenc, ownc, ownr, par, gn, w_t, gw_t, w_out.reshape(640, 2560)

def dot_tn(a, b):
    return lax.dot_general(a, b, (((0,), (0,)), ((), ())), preferred_element_type=jnp.float32)

class Swap:
    def __init__(self, comm, src, dst):
        f = lax.axis_index("fsdp")
        self.cps = []
        for d in (3, 2, 1):
            _, t = fpeer(d)
            self.cps.append(comm.remote(src.at[t], dst.at[f], ("f", d)))
        self.own = comm.local(src.at[f], dst.at[f])
    def finish(self):
        self.own.wait()
        for c in self.cps:
            c.wait_recv()

def backward_kernel(par, mlp_h, dn2_h, cv_h, xb_h, yb_h, gx_h, ga_h, hs_h, msk_h, r_h, g_h, wg_h, tk_h, dt_h, h1_h, w_t, wo_h,
                    bo_o, dtok_o, dxy_o, dr_o, drt_o, sg_o, sm_o,
                    pm, pd, cv, xb, yb, gx, ga, hs, msk, rb, gnb, wg, tk, dtb, h1, wv, wo,
                    aa, uu, gg, dc1, dr, pb, dp, dxy, dna, dnp, dh1, bo, bob, dto, dtr, gs, gr, sm, sg, dob,
                    m1, m2, m3, d1, d2, d3, e1, e2, e3, f1, f2, f3,
                    ssem, rsem, lsem):
    cm = Comm(ssem, rsem, lsem)
    f = lax.axis_index("fsdp")
    own = pl.ds(pl.multiple_of(f * 64, 64), 64)
    ld = [cm.local(dn2_h.at[c], pd.at[c]) for c in range(4)]
    lh = [cm.local(h1_h, h1), cm.local(g_h, gnb), cm.local(r_h, rb), cm.local(dt_h.at[own], dtb), cm.local(msk_h, msk)]
    lm = [cm.local(mlp_h.at[c], pm.at[c]) for c in range(4)]
    lb = [cm.local(wo_h, wo), cm.local(yb_h, yb), cm.local(hs_h, hs), cm.local(ga_h, ga), cm.local(gx_h, gx), cm.local(cv_h, cv),
          cm.local(wg_h, wg), cm.local(xb_h, xb), cm.local(w_t, wv), cm.local(tk_h.at[:, own], tk)]
    group_barrier((1, 2, 3))
    rd = Reduce(cm, pd, d1, d2, d3)
    rm = Reduce(cm, pm, m1, m2, m3)
    for c in range(4):
        ld[c].wait()
        rd.send(c)
    for c in range(4):
        rd.mid(c)
    for c in range(4):
        lm[c].wait()
        rm.send(c)
    for c in lh:
        c.wait()
    gs[...] = jnp.zeros_like(gs)
    r2 = rb[256:320, 0:1]
    acc = jnp.zeros((64, 1), F32)
    for c in range(4):
        cs = slice(c * 640, c * 640 + 640)
        dn = rd.fin(c)
        h = h1[:, cs]
        gs[c, 1:2, :] = jnp.sum(dn * h * r2, axis=0, keepdims=True)
        v = dn * gnb[c, 1:2, :]
        dh1[:, cs] = v
        acc = acc + jnp.sum(v * h, axis=-1, keepdims=True)
    acc = acc * (1.0 / 2560) * (r2 * r2 * r2)
    for c in range(4):
        cs = slice(c * 640, c * 640 + 640)
        d = dtb[:, cs].astype(F32) + r2 * dh1[:, cs] - h1[:, cs] * acc
        dh1[:, cs] = d
        dr[f, :, cs] = d.astype(BF)
    gdr = Gather(cm, dr, None, [(pl.ds(0, 32),), (pl.ds(32, 32),)])
    gdr.start()
    for c in range(4):
        rm.mid(c)
    for c in lb:
        c.wait()
    gdr.relay()
    for q in range(5):
        sp, a, spread, mult = decay_of(q, ga[:, lanes(q)], par, msk[0])
        up = pltpu.roll(jnp.where(msk[0] == 1.0, 0.0, a), 255, axis=0)
        rows = lax.broadcasted_iota(jnp.int32, (256, 128), 0)
        aa[:, lanes(q)] = jnp.where(rows == 255, 0.0, up)
    gdr.finish()
    uu[...] = dot_nt(dr[...].reshape(256, 2560), wo[...])
    outs = [cm.local(dr, dr_o)]
    for q in range(5):
        yg, dgl = gelu_parts(yb[:, lanes(q)])
        dz = uu[:, lanes(q)]
        dxy[1, :, lanes(q)] = (dz * hs[:, lanes(q)] * dgl).astype(BF)
        uu[:, lanes(q)] = dz * yg
    scan_rows(aa, uu, gg, True)
    re = Reduce(cm, pb, e1, e2, e3)
    for q in range(5):
        ls = lanes(q)
        start = msk[0]
        gxq, gaq, g = gx[:, ls], ga[:, ls], gg[:, ls]
        sp, a, spread, mult = decay_of(q, gaq, par, start)
        cvq = cv[f, :, ls].astype(F32)
        prev = jnp.where(start == 1.0, 0.0, pltpu.roll(hs[:, ls], 1, axis=0))
        slope = jnp.where((start == 1.0) | (spread <= 0.01), 0.0, -a / mult)
        da = g * prev + g * gxq * cvq * slope
        dc1[:, ls] = g * mult * gxq
        dlog = da * a
        da_p = jnp.sum(dlog * (-8.0 * gaq), axis=0, keepdims=True) * sigmoid(par[7:8, ls])
        px = (g * mult * cvq * gxq * (1.0 - gxq)).astype(BF)
        pa = (-8.0 * dlog * sp * gaq * (1.0 - gaq)).astype(BF)
        dp[q, :, 0:128] = px
        dp[q, :, 128:256] = pa
        sm[7:8, ls] = jnp.sum(px.astype(F32), axis=0, keepdims=True)
        sm[8:9, ls] = jnp.sum(pa.astype(F32), axis=0, keepdims=True)
        sm[9:10, ls] = da_p
        db = dot(dp[q], wg[q]).astype(BF)
        for p in range(4):
            pb[q, p] = db[:, lanes(p)]
        re.send(q)
        if q: re.mid(q - 1)
    re.mid(4)
    for c in range(4):
        cs = slice(c * 640, c * 640 + 640)
        dna[c] = dot(dxy[1], wv[1, :, cs])
    low = lax.broadcasted_iota(jnp.int32, (64, 128), 1) < 64
    for q in range(5):
        lhs = jnp.concatenate([cv[p, :, lanes(q)] for p in range(4)], axis=1)
        gwt = dot_tn(lhs, dp[q])
        for p in range(4):
            for k in range(2):
                blk = gwt[p * 128:p * 128 + 128, k * 128:k * 128 + 128]
                sg[k, q, p] = jnp.where(low, blk[0:64], blk[64:128]).astype(BF)
    outs.append(cm.local(sg, sg_o))
    live = msk[4, own, 0:1]
    for c in range(4):
        bo[c] = (live * (h1[:, c * 640:c * 640 + 640] + rm.fin(c))).astype(BF)
    sbo = Swap(cm, bo, bob)
    for q in range(5):
        ls = lanes(q)
        d = dc1[:, ls] + re.fin(q)
        x = xb[:, ls]
        sm[6:7, ls] = jnp.sum(d, axis=0, keepdims=True)
        sm[2:3, ls] = jnp.sum(d * x, axis=0, keepdims=True)
        dx = par[0:1, ls] * d
        for k in (1, 2, 3):
            m = d * msk[k]
            sm[2 + k:3 + k, ls] = jnp.sum(m * pltpu.roll(x, k, axis=0), axis=0, keepdims=True)
            dx = dx + par[k:k + 1, ls] * pltpu.roll(m, 256 - k, axis=0)
        dxy[0, :, ls] = dx.astype(BF)
    outs.append(cm.local(dxy, dxy_o))
    rf = Reduce(cm, dnp, f1, f2, f3)
    for c in range(4):
        cs = slice(c * 640, c * 640 + 640)
        dnp[c] = (dna[c] + dot(dxy[0], wv[0, :, cs])).astype(BF).reshape(4, 64, 640)
        rf.send(c)
        if c: rf.mid(c - 1)
    rf.mid(3)
    for p in range(4):
        for o in range(4):
            pass
    drt = dr[...].reshape(256, 2560)
    for c in range(4):
        dtr[c] = drt[:, c * 640:c * 640 + 640].T.reshape(4, 160, 256)
    outs.append(cm.local(dtr, drt_o))
    r1 = rb[own, 0:1]
    acc = jnp.zeros((64, 1), F32)
    for c in range(4):
        dn = rf.fin(c)
        x = tk[c].astype(F32)
        gs[c, 0:1, :] = jnp.sum(dn * x * r1, axis=0, keepdims=True)
        v = dn * gnb[c, 0:1, :]
        dna[c, 0:64, :] = v
        acc = acc + jnp.sum(v * x, axis=-1, keepdims=True)
    acc = acc * (1.0 / 2560) * (r1 * r1 * r1)
    for c in range(4):
        dob[c] = (dh1[:, c * 640:c * 640 + 640] + r1 * dna[c, 0:64, :] - tk[c].astype(F32) * acc).astype(BF)
    sdt = Swap(cm, dob, dto)
    gcp = []
    for d in (3, 2, 1):
        _, t = fpeer(d)
        gcp.append(cm.remote(gs.at[t], gr.at[d - 1], ("f", d)))
    sbo.finish()
    outs.append(cm.local(bob, bo_o))
    for c in gcp:
        c.wait_recv()
    sm[0:2, :] = (gs[f, 0:2, :] + gr[0, 0:2, :]) + (gr[1, 0:2, :] + gr[2, 0:2, :])
    sm[10:16, :] = jnp.zeros((6, 640), F32)
    outs.append(cm.local(sm, sm_o))
    sdt.finish()
    uu[...] = dto[...].astype(F32).reshape(256, 640)
    outs.append(cm.local(uu, dtok_o))
    for c in outs:
        c.wait()
    cm.drain()

def backward(par, mlp, dn2, cv, xb, yb, gx, ga, hs, msk, r, g, wg, tk, dt, h1, w_t, wo):
    s = jax.ShapeDtypeStruct
    R = 256
    V = pltpu.VMEM
    out_shape = [s((4, 64, 640), BF), s((R, 640), F32), s((2, R, 640), BF), s((4, 64, 2560), BF), s((4, 4, 160, 256), BF), s((2, 5, 4, 64, 128), BF), s((16, 640), F32)]
    w = V((R, 640), F32)
    blk = V((4, 4, 64, 640), BF)
    red = [V((4, 2, 64, 640), BF), V((4, 64, 640), BF), V((4, 64, 640), BF)]
    red5 = [V((5, 2, R, 128), BF), V((5, R, 128), BF), V((5, R, 128), BF)]
    scratch = [blk, blk, V((4, R, 640), BF), w, w, w, w, w, V((5, R, 128), F32), V((320, 128), F32), V((4, 8, 640), F32), V((5, 256, 512), BF),
               V((4, 64, 640), BF), V((64, 2560), BF), V((64, 2560), F32), V((2, 640, 2560), BF), V((640, 2560), BF),
               w, w, w, w, V((4, 64, 2560), BF), V((5, 4, R, 128), BF), V((5, R, 256), BF), V((2, R, 640), BF), V((4, R, 640), F32), blk, V((64, 2560), F32),
               V((4, 64, 640), BF), V((4, 64, 640), BF), V((4, 64, 640), BF), V((4, 4, 160, 256), BF), V((4, 8, 640), F32), V((3, 8, 640), F32), V((16, 640), F32),
               V((2, 5, 4, 64, 128), BF), V((4, 64, 640), BF)] + red + red + red5 + red + [
               pltpu.SemaphoreType.DMA((80,)), pltpu.SemaphoreType.DMA((80,)), pltpu.SemaphoreType.DMA((40,))]
    return pl.pallas_call(
        backward_kernel, out_shape=out_shape,
        in_specs=[VMEM] + [ANY] * 17,
        out_specs=[ANY] * len(out_shape),
        scratch_shapes=scratch,
        compiler_params=pltpu.CompilerParams(collective_id=4, has_side_effects=True, vmem_limit_bytes=VM),
        name="backward",
    )(par, mlp, dn2, cv, xb, yb, gx, ga, hs, msk, r, g, wg, tk, dt, h1, w_t, wo)

CHUNK_FEATURES = [0] * 6 + [1] * 3 + [2, 3, 4]
FEATURE_AXIS = ["x", "z", "x", "z", "z"]
FEATURE_SLOT = [0, 1, 0, 1, 2]

class Sums:
    def __init__(self, cm, ubh, rrh, fth, yr, usrc, fsrc, out):
        self.cm, self.ubh, self.rrh, self.fth, self.yr = cm, ubh, rrh, fth, yr
        self.usrc, self.fsrc, self.out = usrc, fsrc, out
        self.x, self.z, self.y, _ = coords()
        self.u, self.f, self.r, self.yc = {}, {}, {}, {}
        self.nw = self.nst = self.nr = self.ntt = 0
        self.win, self.stc, self.rwin, self.ttc = {}, {}, {}, {}
        self.loaded = {}
    def work(self, ft, uw, st, rw, tt):
        self.ft, self.uw, self.st, self.rw, self.tt = ft, uw, st, rw, tt
    def axis(self, c):
        return FEATURE_AXIS[CHUNK_FEATURES[c]]
    def pos(self, axis):
        return self.x if axis == "x" else self.z
    def block(self, k, t):
        src = self.fsrc[k]
        return src.at[t] if FEATURE_AXIS[k] == "x" else src.at[:, t]
    def send_f(self, k):
        axis = FEATURE_AXIS[k]
        me = self.pos(axis)
        def one(d):
            return self.cm.remote(lambda: self.block(k, (me + d) % 4), lambda: self.fth.at[k, d - 1], (axis, d))
        self.f[k] = [one(d) for d in (1, 3, 2)]
    def send_u(self, c):
        def one(d):
            return self.cm.remote(lambda: self.usrc[c], lambda: self.ubh.at[c, d - 1], (self.axis(c), d))
        self.u[c] = [one(d) for d in (1, 3, 2)]
    def load_f(self, k):
        s = FEATURE_SLOT[k]
        me = self.pos(FEATURE_AXIS[k])
        cps = [self.cm.local(self.block(k, me), self.ft.at[s, :, :, pl.ds(0, 256)])]
        for c in self.f[k]:
            c.wait_recv()
        for d in (1, 2, 3):
            cps.append(self.cm.local(self.fth.at[k, d - 1], self.ft.at[s, :, :, pl.ds(d * 256, 256)]))
        self.loaded[k] = cps
    def prep(self, c):
        k = CHUNK_FEATURES[c]
        if k not in self.loaded:
            self.load_f(k)
        w = self.nw % 2
        self.nw += 1
        cps = [self.cm.local(self.usrc[c], self.uw.at[w, 0])]
        for u in self.u[c]:
            u.wait_recv()
        cps.append(self.cm.local(self.ubh.at[c], self.uw.at[w, pl.ds(1, 3)]))
        self.win[c] = (w, cps)
    def mm(self, c):
        k = CHUNK_FEATURES[c]
        for l in self.loaded[k]:
            l.wait()
        self.loaded[k] = []
        w, cps = self.win[c]
        for l in cps:
            l.wait()
        i = self.nst % 3
        self.nst += 1
        for old in self.stc.get(i, []):
            self.cm.sent(old)
        s = self.st
        for h in (0, 2):
            v = dot(self.ft[FEATURE_SLOT[k], h:h + 2].reshape(320, 1024), self.uw[w].reshape(1024, 640))
            s[i, h:h + 2] = v.astype(BF).reshape(2, 160, 640)
        axis = "z" if self.axis(c) == "x" else "x"
        me = self.pos(axis)
        cps = [self.cm.remote(s.at[i, (me + d) % 4], self.rrh.at[c, d - 1], (axis, d)) for d in (1, 3, 2)]
        self.stc[i] = cps
        t = self.ntt % 6
        self.ntt += 1
        self.r[c] = (t, cps)
        for old in self.ttc.get(t, []):
            self.cm.sent(old)
        self.tt[t] = s[i, me].reshape(2, 80, 640)
    def rprep(self, c):
        t, cps = self.r[c]
        for r in cps:
            r.wait_recv()
        w = self.nr % 2
        self.nr += 1
        self.rwin[c] = (w, self.cm.local(self.rrh.at[c], self.rw.at[w]))
    def rsum(self, c):
        t, _ = self.r[c]
        w, l = self.rwin[c]
        l.wait()
        total = (self.tt[t].reshape(160, 640).astype(F32) + self.rw[w, 0].astype(F32)) + (self.rw[w, 1].astype(F32) + self.rw[w, 2].astype(F32))
        self.tt[t] = total.astype(BF).reshape(2, 80, 640)
        cp = self.cm.remote(self.tt.at[t, 1 - self.y], self.yr.at[c], ("y", 1))
        self.ttc[t] = [cp]
        self.yc[c] = cp
    def fin(self, c):
        self.yc[c].wait_recv()
        t, _ = self.r[c]
        self.out(c, self.tt[t, self.y].astype(F32) + self.yr[c].astype(F32))

def spread(cm, src, dst, axis):
    return [cm.remote(src(d), dst.at[d - 1], (axis, d)) for d in (1, 3, 2)]

def arrived(cps):
    for c in cps:
        c.wait_recv()

def tail_kernel(par, n2_h, dt_h, w_in, w_dn, n1t_h, z_h, cv_h, xb_h, yb_h, gx_h, ga_h, hs_h, msk_h, r_h, g_h, wg_h, tk_h, h1_h, w_t, wo_h,
                bo_o, dtok_o, in_o, dn_o, xy_o, wout_o, gate_o, sm_o, ubh, rrh, fth,
                un, yr, fts, dr, pd, pm, bob, dto, gs, gr, sm, sgr, sgt, sgr2, sgy, sma, smr, smy,
                m1, m2, m3, d1, d2, d3, e1, e2, e3, f1, f2, f3, gnb, rb, h1, dtb, tk,
                ssem, rsem, lsem):
    cm = Comm(ssem, rsem, lsem)
    f = lax.axis_index("fsdp")
    x, z, y, _ = coords()
    own = pl.ds(pl.multiple_of(f * 64, 64), 64)
    rd = Reduce(cm, pd, d1, d2, d3)
    rm = Reduce(cm, pm, m1, m2, m3)
    def put(c, v):
        if c < 6:
            in_o[c // 3, :, c % 3 * 640:c % 3 * 640 + 640] = v
        elif c < 9:
            dn_o[:, (c - 6) * 640:(c - 6) * 640 + 640] = v
        elif c < 11:
            xy_o[c - 9] = v.T
        else:
            wout_o[...] = v.T
    usrc = [un.at[c] for c in range(9)] + [None, None, z_h]
    S = Sums(cm, ubh, rrh, fth, yr, usrc, [fts.at[0], fts.at[1], n1t_h, n1t_h, fts.at[0]], put)
    lh = [cm.local(h1_h, h1), cm.local(g_h, gnb), cm.local(r_h, rb), cm.local(dt_h.at[own], dtb), cm.local(tk_h.at[:, own], tk)]

    w = pltpu.VMEM((256, 640), F32)

    def ffn_phase(wa, wd, am, ad, fg, fu, fd, n2, dt):
        ln = [cm.local(n2_h, n2), cm.local(dt_h, dt)]
        def load(i):
            s = i % 2
            return [cm.local(w_in.at[:, :, pl.ds(i * 640, 640)], wa.at[s]), cm.local(w_dn.at[pl.ds(i * 640, 640)], wd.at[s])]
        lw = {0: load(0), 1: load(1)}
        b = pltpu.get_barrier_semaphore()
        for axis, d in REP:
            pl.semaphore_signal(b, inc=1, device_id=peer(axis, d), device_id_type=MESH)
        for d in (1, 2, 3):
            pl.semaphore_signal(b, inc=1, device_id=fpeer(d), device_id_type=MESH)
        for c in ln:
            c.wait()
        pl.semaphore_wait(b, len(REP) + 3)
        for c in range(4):
            fts[0, c] = n2[:, c * 640:c * 640 + 640].T.reshape(4, 160, 256)
        S.send_f(0)
        for c in range(4):
            fts[1, c] = dt[:, c * 640:c * 640 + 640].T.reshape(4, 160, 256)
        S.send_f(1)
        S.send_u(11)
        for i in range(3):
            s = i % 2
            lw[i][0].wait()
            fg[...] = dot(n2[...], wa[s, 0])
            fu[...] = dot(n2[...], wa[s, 1])
            for q in range(5):
                gl, _ = gelu_parts(fg[:, lanes(q)])
                un[6 + i, :, lanes(q)] = (gl * fu[:, lanes(q)]).astype(BF)
            S.send_u(6 + i)
            lw[i][1].wait()
            fd[...] = dot_nt(dt[...], wd[s])
            for q in range(5):
                gl, dgl = gelu_parts(fg[:, lanes(q)])
                dh = fd[:, lanes(q)]
                un[i, :, lanes(q)] = (dh * fu[:, lanes(q)] * dgl).astype(BF)
                un[3 + i, :, lanes(q)] = (dh * gl).astype(BF)
            S.send_u(i)
            S.send_u(3 + i)
            for c in range(4):
                cs = slice(c * 640, c * 640 + 640)
                v = dot_nt(un[i], wa[s, 0, cs, :]) + dot_nt(un[3 + i], wa[s, 1, cs, :])
                if i == 0:
                    ad[:, cs] = v
                elif i == 1:
                    ad[:, cs] = ad[:, cs] + v
                else:
                    pd[c] = (ad[:, cs] + v).astype(BF).reshape(4, 64, 640)
                    rd.send(c)
                    if c: rd.mid(c - 1)
            if i == 2:
                rd.mid(3)
            for c in range(4):
                cs = slice(c * 640, c * 640 + 640)
                v = dot(un[6 + i], wd[s, :, cs])
                if i == 0:
                    am[:, cs] = v
                elif i == 1:
                    am[:, cs] = am[:, cs] + v
                else:
                    pm[c] = (am[:, cs] + v).astype(BF).reshape(4, 64, 640)
            if i == 0:
                lw[2] = load(2)
        S.send_f(3)
        S.send_f(2)

    pl.run_scoped(ffn_phase, pltpu.VMEM((2, 2, 2560, 640), BF), pltpu.VMEM((2, 640, 2560), BF), pltpu.VMEM((256, 2560), F32), pltpu.VMEM((256, 2560), F32), w, w, w, pltpu.VMEM((256, 2560), BF), pltpu.VMEM((256, 2560), BF))

    def chain_phase(cv, xb, yb, gx, ga, hs, msk, wg, wbuf, aa, uu, gg, dc1, dp, dna, ft, uw, st, rw, tt, bo, dob, sg, dxy, dxx, pb, dnp, dh1):
        S.work(ft, uw, st, rw, tt)
        S.usrc[9], S.usrc[10] = dxy.at[0], dxy.at[1]
        lb = [cm.local(wo_h, wbuf.at[0]), cm.local(yb_h, yb), cm.local(hs_h, hs), cm.local(ga_h, ga), cm.local(msk_h, msk), cm.local(gx_h, gx), cm.local(cv_h, cv),
              cm.local(wg_h, wg), cm.local(xb_h, xb), cm.local(w_t.at[1], wbuf.at[1])]
        for c in range(4):
            rm.send(c)
        S.prep(6)
        for c in lh:
            c.wait()
        gs[...] = jnp.zeros_like(gs)
        r2 = rb[256:320, 0:1]
        acc = jnp.zeros((64, 1), F32)
        for c in range(4):
            cs = slice(c * 640, c * 640 + 640)
            dn = rd.fin(c)
            h = h1[:, cs]
            gs[c, 1:2, :] = jnp.sum(dn * h * r2, axis=0, keepdims=True)
            v = dn * gnb[c, 1:2, :]
            dh1[:, cs] = v
            acc = acc + jnp.sum(v * h, axis=-1, keepdims=True)
        acc = acc * (1.0 / 2560) * (r2 * r2 * r2)
        for c in range(4):
            cs = slice(c * 640, c * 640 + 640)
            d = dtb[:, cs].astype(F32) + r2 * dh1[:, cs] - h1[:, cs] * acc
            dh1[:, cs] = d
            dr[f, :, cs] = d.astype(BF)
        gdr = Gather(cm, dr, None, [(pl.ds(0, 32),), (pl.ds(32, 32),)])
        gdr.start()
        for c in range(4):
            rm.mid(c)
        S.mm(6)
        for c in lb:
            c.wait()
        for q in range(5):
            sp, a, spread_, mult = decay_of(q, ga[:, lanes(q)], par, msk[0])
            up = pltpu.roll(jnp.where(msk[0] == 1.0, 0.0, a), 255, axis=0)
            rows = lax.broadcasted_iota(jnp.int32, (256, 128), 0)
            aa[:, lanes(q)] = jnp.where(rows == 255, 0.0, up)
        gdr.relay()
        S.prep(0)
        S.mm(0)
        gdr.finish()
        uu[...] = dot_nt(dr[...].reshape(256, 2560), wbuf[0])
        lw0 = cm.local(w_t.at[0], wbuf.at[0])
        for q in range(5):
            yg, dgl = gelu_parts(yb[:, lanes(q)])
            dz = uu[:, lanes(q)]
            dxy[1, :, lanes(q)] = (dz * hs[:, lanes(q)] * dgl).astype(BF)
            uu[:, lanes(q)] = dz * yg
        S.send_u(10)
        scan_rows(aa, uu, gg, True)
        re = Reduce(cm, pb, e1, e2, e3)
        for q in range(5):
            ls = lanes(q)
            start = msk[0]
            gxq, gaq, g = gx[:, ls], ga[:, ls], gg[:, ls]
            sp, a, spread_, mult = decay_of(q, gaq, par, start)
            cvq = cv[f, :, ls].astype(F32)
            prev = jnp.where(start == 1.0, 0.0, pltpu.roll(hs[:, ls], 1, axis=0))
            slope = jnp.where((start == 1.0) | (spread_ <= 0.01), 0.0, -a / mult)
            da = g * prev + g * gxq * cvq * slope
            dc1[:, ls] = g * mult * gxq
            dlog = da * a
            da_p = jnp.sum(dlog * (-8.0 * gaq), axis=0, keepdims=True) * sigmoid(par[7:8, ls])
            px = (g * mult * cvq * gxq * (1.0 - gxq)).astype(BF)
            pa = (-8.0 * dlog * sp * gaq * (1.0 - gaq)).astype(BF)
            dp[q, :, 0:128] = px
            dp[q, :, 128:256] = pa
            sm[7:8, ls] = jnp.sum(px.astype(F32), axis=0, keepdims=True)
            sm[8:9, ls] = jnp.sum(pa.astype(F32), axis=0, keepdims=True)
            sm[9:10, ls] = da_p
            db = dot(dp[q], wg[q]).astype(BF)
            for p in range(4):
                pb[q, p] = db[:, lanes(p)]
            re.send(q)
            if q: re.mid(q - 1)
        re.mid(4)
        for old in S.f[0]:
            cm.sent(old)
        drt = dr[...].reshape(256, 2560)
        for c in range(4):
            fts[0, c] = drt[:, c * 640:c * 640 + 640].T.reshape(4, 160, 256)
        S.send_f(4)
        for c in range(4):
            cs = slice(c * 640, c * 640 + 640)
            dna[c] = dot(dxy[1], wbuf[1, :, cs])
        low = lax.broadcasted_iota(jnp.int32, (64, 128), 1) < 64
        for q in range(5):
            lhs = jnp.concatenate([cv[p, :, lanes(q)] for p in range(4)], axis=1)
            gwt = dot_tn(lhs, dp[q])
            for p in range(4):
                for k in range(2):
                    blk = gwt[p * 128:p * 128 + 128, k * 128:k * 128 + 128]
                    sg[p, k, q] = jnp.where(low, blk[0:64], blk[64:128]).astype(BF)
        g1 = spread(cm, lambda d: sg.at[(x + d) % 4], sgr, "x")
        S.prep(3)
        live = msk[4, own, 0:1]
        for c in range(4):
            bo[c] = (live * (h1[:, c * 640:c * 640 + 640] + rm.fin(c))).astype(BF)
        sbo = Swap(cm, bo, bob)
        S.mm(3)
        S.rprep(6)
        S.rsum(6)
        for q in range(5):
            ls = lanes(q)
            d = dc1[:, ls] + re.fin(q)
            xq = xb[:, ls]
            sm[6:7, ls] = jnp.sum(d, axis=0, keepdims=True)
            sm[2:3, ls] = jnp.sum(d * xq, axis=0, keepdims=True)
            dx = par[0:1, ls] * d
            for k in (1, 2, 3):
                m = d * msk[k]
                sm[2 + k:3 + k, ls] = jnp.sum(m * pltpu.roll(xq, k, axis=0), axis=0, keepdims=True)
                dx = dx + par[k:k + 1, ls] * pltpu.roll(m, 256 - k, axis=0)
            dxy[0, :, ls] = dx.astype(BF)
        S.send_u(9)
        lw0.wait()
        rf = Reduce(cm, dnp, f1, f2, f3)
        for c in range(4):
            cs = slice(c * 640, c * 640 + 640)
            dnp[c] = (dna[c] + dot(dxy[0], wbuf[0, :, cs])).astype(BF).reshape(4, 64, 640)
            rf.send(c)
            if c: rf.mid(c - 1)
        rf.mid(3)
        S.prep(7)
        S.mm(7)
        S.rprep(0)
        S.rsum(0)
        r1 = rb[own, 0:1]
        acc = jnp.zeros((64, 1), F32)
        for c in range(4):
            dn = rf.fin(c)
            xr = tk[c].astype(F32)
            gs[c, 0:1, :] = jnp.sum(dn * xr * r1, axis=0, keepdims=True)
            v = dn * gnb[c, 0:1, :]
            dna[c, 0:64, :] = v
            acc = acc + jnp.sum(v * xr, axis=-1, keepdims=True)
        acc = acc * (1.0 / 2560) * (r1 * r1 * r1)
        for c in range(4):
            dob[c] = (dh1[:, c * 640:c * 640 + 640] + r1 * dna[c, 0:64, :] - tk[c].astype(F32) * acc).astype(BF)
        sdt = Swap(cm, dob, dto)
        gcp = []
        for d in (3, 2, 1):
            _, t = fpeer(d)
            gcp.append(cm.remote(gs.at[t], gr.at[d - 1], ("f", d)))
        sbo.finish()
        outs = [cm.local(bob, bo_o)]
        arrived(g1)
        t = (sg[x].astype(F32) + sgr[0].astype(F32)) + (sgr[1].astype(F32) + sgr[2].astype(F32))
        sgt[...] = t.astype(BF)
        g2 = spread(cm, lambda d: sgt.at[:, :, pl.ds(pl.multiple_of((z + d) % 4 * 16, 16), 16)], sgr2, "z")
        arrived(gcp)
        sm[0:2, :] = (gs[f, 0:2, :] + gr[0, 0:2, :]) + (gr[1, 0:2, :] + gr[2, 0:2, :])
        sm[10:16, :] = jnp.zeros((6, 640), F32)
        sma[0] = sm[...]
        v1 = spread(cm, lambda d: sma.at[0], smr.at[0], "x")
        sdt.finish()
        dxx[...] = dto[...].astype(F32).reshape(256, 640)
        outs.append(cm.local(dxx, dtok_o))
        small = {}
        def small_step(j):
            if j == 0:
                arrived(g2)
                sgy[0] = sgt[:, :, pl.ds(pl.multiple_of(z * 16, 16), 16), :].astype(F32) + sgr2[0].astype(F32) + sgr2[1].astype(F32) + sgr2[2].astype(F32)
                small[0] = cm.remote(sgy.at[0], sgy.at[1], ("y", 1))
                arrived(v1)
                sma[1] = (sma[0] + smr[0, 0]) + (smr[0, 1] + smr[0, 2])
                small[1] = spread(cm, lambda d: sma.at[1], smr.at[1], "z")
            if j == 1:
                arrived(small[1])
                sma[2] = (sma[1] + smr[1, 0]) + (smr[1, 1] + smr[1, 2])
                small[2] = cm.remote(sma.at[2], smy, ("y", 1))
                small[0].wait_recv()
                half = pl.ds(pl.multiple_of(y * 8, 8), 8)
                gate_o[...] = sgy[0, :, :, half, :] + sgy[1, :, :, half, :]
            if j == 2:
                small[2].wait_recv()
                sm_o[...] = sma[2] + smy[...]
        rest = [1, 8, 4, 11, 2, 10, 5, 9]
        every = [6, 0, 3, 7] + rest
        S.prep(rest[0])
        for j in range(len(rest) + 4):
            i = j + 4
            if i < 12:
                S.mm(every[i])
                if i + 1 < 12: S.prep(every[i + 1])
            small_step(j)
            if i - 2 < 12:
                S.rprep(every[i - 2])
                S.rsum(every[i - 2])
            S.fin(every[i - 4])
        for c in outs:
            c.wait()
        cm.drain()

    pl.run_scoped(chain_phase, pltpu.VMEM((4, 256, 640), BF), w, w, w, w, w, pltpu.VMEM((5, 256, 128), F32), pltpu.VMEM((5, 256, 512), BF), pltpu.VMEM((2, 640, 2560), BF),
                  w, w, w, w, pltpu.VMEM((5, 256, 256), BF), pltpu.VMEM((4, 256, 640), F32),
                  pltpu.VMEM((3, 4, 160, 1024), BF), pltpu.VMEM((2, 4, 256, 640), BF), pltpu.VMEM((3, 4, 160, 640), BF), pltpu.VMEM((2, 3, 160, 640), BF), pltpu.VMEM((6, 2, 80, 640), BF),
                  pltpu.VMEM((4, 64, 640), BF), pltpu.VMEM((4, 64, 640), BF), pltpu.VMEM((4, 2, 5, 64, 128), BF), pltpu.VMEM((2, 256, 640), BF), w,
                  pltpu.VMEM((5, 4, 256, 128), BF), pltpu.VMEM((4, 4, 64, 640), BF), pltpu.VMEM((64, 2560), F32))

def tail(par, n2, dt, w_in, w_dn, n1t, z, cv, xb, yb, gx, ga, hs, msk, r, g, wg, tk, h1, w_t, wo):
    s = jax.ShapeDtypeStruct
    R = 256
    V = pltpu.VMEM
    out_shape = [s((4, 64, 640), BF), s((R, 640), F32), s((2, 80, 1920), F32), s((80, 1920), F32), s((2, 640, 80), F32), s((640, 80), F32),
                 s((2, 5, 8, 128), F32), s((16, 640), F32), s((12, 3, R, 640), BF), s((12, 3, 160, 640), BF), s((5, 3, 4, 160, 256), BF)]
    blk = V((4, 4, 64, 640), BF)
    row = V((4, 64, 640), BF)
    red = [V((4, 2, 64, 640), BF), row, row]
    red5 = [V((5, 2, R, 128), BF), V((5, R, 128), BF), V((5, R, 128), BF)]
    scratch = [V((9, R, 640), BF), V((12, 80, 640), BF), V((2, 4, 4, 160, 256), BF), V((4, 64, 2560), BF), blk, blk, row, row,
               V((4, 8, 640), F32), V((3, 8, 640), F32), V((16, 640), F32),
               V((3, 2, 5, 64, 128), BF), V((2, 5, 64, 128), BF), V((3, 2, 5, 16, 128), BF), V((2, 2, 5, 16, 128), F32),
               V((3, 16, 640), F32), V((2, 3, 16, 640), F32), V((16, 640), F32)] + red + red + red5 + red + [
               V((4, 8, 640), F32), V((320, 128), F32), V((64, 2560), F32), V((64, 2560), BF), V((4, 64, 640), BF),
               pltpu.SemaphoreType.DMA((224,)), pltpu.SemaphoreType.DMA((224,)), pltpu.SemaphoreType.DMA((128,))]
    return pl.pallas_call(
        tail_kernel, out_shape=out_shape,
        in_specs=[VMEM] + [ANY] * 20,
        out_specs=[ANY] * 2 + [VMEM] * 6 + [ANY] * 3,
        scratch_shapes=scratch,
        compiler_params=pltpu.CompilerParams(collective_id=5, has_side_effects=True, vmem_limit_bytes=VM),
        name="tail",
    )(par, n2, dt, w_in, w_dn, n1t, z, cv, xb, yb, gx, ga, hs, msk, r, g, wg, tk, h1, w_t, wo)

def body(tokens, seq_len, seq_owner, gain_1, gain_2, w_xy, conv_w, conv_b, gate_w, gate_b, a_param, w_out, w_in, w_down, cotangent):
    lenc, ownc, ownr, par, gn, w_t, gw_t, wo = prep(seq_len, seq_owner, gain_1, gain_2, w_xy, conv_w, conv_b, gate_w, gate_b, a_param, w_out)
    (n1, cv, xb, yb, gx, ga, hs, z, n2, dt, h1, msk, r, g, wg, tk, n1t) = forward(lenc, ownc, ownr, par, gn, tokens, cotangent, w_t, gw_t, wo)
    bo, dtok, r_in, r_dn, r_xy, r_wo, r_gate, r_sm = tail(par, n2.reshape(256, 2560), dt, w_in, w_down, n1t, z, cv, xb, yb, gx, ga, hs, msk, r, g, wg, tk, h1, w_t, wo)[:8]
    red_xy = jnp.transpose(r_xy.reshape(2, 10, 64, 80), (0, 3, 1, 2))
    red_gate = jnp.transpose(r_gate.reshape(2, 5, 8, 2, 64), (0, 1, 3, 2, 4)).reshape(2, 10, 8, 64)
    return (bo.reshape(256, 640), dtok, r_sm[0], r_sm[1], red_xy, r_sm[2:6].reshape(4, 10, 64), r_sm[6].reshape(10, 64),
            red_gate, r_sm[7:9].reshape(2, 10, 64), r_sm[9].reshape(10, 64), r_wo.reshape(10, 64, 80), r_in, r_dn.T)


def solution(mesh):
    return jax.shard_map(
        body,
        mesh=mesh,
        in_specs=(
            P("rep", "fsdp"), P(), P(), P("fsdp"), P("fsdp"), P(None, None, None, "fsdp"), P(None, None, "fsdp"), P(None, "fsdp"),
            P(None, None, None, "fsdp"), P(None, None, "fsdp"), P(None, "fsdp"), P(None, "fsdp", None), P(None, None, "fsdp"), P("fsdp", None), P("rep", "fsdp"),
        ),
        out_specs=(
            P("rep", "fsdp"), P("rep", "fsdp"), P("fsdp"), P("fsdp"), P(None, "rep", None, "fsdp"), P(None, None, "fsdp"), P(None, "fsdp"),
            P(None, None, "rep", "fsdp"), P(None, None, "fsdp"), P(None, "fsdp"), P(None, "fsdp", "rep"), P(None, "rep", "fsdp"), P("fsdp", "rep"),
        ),
        check_vma=False,
    )
```

```python
import functools

import jax
import jax.numpy as jnp
from jax import lax
from jax.experimental import pallas as pl
from jax.experimental.pallas import tpu as pltpu
from jax.sharding import PartitionSpec as P

MESH = pl.DeviceIdType.MESH
VM = 63 * 2**20
GC = 0.7978845608028654

def gelu_parts(v):
    v2 = v * v
    t = jnp.tanh(GC * v * (1.0 + 0.044715 * v2))
    half = 0.5 * (1.0 + t)
    g = v * half
    dg = half + 0.5 * v * (1.0 - t * t) * (GC * (1.0 + 3 * 0.044715 * v2))
    return g, dg

def dot(a, b):
    return jnp.dot(a, b, preferred_element_type=jnp.float32)

def dot_nt(a, b):
    return lax.dot_general(a, b, (((1,), (1,)), ((), ())), preferred_element_type=jnp.float32)

def ffn_kernel(n2, dt, w_in, w_dn, hid, dg, du, mlp, dn2, n2t, dtt, am, ad):
    i = pl.program_id(0)
    @pl.when(i == 1)
    def _():
        for c in range(4):
            n2t[c] = n2[:, c * 640:c * 640 + 640].T.reshape(4, 160, 256)
            dtt[c] = dt[:, c * 640:c * 640 + 640].T.reshape(4, 160, 256)
    @pl.when(i == 0)
    def _():
        am[...] = jnp.zeros_like(am)
        ad[...] = jnp.zeros_like(ad)
    gate = dot(n2[...], w_in[0])
    up = dot(n2[...], w_in[1])
    g, dgl = gelu_parts(gate)
    h = (g * up).astype(jnp.bfloat16)
    hid[0] = h
    dh = dot_nt(dt[...], w_dn[...])
    a = (dh * up * dgl).astype(jnp.bfloat16)
    b = (dh * g).astype(jnp.bfloat16)
    dg[0] = a
    du[0] = b
    am[...] += dot(h, w_dn[...])
    ad[...] += dot_nt(a, w_in[0])
    ad[...] += dot_nt(b, w_in[1])
    @pl.when(i == 2)
    def _():
        for c in range(4):
            mlp[c] = am[:, c * 640:c * 640 + 640].astype(jnp.bfloat16).reshape(4, 64, 640)
            dn2[c] = ad[:, c * 640:c * 640 + 640].astype(jnp.bfloat16).reshape(4, 64, 640)

def ffn(n2, dt, w_in, w_dn):
    R, D = n2.shape
    T = 640
    nt = w_dn.shape[0] // T
    full = pl.BlockSpec((R, D), lambda i: (0, 0))
    tile = pl.BlockSpec((1, R, T), lambda i: (i, 0, 0))
    ch = jax.ShapeDtypeStruct((nt, R, T), jnp.bfloat16)
    rd = jax.ShapeDtypeStruct((4, 4, 64, 640), jnp.bfloat16)
    td = jax.ShapeDtypeStruct((4, 4, 160, 256), jnp.bfloat16)
    part = pl.BlockSpec((4, 4, 64, 640), lambda i: (0, 0, 0, 0))
    turned = pl.BlockSpec((4, 4, 160, 256), lambda i: (0, 0, 0, 0))
    return pl.pallas_call(
        ffn_kernel, grid=(nt,),
        in_specs=[full, full, pl.BlockSpec((2, D, T), lambda i: (0, 0, i)), pl.BlockSpec((T, D), lambda i: (i, 0))],
        out_specs=[tile, tile, tile, part, part, turned, turned],
        out_shape=[ch, ch, ch, rd, rd, td, td],
        scratch_shapes=[pltpu.VMEM((R, D), jnp.float32)] * 2,
        compiler_params=pltpu.CompilerParams(vmem_limit_bytes=VM),
        name="ffn",
    )(n2, dt, w_in, w_dn)

def coords():
    r = lax.axis_index("rep")
    f = lax.axis_index("fsdp")
    return r // 8, (r // 2) % 4, r % 2, f

def peer(axis, d):
    x, z, y, f = coords()
    if axis == "x":
        x = (x + d) % 4
    elif axis == "z":
        z = (z + d) % 4
    elif axis == "y":
        y = 1 - y
    else:
        f = (f + d) % 4
    return ((x * 4 + z) * 2 + y, f)

class Grads:
    def __init__(self, plan, fplan):
        self.plan = plan
        self.fplan = fplan
    def scratch(self):
        n, m = len(self.plan), len(self.fplan)
        b = jnp.bfloat16
        return [
            pltpu.VMEM((n, 4, 256, 640), b),
            pltpu.VMEM((m, 4, 160, 1024), b),
            pltpu.VMEM((n, 4, 160, 640), b),
            pltpu.VMEM((n, 3, 160, 640), b),
            pltpu.VMEM((n, 2, 80, 640), b),
            pltpu.VMEM((n, 80, 640), b),
            pltpu.SemaphoreType.DMA((n, 3)), pltpu.SemaphoreType.DMA((n, 3)),
            pltpu.SemaphoreType.DMA((m, 3)), pltpu.SemaphoreType.DMA((m, 3)),
            pltpu.SemaphoreType.DMA((n, 3)), pltpu.SemaphoreType.DMA((n, 3)),
            pltpu.SemaphoreType.DMA((n,)), pltpu.SemaphoreType.DMA((n,)),
            pltpu.SemaphoreType.DMA((n,)), pltpu.SemaphoreType.DMA((m,)),
        ]
    def bind(self, refs, usrc, fsrc, out):
        (self.ub, self.ft, self.st, self.rr, self.tt, self.yr, self.us, self.ur, self.fs, self.fr,
         self.rq, self.rv, self.ys, self.yv, self.lu, self.lf) = refs
        self.usrc, self.fsrc, self.out = usrc, fsrc, out
    def rc(self, src, dst, s, r, axis, d):
        return pltpu.make_async_remote_copy(src_ref=src, dst_ref=dst, send_sem=s, recv_sem=r, device_id=peer(axis, d), device_id_type=MESH)
    def fcopies(self, k):
        i, axis = self.fplan[k]
        x, z, y, f = coords()
        src = self.fsrc[i]
        me = x if axis == "x" else z
        pick = (lambda t: src.at[t]) if axis == "x" else (lambda t: src.at[:, t])
        loc = pltpu.make_async_copy(pick(me), self.ft.at[k, :, :, pl.ds(0, 256)], self.lf.at[k])
        rem = [self.rc(pick((me + d) % 4), self.ft.at[k, :, :, pl.ds(d * 256, 256)], self.fs.at[k, d - 1], self.fr.at[k, d - 1], axis, d) for d in (1, 3, 2)]
        return loc, rem
    def ucopies(self, c):
        k, axis = self.plan[c]
        src = self.usrc(c)
        loc = pltpu.make_async_copy(src, self.ub.at[c, 0], self.lu.at[c])
        rem = [self.rc(src, self.ub.at[c, d], self.us.at[c, d - 1], self.ur.at[c, d - 1], axis, d) for d in (1, 3, 2)]
        return loc, rem
    def rscopies(self, c):
        k, axis = self.plan[c]
        ra = "z" if axis == "x" else "x"
        x, z, y, f = coords()
        me = z if axis == "x" else x
        return me, [self.rc(self.st.at[c, (me + d) % 4], self.rr.at[c, d - 1], self.rq.at[c, d - 1], self.rv.at[c, d - 1], ra, d) for d in (1, 3, 2)]
    def ycopy(self, c):
        x, z, y, f = coords()
        return self.rc(self.tt.at[c, 1 - y], self.yr.at[c], self.ys.at[c], self.yv.at[c], "y", 0)
    def send_f(self, k):
        loc, rem = self.fcopies(k)
        loc.start()
        for r in rem: r.start()
    def send_u(self, c):
        loc, rem = self.ucopies(c)
        loc.start()
        for r in rem: r.start()
    def mm(self, c):
        k, axis = self.plan[c]
        loc, rem = self.ucopies(c)
        loc.wait()
        for r in rem: r.wait()
        if not self.fdone[k]:
            loc, rem = self.fcopies(k)
            loc.wait()
            for r in rem: r.wait()
            self.fdone[k] = True
        self.st[c] = dot(self.ft[k].reshape(640, 1024), self.ub[c].reshape(1024, 640)).astype(jnp.bfloat16).reshape(4, 160, 640)
        me, cps = self.rscopies(c)
        for r in cps: r.start()
    def rs(self, c):
        me, cps = self.rscopies(c)
        for r in cps: r.wait()
        f = jnp.float32
        t = (self.st[c, me].astype(f) + self.rr[c, 0].astype(f)) + (self.rr[c, 1].astype(f) + self.rr[c, 2].astype(f))
        self.tt[c] = t.astype(jnp.bfloat16).reshape(2, 80, 640)
        self.ycopy(c).start()
    def fin(self, c):
        x, z, y, f = coords()
        self.ycopy(c).wait()
        self.out[c] = self.tt[c, y].astype(jnp.float32) + self.yr[c].astype(jnp.float32)

def entry_barrier(peers):
    b = pltpu.get_barrier_semaphore()
    for axis, d in peers:
        pl.semaphore_signal(b, inc=1, device_id=peer(axis, d), device_id_type=MESH)
    pl.semaphore_wait(b, len(peers))

REP = [("x", 1), ("x", 2), ("x", 3), ("z", 1), ("z", 2), ("z", 3), ("y", 1)]

PLAN = [(0, "x")] * 6 + [(1, "z")] * 3 + [(2, "x"), (3, "z"), (4, "z")]
FPLAN = [(0, "x"), (1, "z"), (2, "x"), (2, "z"), (3, "z")]

def grads_kernel(g, n2t, dtt, n1t, drt, dgs, dus, hids, dxs, zs, out, *refs):
    def usrc(c):
        if c < 3: return dgs.at[c]
        if c < 6: return dus.at[c - 3]
        if c < 9: return hids.at[c - 6]
        if c < 11: return dxs.at[c - 9]
        return zs
    g.bind(refs, usrc, [n2t, dtt, n1t, drt], out)
    g.fdone = [False] * len(g.fplan)
    entry_barrier(REP)
    g.send_f(0); g.send_f(1)
    order = [0, 6, 1, 3, 7, 2, 4, 8, 5, 9, 10, 11]
    for j, c in enumerate(order):
        if j == 6:
            for k in (2, 3, 4): g.send_f(k)
        g.send_u(c)
    n = len(order)
    for j in range(n + 4):
        if j < n: g.mm(order[j])
        if 0 <= j - 2 < n: g.rs(order[j - 2])
        if 0 <= j - 4 < n: g.fin(order[j - 4])

def grads(n2t, dtt, n1t, drt, dgs, dus, hids, dxs, zs):
    g = Grads(PLAN, FPLAN)
    return pl.pallas_call(
        functools.partial(grads_kernel, g),
        out_shape=jax.ShapeDtypeStruct((12, 80, 640), jnp.float32),
        in_specs=[pl.BlockSpec(memory_space=pl.ANY)] * 9,
        out_specs=pl.BlockSpec(memory_space=pltpu.VMEM),
        scratch_shapes=g.scratch(),
        compiler_params=pltpu.CompilerParams(collective_id=7, has_side_effects=True, vmem_limit_bytes=VM),
        name="grads",
    )(n2t, dtt, n1t, drt, dgs, dus, hids, dxs, zs)

F32 = jnp.float32
BF = jnp.bfloat16
EPS = 1e-06
ANY = pl.BlockSpec(memory_space=pl.ANY)
VMEM = pl.BlockSpec(memory_space=pltpu.VMEM)

def fpeer(d):
    r = lax.axis_index("rep")
    f = lax.axis_index("fsdp")
    h, c = f // 2, f % 2
    if d % 2:
        c = 1 - c
    if d // 2:
        h = 1 - h
    return r, h * 2 + c

def device(to):
    axis, d = to
    return fpeer(d) if axis == "f" else peer(axis, d)

class Sent:
    def __init__(self, src, dst, to, ssem, rsem):
        self.src, self.dst, self.to, self.ssem, self.rsem = src, dst, to, ssem, rsem
    def make(self):
        return pltpu.make_async_remote_copy(
            src_ref=self.src(), dst_ref=self.dst(), send_sem=self.ssem(), recv_sem=self.rsem(), device_id=device(self.to), device_id_type=MESH)
    def wait_recv(self):
        self.make().wait_recv()
    def wait_send(self):
        self.make().wait_send()

class Comm:
    def __init__(self, ssem, rsem, lsem):
        self.ssem, self.rsem, self.lsem = ssem, rsem, lsem
        self.n = self.m = 0
        self.open = []
    def remote(self, src, dst, to):
        k = self.n
        self.n += 1
        c = Sent(src if callable(src) else lambda: src, dst if callable(dst) else lambda: dst, to, lambda: self.ssem.at[k], lambda: self.rsem.at[k])
        c.make().start()
        self.open.append(c)
        return c
    def local(self, src, dst):
        k = self.m
        self.m += 1
        c = pltpu.make_async_copy(src, dst, self.lsem.at[k])
        c.start()
        return c
    def sent(self, c):
        c.wait_send()
        self.open = [o for o in self.open if o is not c]
    def drain(self):
        for c in self.open:
            c.wait_send()
        self.open = []

class Gather:
    def __init__(self, comm, buf, own=None, parts=None):
        self.comm, self.buf = comm, buf
        self.f = lax.axis_index("fsdp")
        self.parts = parts or [()]
        self.own = own
        self.far, self.near = [], []
    def start(self):
        f, cm = self.f, self.comm
        for p in self.parts:
            dst = self.buf.at[(f, *p)]
            src = self.own.at[p] if self.own is not None else dst
            self.far.append(cm.remote(src, dst, ("f", 2)))
            self.near.append(cm.remote(src, dst, ("f", 1)))
    def relay(self):
        _, o = fpeer(2)
        self.late = []
        for p, c in zip(self.parts, self.far):
            c.wait_recv()
            dst = self.buf.at[(o, *p)]
            self.late.append(self.comm.remote(dst, dst, ("f", 1)))
    def finish(self):
        for c in self.near + self.late:
            c.wait_recv()

class Reduce:
    def __init__(self, comm, part, r1, s2, r2):
        self.comm, self.part, self.r1, self.s2, self.r2 = comm, part, r1, s2, r2
        self.f = lax.axis_index("fsdp")
        self.a, self.b, self.c = {}, {}, {}
    def send(self, c):
        self.a[c] = self.comm.remote(lambda: self.part.at[c, fpeer(3)[1]], lambda: self.r1.at[c, 1], ("f", 1))
        self.b[c] = self.comm.remote(lambda: self.part.at[c, fpeer(1)[1]], lambda: self.r1.at[c, 0], ("f", 1))
    def mid(self, c):
        _, o2 = fpeer(2)
        self.a[c].wait_recv()
        self.s2[c] = (self.part[c, o2].astype(F32) + self.r1[c, 1].astype(F32)).astype(BF)
        self.c[c] = self.comm.remote(lambda: self.s2.at[c], lambda: self.r2.at[c], ("f", 2))
    def fin(self, c):
        self.b[c].wait_recv()
        self.c[c].wait_recv()
        return self.part[c, self.f].astype(F32) + self.r1[c, 0].astype(F32) + self.r2[c].astype(F32)

def group_barrier(ds):
    b = pltpu.get_barrier_semaphore()
    for d in ds:
        pl.semaphore_signal(b, inc=1, device_id=fpeer(d), device_id_type=MESH)
    pl.semaphore_wait(b, len(ds))

def lanes(q):
    return slice(q * 128, q * 128 + 128)

def row_masks(lenr, ownr, msk):
    me = lax.axis_index("rep")
    j = lax.broadcasted_iota(jnp.int32, (128, 128), 0)
    i = lax.broadcasted_iota(jnp.int32, (128, 128), 1)
    counted = jnp.where(ownr[...] == me, lenr[...], 0)
    mine = jnp.sum(jnp.where(i == j, counted, 0), axis=1, keepdims=True)
    offset = jnp.sum(jnp.where(j < i, mine, 0), axis=0, keepdims=True)
    total = jnp.sum(mine, axis=0, keepdims=True)
    place = lax.broadcasted_iota(jnp.int32, (256, 128), 0)
    hit = jnp.where((ownr[...] == me) & (offset == place), 1.0, 0.0)
    start = jnp.broadcast_to(jnp.max(hit, axis=1, keepdims=True), (256, 128))
    msk[0] = start
    run = start
    for k in (1, 2, 3):
        msk[k] = jnp.where((run == 0.0) & (place >= k), 1.0, 0.0)
        run = jnp.maximum(run, jnp.where(place >= k, pltpu.roll(start, k, axis=0), 0.0))
    msk[4] = jnp.where(place < total, 1.0, 0.0)

def wide_gates(gw, wg):
    row = lax.broadcasted_iota(jnp.int32, (128, 128), 0) // 64
    col = lax.broadcasted_iota(jnp.int32, (128, 128), 1) // 64
    for q in range(5):
        for k in range(2):
            for g in range(2):
                v = gw[k, q * 128:q * 128 + 128, g * 128:g * 128 + 128].astype(F32)
                r = pltpu.roll(v, 64, axis=1)
                for e in range(2):
                    twice = jnp.where(col == e, v, r)
                    p = 2 * g + e
                    wg[q, k * 128:k * 128 + 128, p * 128:p * 128 + 128] = jnp.where(row == col, twice, 0.0).astype(BF)

def softplus(v):
    return jnp.maximum(v, 0.0) + jnp.log1p(jnp.exp(-jnp.abs(v)))

def sigmoid(v):
    return 1.0 / (1.0 + jnp.exp(-v))

def scan_rows(a_ref, u_ref, h_ref, back):
    rows = lax.broadcasted_iota(jnp.int32, (8, 640), 0)
    carry = jnp.zeros((1, 640), F32)
    order = range(31, -1, -1) if back else range(32)
    for i in order:
        a = a_ref[i * 8:i * 8 + 8, :]
        u = u_ref[i * 8:i * 8 + 8, :]
        for s in (1, 2, 4):
            if back:
                ok = rows < 8 - s
                a2 = jnp.where(ok, pltpu.roll(a, 8 - s, axis=0), 1.0)
                u2 = jnp.where(ok, pltpu.roll(u, 8 - s, axis=0), 0.0)
            else:
                ok = rows >= s
                a2 = jnp.where(ok, pltpu.roll(a, s, axis=0), 1.0)
                u2 = jnp.where(ok, pltpu.roll(u, s, axis=0), 0.0)
            u = u + a * u2
            a = a * a2
        h = u + a * carry
        h_ref[i * 8:i * 8 + 8, :] = h
        carry = h[0:1, :] if back else h[7:8, :]

def gate_values(q, pre, par, start):
    gx = sigmoid(pre[:, 0:128] + par[5:6, lanes(q)])
    ga = sigmoid(pre[:, 128:256] + par[6:7, lanes(q)])
    return gx, ga

def decay_of(q, ga, par, start):
    sp = softplus(par[7:8, lanes(q)])
    a = jnp.exp(-8.0 * ga * sp)
    spread = 1.0 - a * a
    mult = jnp.where(start == 1.0, 1.0, jnp.sqrt(jnp.maximum(spread, 0.01)))
    return sp, a, spread, mult

def prep(seq_len, seq_owner, gain_1, gain_2, w_xy, conv_w, conv_b, gate_w, gate_b, a_param, w_out):
    small = (seq_len.reshape(1, 128), seq_owner.reshape(1, 128), gain_1, gain_2,
             jnp.transpose(conv_w, (1, 0, 2)), conv_b, jnp.transpose(gate_b, (1, 0, 2)), a_param)
    w_t = jnp.transpose(w_xy, (0, 2, 3, 1)).reshape(2, 640, 2560)
    gw_t = jnp.swapaxes(gate_w, 2, 3).reshape(2, 640, 256)
    return small, w_t, gw_t, w_out.reshape(640, 2560)

def dot_tn(a, b):
    return lax.dot_general(a, b, (((0,), (0,)), ((), ())), preferred_element_type=jnp.float32)

class Swap:
    def __init__(self, comm, src, dst):
        f = lax.axis_index("fsdp")
        self.cps = []
        for d in (3, 2, 1):
            _, t = fpeer(d)
            self.cps.append(comm.remote(src.at[t], dst.at[f], ("f", d)))
        self.own = comm.local(src.at[f], dst.at[f])
    def finish(self):
        self.own.wait()
        for c in self.cps:
            c.wait_recv()

def spread(cm, src, dst, axis):
    return [cm.remote(src(d), dst.at[d - 1], (axis, d)) for d in (1, 3, 2)]

def arrived(cps):
    for c in cps:
        c.wait_recv()

CHUNK_FEATURES = [0] * 6 + [1] * 3 + [2, 3, 4]
FEATURE_AXIS = ["x", "z", "x", "z", "x"]
FEATURE_SLOT = [0, 1, 0, 1, 2]

class Sums:
    def __init__(self, cm, uland, fland, rrh, yr, usrc, fsrc, out):
        self.cm, self.uland, self.fland, self.rrh, self.yr = cm, uland, fland, rrh, yr
        self.usrc, self.fsrc, self.out = usrc, fsrc, out
        self.x, self.z, self.y, f = coords()
        self.core = f % 2
        self.u, self.u2, self.f, self.f2, self.r, self.yc = {}, {}, {}, {}, {}, {}
        self.nw = self.nst = self.nr = self.ntt = 0
        self.win, self.stc, self.rwin, self.ttc = {}, {}, {}, {}
        self.loaded = {}
        self.tu = {}
    def work(self, ft, uw, st, rw, tt):
        self.ft, self.uw, self.st, self.rw, self.tt = ft, uw, st, rw, tt
    def axis(self, c):
        return FEATURE_AXIS[CHUNK_FEATURES[c]]
    def pos(self, axis):
        return self.x if axis == "x" else self.z
    def send_f(self, k):
        axis = FEATURE_AXIS[k]
        me = self.pos(axis)
        def one(d):
            def src():
                t, h = (me + d) % 4, pl.ds(2 * self.core, 2)
                return self.fsrc[k].at[t, h] if axis == "x" else self.fsrc[k].at[h, t]
            return self.cm.remote(src, lambda: self.fland[k].at[d - 1, pl.ds(2 * self.core, 2)], (axis, d))
        self.f[k] = {d: one(d) for d in (1, 3, 2)}
    def relay_f(self, k):
        def one(d):
            self.f[k][d].wait_recv()
            half = lambda: self.fland[k].at[d - 1, pl.ds(2 * self.core, 2)]
            return self.cm.remote(half, half, ("f", 1))
        self.f2[k] = [one(d) for d in (1, 3, 2)]
    def send_u(self, c, direct=False):
        def one(d):
            return self.cm.remote(lambda: self.usrc[c], lambda: self.uland[c].at[d - 1], (self.axis(c), d))
        self.u[c] = {d: one(d) for d in ((1, 3, 2) if direct else (1, 3))}
        if direct:
            self.u2[c] = list(self.u[c].values())
    def relay_u(self, c):
        low, high = pl.ds(0, 128), pl.ds(128, 128)
        self.u[c][1].wait_recv()
        a = self.cm.remote(lambda: self.uland[c].at[0, low], lambda: self.uland[c].at[1, low], (self.axis(c), 1))
        self.u[c][3].wait_recv()
        b = self.cm.remote(lambda: self.uland[c].at[2, high], lambda: self.uland[c].at[1, high], (self.axis(c), 3))
        self.u2[c] = [a, b]
    def load_f(self, k):
        s = FEATURE_SLOT[k]
        axis = FEATURE_AXIS[k]
        me = self.pos(axis)
        own = self.fsrc[k].at[me] if axis == "x" else self.fsrc[k].at[:, me]
        cps = [self.cm.local(own, self.ft.at[s, :, :, pl.ds(0, 256)])]
        arrived(self.f2.get(k, []))
        for d in (1, 2, 3):
            cps.append(self.cm.local(self.fland[k].at[d - 1], self.ft.at[s, :, :, pl.ds(d * 256, 256)]))
        self.loaded[k] = cps
    def prep(self, c):
        k = CHUNK_FEATURES[c]
        if k not in self.loaded:
            self.load_f(k)
        w = self.nw % 2
        self.nw += 1
        cps = [self.cm.local(self.usrc[c], self.uw.at[w, 0])]
        arrived(self.u2.get(c, []))
        cps.append(self.cm.local(self.uland[c], self.uw.at[w, pl.ds(1, 3)]))
        self.win[c] = (w, cps)
    def mm(self, c):
        k = CHUNK_FEATURES[c]
        for l in self.loaded[k]:
            l.wait()
        self.loaded[k] = []
        w, cps = self.win[c]
        for l in cps:
            l.wait()
        i = self.nst % 4
        self.nst += 1
        for old in self.stc.get(i, []):
            self.cm.sent(old)
        s = self.st
        for h in (0, 2):
            v = dot(self.ft[FEATURE_SLOT[k], h:h + 2].reshape(320, 1024), self.uw[w].reshape(1024, 640))
            s[i, h:h + 2] = v.astype(BF).reshape(2, 160, 640)
        axis = "z" if self.axis(c) == "x" else "x"
        me = self.pos(axis)
        cps = [self.cm.remote(s.at[i, (me + d) % 4], self.rrh.at[c, d - 1], (axis, d)) for d in (1, 3, 2)]
        self.stc[i] = cps
        t = self.ntt % 12
        self.ntt += 1
        self.r[c] = (t, cps)
        assert self.tu.get(t) is None, c
        self.tu[t] = c
        for old in self.ttc.get(t, []):
            self.cm.sent(old)
        self.tt[t] = s[i, me].reshape(2, 80, 640)
    def rprep(self, c):
        t, cps = self.r[c]
        for r in cps:
            r.wait_recv()
        w = self.nr % 2
        self.nr += 1
        self.rwin[c] = (w, self.cm.local(self.rrh.at[c], self.rw.at[w]))
    def rsum(self, c):
        t, _ = self.r[c]
        w, l = self.rwin[c]
        l.wait()
        total = (self.tt[t].reshape(160, 640).astype(F32) + self.rw[w, 0].astype(F32)) + (self.rw[w, 1].astype(F32) + self.rw[w, 2].astype(F32))
        self.tt[t] = total.astype(BF).reshape(2, 80, 640)
        cp = self.cm.remote(self.tt.at[t, 1 - self.y], self.yr.at[c], ("y", 1))
        self.ttc[t] = [cp]
        self.yc[c] = cp
    def fin(self, c):
        self.yc[c].wait_recv()
        t, _ = self.r[c]
        self.tu[t] = None
        self.out(c, self.tt[t, self.y].astype(F32) + self.yr[c].astype(F32))

def forward_kernel(lenr, ownr, g1r, g2r, cwt, cbt, gbt, apt, tok, cot, w_t, gw_h, wo_h,
                   n1_o, cv_o, xb_o, yb_o, gx_o, ga_o, hs_o, z_o, n2_o, dt_o, h1_o, msk_o, r_o, g_o, wg_o, tk_o, n1t_o, dtt_o, pf, pu, par_o,
                   tkb, ctb, gnb, wv, gw, wo, wg, n1, dt, cvb, xb, yb, gx, ga, aa, uu, hs, z, msk, pt, r1, s2, r2, h1, n2b, rs1, rs2, n1t, dtt, par, gn,
                   ssem, rsem, lsem):
    cm = Comm(ssem, rsem, lsem)
    f = lax.axis_index("fsdp")
    lw = [cm.local(w_t.at[0], wv.at[0]), cm.local(gw_h, gw), cm.local(w_t.at[1], wv.at[1]), cm.local(wo_h, wo)]
    lt = [cm.local(tok, tkb.at[f]), cm.local(cot, ctb.at[f])]
    gn[0, :] = g1r[...].astype(F32)
    gn[1, :] = g2r[...].astype(F32)
    lt.append(cm.local(gn, gnb.at[f]))
    b = pltpu.get_barrier_semaphore()
    for axis, d in REP[:6]:
        pl.semaphore_signal(b, inc=1, device_id=peer(axis, d), device_id_type=MESH)
    for d in (1, 2):
        pl.semaphore_signal(b, inc=1, device_id=fpeer(d), device_id_type=MESH)
    pl.semaphore_wait(b, 8)
    S = Sums(cm, [None] * 11 + [pu], [None, pf.at[0], pf.at[1], pf.at[2]], None, None, [None] * 11 + [z], [None, dtt, n1t, n1t], None)
    halves = [(pl.ds(0, 128),), (pl.ds(128, 128),)]
    gtk = Gather(cm, tkb, tok, halves)
    ggn = Gather(cm, gnb, gn)
    gct = Gather(cm, ctb, cot)
    ggn.start()
    gtk.start()
    gct.start()
    for h in range(10):
        ls = slice(h * 64, h * 64 + 64)
        par[0:4, ls] = cwt[h].astype(F32)
        par[4:5, ls] = cbt[h:h + 1].astype(F32)
        par[5:7, ls] = gbt[h].astype(F32)
        par[7:8, ls] = apt[h:h + 1]
    row_masks(lenr, ownr, msk)
    lw[1].wait()
    wide_gates(gw, wg)
    outs = [cm.local(msk, msk_o), cm.local(wg, wg_o), cm.local(par, par_o)]
    ggn.relay()
    gtk.relay()
    for c in lt:
        c.wait()
    ggn.finish()
    gtk.finish()
    @pl.loop(0, 16)
    def _(i):
        rows = pl.ds(pl.multiple_of(i * 16, 16), 16)
        xs = [tkb[p, rows, :].astype(F32) for p in range(4)]
        ss = sum(jnp.sum(x * x, axis=-1, keepdims=True) for x in xs)
        r = lax.rsqrt(ss * (1.0 / 2560) + EPS)
        rs1[rows, :] = jnp.broadcast_to(r, (16, 128))
        for p in range(4):
            n1[rows, p * 640:p * 640 + 640] = (xs[p] * r * gnb[p, 0:1, :]).astype(BF)
    outs += [cm.local(n1, n1_o), cm.local(gnb, g_o), cm.local(tkb, tk_o)]
    lw[0].wait()
    xb[...] = dot_nt(n1[...], wv[0])
    outs.append(cm.local(xb, xb_o))
    for q in range(5):
        x = xb[:, lanes(q)]
        acc = par[4:5, lanes(q)] + par[0:1, lanes(q)] * x
        for k in (1, 2, 3):
            acc = acc + par[k:k + 1, lanes(q)] * pltpu.roll(x, k, axis=0) * msk[k]
        cvb[f, :, lanes(q)] = acc.astype(BF)
    gcv = Gather(cm, cvb, None, halves)
    gcv.start()
    lw[2].wait()
    yb[...] = dot_nt(n1[...], wv[1])
    outs.append(cm.local(yb, yb_o))
    gct.relay()
    for c in range(4):
        n1t[c] = n1[:, c * 640:c * 640 + 640].T.reshape(4, 160, 256)
    S.send_f(2)
    S.send_f(3)
    outs.append(cm.local(n1t, n1t_o))
    gcv.relay()
    gct.finish()
    @pl.loop(0, 16)
    def _(i):
        rows = pl.ds(pl.multiple_of(i * 16, 16), 16)
        live = jnp.broadcast_to(msk[4, rows, 0:1], (16, 640))
        for p in range(4):
            dt[rows, p * 640:p * 640 + 640] = (ctb[p, rows, :].astype(F32) * live).astype(BF)
    outs.append(cm.local(dt, dt_o))
    for c in range(4):
        dtt[c] = dt[:, c * 640:c * 640 + 640].T.reshape(4, 160, 256)
    S.send_f(1)
    outs.append(cm.local(dtt, dtt_o))
    gcv.finish()
    outs.append(cm.local(cvb, cv_o))
    for q in range(5):
        lhs = jnp.concatenate([cvb[p, :, lanes(q)] for p in range(4)], axis=1)
        pre = dot_nt(lhs, wg[q])
        gxq, gaq = gate_values(q, pre, par, msk[0])
        sp, a, spread, mult = decay_of(q, gaq, par, msk[0])
        gx[:, lanes(q)] = gxq
        ga[:, lanes(q)] = gaq
        aa[:, lanes(q)] = jnp.where(msk[0] == 1.0, 0.0, a)
        uu[:, lanes(q)] = mult * gxq * cvb[f, :, lanes(q)].astype(F32)
    outs += [cm.local(gx, gx_o), cm.local(ga, ga_o)]
    scan_rows(aa, uu, hs, False)
    for q in range(5):
        yg, _ = gelu_parts(yb[:, lanes(q)])
        z[:, lanes(q)] = (hs[:, lanes(q)] * yg).astype(BF)
    S.send_u(11, direct=True)
    outs += [cm.local(hs, hs_o), cm.local(z, z_o)]
    lw[3].wait()
    red = Reduce(cm, pt, r1, s2, r2)
    for c in range(4):
        pt[c] = dot(z[...], wo[:, c * 640:c * 640 + 640]).astype(BF).reshape(4, 64, 640)
        red.send(c)
        if c: red.mid(c - 1)
    red.mid(3)
    for k in (2, 3, 1):
        S.relay_f(k)
    own = pl.ds(pl.multiple_of(f * 64, 64), 64)
    ss = jnp.zeros((64, 1), F32)
    for c in range(4):
        h = tkb[c, own, :].astype(F32) + red.fin(c)
        h1[:, c * 640:c * 640 + 640] = h
        ss = ss + jnp.sum(h * h, axis=-1, keepdims=True)
    r = lax.rsqrt(ss * (1.0 / 2560) + EPS)
    rs2[...] = jnp.broadcast_to(r, (64, 128))
    for c in range(4):
        cs = slice(c * 640, c * 640 + 640)
        n2b[f, :, cs] = (h1[:, cs] * r * gnb[c, 1:2, :]).astype(BF)
    gn2 = Gather(cm, n2b, None, [(pl.ds(0, 32),), (pl.ds(32, 32),)])
    gn2.start()
    outs += [cm.local(h1, h1_o), cm.local(rs1, r_o.at[pl.ds(0, 256)]), cm.local(rs2, r_o.at[pl.ds(256, 64)])]
    gn2.relay()
    gn2.finish()
    outs.append(cm.local(n2b, n2_o))
    for k in (2, 3, 1):
        arrived(S.f2[k])
    arrived(S.u[11].values())
    for c in outs:
        c.wait()
    cm.drain()

def forward(lenr, ownr, g1r, g2r, cwt, cbt, gbt, apt, tok, cot, w_t, gw_t, wo):
    s = jax.ShapeDtypeStruct
    R = 256
    fw = s((R, 640), F32)
    out_shape = [s((R, 2560), BF), s((4, R, 640), BF), fw, fw, fw, fw, fw, s((R, 640), BF), s((4, 64, 2560), BF), s((R, 2560), BF),
                 s((64, 2560), F32), s((5, R, 128), F32), s((320, 128), F32), s((4, 8, 640), F32), s((5, 256, 512), BF), s((4, R, 640), BF), s((4, 4, 160, 256), BF), s((4, 4, 160, 256), BF), s((3, 3, 4, 160, 256), BF), s((3, R, 640), BF), s((8, 640), F32)]
    V = pltpu.VMEM
    f640 = V((R, 640), F32)
    scratch = [V((4, R, 640), BF), V((4, R, 640), BF), V((4, 8, 640), F32), V((2, 640, 2560), BF), V((2, 640, 256), BF), V((640, 2560), BF),
               V((5, 256, 512), BF), V((R, 2560), BF), V((R, 2560), BF), V((4, R, 640), BF), f640, f640, f640, f640, f640, f640, f640,
               V((R, 640), BF), V((5, R, 128), F32), V((4, 4, 64, 640), BF), V((4, 2, 64, 640), BF), V((4, 64, 640), BF), V((4, 64, 640), BF),
               V((64, 2560), F32), V((4, 64, 2560), BF), V((R, 128), F32), V((64, 128), F32), V((4, 4, 160, 256), BF), V((4, 4, 160, 256), BF), V((8, 640), F32), V((8, 640), F32),
               pltpu.SemaphoreType.DMA((80,)), pltpu.SemaphoreType.DMA((80,)), pltpu.SemaphoreType.DMA((40,))]
    return pl.pallas_call(
        forward_kernel, out_shape=out_shape,
        in_specs=[VMEM] * 8 + [ANY] * 5,
        out_specs=[ANY] * len(out_shape),
        scratch_shapes=scratch,
        compiler_params=pltpu.CompilerParams(collective_id=3, has_side_effects=True, vmem_limit_bytes=VM),
        name="forward",
    )(lenr, ownr, g1r, g2r, cwt, cbt, gbt, apt, tok, cot, w_t, gw_t, wo)

def finish_kernel(bo, dtok, d_in, d_dn, d_xy, d_wo, gate, sm, bo_o, dtok_o, in_o, dn_o, xy_o, wo_o, gate_o, g1_o, g2_o, cw_o, cb_o, gb_o, a_o):
    for source, target in ((bo, bo_o), (dtok, dtok_o), (d_in, in_o), (d_dn, dn_o), (d_xy, xy_o), (d_wo, wo_o)):
        target[...] = source[...]
    g1_o[...] = sm[0]
    g2_o[...] = sm[1]
    for h in range(10):
        ls = slice(h * 64, h * 64 + 64)
        cw_o[h] = sm[2:6, ls]
        cb_o[h:h + 1] = sm[6:7, ls]
        gb_o[h] = sm[7:9, ls]
        a_o[h:h + 1] = sm[9:10, ls]
        for k in range(2):
            gate_o[k, h] = gate[k, h // 2, :, h % 2 * 64:h % 2 * 64 + 64]

def finish(bo, dtok, d_in, d_dn, d_xy, d_wo, gate, sm):
    s = jax.ShapeDtypeStruct
    out_shape = [s((4, 64, 640), BF), s((256, 640), F32), s((2, 80, 1920), F32), s((80, 1920), F32), s((2, 640, 80), F32), s((640, 80), F32),
                 s((2, 10, 8, 64), F32), s((640,), F32), s((640,), F32), s((10, 4, 64), F32), s((10, 64), F32), s((10, 2, 64), F32), s((10, 64), F32)]
    return pl.pallas_call(
        finish_kernel, out_shape=out_shape,
        in_specs=[VMEM] * 8,
        out_specs=[VMEM] * 13,
        compiler_params=pltpu.CompilerParams(vmem_limit_bytes=VM),
        name="finish",
    )(bo, dtok, d_in, d_dn, d_xy, d_wo, gate, sm)

PLAN = {
    "F0h": "d6",
    "F0g": "u0 u3",
    "F0": "",
    "F1h": "",
    "F1g": "",
    "F1": "u1 u7 r0",
    "F2h": "u8",
    "F2g": "r3",
    "F2": "",
    "C0": "r1 p6 q0 r7 p0 u4 r8",
    "C1": "m6 m0 p3 m3 p1 u2 r4 m1",
    "C2": "",
    "C2b": "p7 u5",
    "C3": "v6 v0 s6 r2",
    "C3b": "r5 s0 m7 v3 r10 v1 p4 f0 s3 s1 m4 q4 p2",
    "C5": "p5 m2 p8 m5 m8 v7",
    "C6": "p11 r9 m11",
    "E": "s7 v4 s4 f3 p10 v2 p9 v8 m10 s2 m9 v5 s8 f1 v11 s5 f2 f7 g0 s11 f6 v10 f4 s10 v9 s9 f8 f5 f11 g1 f10 f9 g2",
}

def tail_kernel(plan, par, n2_h, dt_h, w_in, w_dn, n1t_h, dtt_h, pf, pu, z_h, cv_h, xb_h, yb_h, gx_h, ga_h, hs_h, msk_h, r_h, g_h, wg_h, tk_h, h1_h, w_t, wo_h,
                bo_o, dtok_o, in_o, dn_o, xy_o, wout_o, gate_o, sm_o, ubh, rrh, fth,
                un, gu, yr, fts, dr, pd, pm, bob, dto, gs, gr, sm, sgr, sgt, sgr2, sgy, sma, smr, smy,
                m1, m2, m3, d1, d2, d3, e1, e2, e3, f1, f2, f3, gnb, rb, h1, dtb, tk,
                ssem, rsem, lsem):
    cm = Comm(ssem, rsem, lsem)
    f = lax.axis_index("fsdp")
    x, z, y, _ = coords()
    own = pl.ds(pl.multiple_of(f * 64, 64), 64)
    rd = Reduce(cm, pd, d1, d2, d3)
    rm = Reduce(cm, pm, m1, m2, m3)
    def put(c, v):
        if c < 6:
            in_o[c // 3, :, c % 3 * 640:c % 3 * 640 + 640] = v
        elif c < 9:
            dn_o[:, (c - 6) * 640:(c - 6) * 640 + 640] = v
        elif c < 11:
            xy_o[c - 9] = v.T
        else:
            wout_o[...] = v.T
    usrc = [gu.at[i, :, pl.ds(j, 640)] for j in (0, 640) for i in range(3)] + [un.at[i] for i in range(3)] + [None, None, z_h]
    uland = [ubh.at[c] for c in range(11)] + [pu]
    fland = [fth.at[0], pf.at[0], pf.at[1], pf.at[2], fth.at[1]]
    S = Sums(cm, uland, fland, rrh, yr, usrc, [fts, dtt_h, n1t_h, n1t_h, fts], put)
    lh = [cm.local(h1_h, h1), cm.local(g_h, gnb), cm.local(r_h, rb), cm.local(dt_h.at[own], dtb), cm.local(tk_h.at[:, own], tk)]

    w = pltpu.VMEM((256, 640), F32)

    small = {}
    def at(point):
        for t in plan[point].split():
            run(t[0], int(t[1:]))
    def run(t, c):
        if t == "u": S.send_u(c)
        elif t == "d": S.send_u(c, direct=True)
        elif t == "r": S.relay_u(c)
        elif t == "q": S.relay_f(c)
        elif t == "p": S.prep(c)
        elif t == "m": S.mm(c)
        elif t == "v": S.rprep(c)
        elif t == "s": S.rsum(c)
        elif t == "f": S.fin(c)
        else: small_step(c)
    def small_step(j):
        if j == 0:
            arrived(small["g2"])
            sgy[0] = sgt[x].astype(F32) + sgr2[0].astype(F32) + sgr2[1].astype(F32) + sgr2[2].astype(F32)
            small[0] = cm.remote(sgy.at[0], sgy.at[1], ("y", 1))
            arrived(small["v1"])
            sma[1] = (sma[0] + smr[0, 0]) + (smr[0, 1] + smr[0, 2])
            small[1] = spread(cm, lambda d: sma.at[1], smr.at[1], "z")
        if j == 1:
            arrived(small[1])
            sma[2] = (sma[1] + smr[1, 0]) + (smr[1, 1] + smr[1, 2])
            small[2] = cm.remote(sma.at[2], smy, ("y", 1))
            small[0].wait_recv()
            half = pl.ds(pl.multiple_of(y * 8, 8), 8)
            gate_o[...] = sgy[0, :, :, half, :] + sgy[1, :, :, half, :]
        if j == 2:
            small[2].wait_recv()
            sm_o[...] = sma[2] + smy[...]

    def ffn_phase(wa, wd, am, ad, fg, fd, n2, dt):
        def load(i):
            s = i % 2
            cols = pl.ds(i * 640, 640)
            return [cm.local(w_in.at[0, :, cols], wa.at[s, :, pl.ds(0, 640)]), cm.local(w_in.at[1, :, cols], wa.at[s, :, pl.ds(640, 640)]), cm.local(w_dn.at[cols], wd.at[s])]
        ln = cm.local(n2_h, n2)
        lw = {0: load(0)}
        ld = cm.local(dt_h, dt)
        b = pltpu.get_barrier_semaphore()
        for axis, d in REP:
            pl.semaphore_signal(b, inc=1, device_id=peer(axis, d), device_id_type=MESH)
        for d in (1, 2, 3):
            pl.semaphore_signal(b, inc=1, device_id=fpeer(d), device_id_type=MESH)
        ln.wait()
        for c in range(4):
            fts[c] = n2[:, c * 640:c * 640 + 640].T.reshape(4, 160, 256)
        pl.semaphore_wait(b, len(REP) + 3)
        S.send_f(0)
        for i in range(3):
            s = i % 2
            lw[i][0].wait()
            lw[i][1].wait()
            fg[...] = dot(n2[...], wa[s])
            for q in range(5):
                gl, _ = gelu_parts(fg[:, lanes(q)])
                un[i, :, lanes(q)] = (gl * fg[:, lanes(q + 5)]).astype(BF)
            at(f"F{i}h")
            lw[i][2].wait()
            if i == 0:
                lw[1] = load(1)
                ld.wait()
            fd[...] = dot_nt(dt[...], wd[s])
            for q in range(5):
                gl, dgl = gelu_parts(fg[:, lanes(q)])
                dh = fd[:, lanes(q)]
                gu[i, :, lanes(q)] = (dh * fg[:, lanes(q + 5)] * dgl).astype(BF)
                gu[i, :, lanes(q + 5)] = (dh * gl).astype(BF)
            at(f"F{i}g")
            for c in range(4):
                cs = slice(c * 640, c * 640 + 640)
                v = dot_nt(gu[i], wa[s, cs, :])
                if i == 0:
                    ad[:, cs] = v
                elif i == 1:
                    ad[:, cs] = ad[:, cs] + v
                else:
                    pd[c] = (ad[:, cs] + v).astype(BF).reshape(4, 64, 640)
                    rd.send(c)
                    if c: rd.mid(c - 1)
            if i == 2:
                rd.mid(3)
            for c in range(4):
                cs = slice(c * 640, c * 640 + 640)
                v = dot(un[i], wd[s, :, cs])
                if i == 0:
                    am[:, cs] = v
                elif i == 1:
                    am[:, cs] = am[:, cs] + v
                else:
                    pm[c] = (am[:, cs] + v).astype(BF).reshape(4, 64, 640)
            if i == 0:
                lw[2] = load(2)
            at(f"F{i}")

    pl.run_scoped(ffn_phase, pltpu.VMEM((2, 2560, 1280), BF), pltpu.VMEM((2, 640, 2560), BF), pltpu.VMEM((256, 2560), F32), pltpu.VMEM((256, 2560), F32), pltpu.VMEM((256, 1280), F32), w, pltpu.VMEM((256, 2560), BF), pltpu.VMEM((256, 2560), BF))

    def chain_phase(cv, xb, yb, gx, ga, hs, msk, wg, wbuf, aa, uu, gg, dc1, dp, dna, ft, uw, st, rw, tt, bo, dob, sg, dxy, dxx, pb, dnp, dh1):
        S.work(ft, uw, st, rw, tt)
        S.usrc[9], S.usrc[10] = dxy.at[0], dxy.at[1]
        lb = [cm.local(wo_h, wbuf.at[0]), cm.local(yb_h, yb), cm.local(hs_h, hs), cm.local(ga_h, ga), cm.local(msk_h, msk), cm.local(gx_h, gx), cm.local(cv_h, cv),
              cm.local(wg_h, wg), cm.local(xb_h, xb), cm.local(w_t.at[1], wbuf.at[1])]
        for c in range(4):
            rm.send(c)
        at("C0")
        for c in lh:
            c.wait()
        gs[...] = jnp.zeros_like(gs)
        r2 = rb[256:320, 0:1]
        acc = jnp.zeros((64, 1), F32)
        for c in range(4):
            cs = slice(c * 640, c * 640 + 640)
            dn = rd.fin(c)
            h = h1[:, cs]
            gs[c, 1:2, :] = jnp.sum(dn * h * r2, axis=0, keepdims=True)
            v = dn * gnb[c, 1:2, :]
            dh1[:, cs] = v
            acc = acc + jnp.sum(v * h, axis=-1, keepdims=True)
        acc = acc * (1.0 / 2560) * (r2 * r2 * r2)
        for c in range(4):
            cs = slice(c * 640, c * 640 + 640)
            d = dtb[:, cs].astype(F32) + r2 * dh1[:, cs] - h1[:, cs] * acc
            dh1[:, cs] = d
            dr[f, :, cs] = d.astype(BF)
        gdr = Gather(cm, dr, None, [(pl.ds(0, 32),), (pl.ds(32, 32),)])
        gdr.start()
        for c in range(4):
            rm.mid(c)
        at("C1")
        for c in lb:
            c.wait()
        for q in range(5):
            sp, a, spread_, mult = decay_of(q, ga[:, lanes(q)], par, msk[0])
            up = pltpu.roll(jnp.where(msk[0] == 1.0, 0.0, a), 255, axis=0)
            rows = lax.broadcasted_iota(jnp.int32, (256, 128), 0)
            aa[:, lanes(q)] = jnp.where(rows == 255, 0.0, up)
        gdr.relay()
        at("C2")
        gdr.finish()
        uu[...] = dot_nt(dr[...].reshape(256, 2560), wbuf[0])
        lw0 = cm.local(w_t.at[0], wbuf.at[0])
        for q in range(5):
            yg, dgl = gelu_parts(yb[:, lanes(q)])
            dz = uu[:, lanes(q)]
            dxy[1, :, lanes(q)] = (dz * hs[:, lanes(q)] * dgl).astype(BF)
            uu[:, lanes(q)] = dz * yg
        S.send_u(10)
        at("C2b")
        scan_rows(aa, uu, gg, True)
        re = Reduce(cm, pb, e1, e2, e3)
        for q in range(5):
            ls = lanes(q)
            start = msk[0]
            gxq, gaq, g = gx[:, ls], ga[:, ls], gg[:, ls]
            sp, a, spread_, mult = decay_of(q, gaq, par, start)
            cvq = cv[f, :, ls].astype(F32)
            prev = jnp.where(start == 1.0, 0.0, pltpu.roll(hs[:, ls], 1, axis=0))
            slope = jnp.where((start == 1.0) | (spread_ <= 0.01), 0.0, -a / mult)
            da = g * prev + g * gxq * cvq * slope
            dc1[:, ls] = g * mult * gxq
            dlog = da * a
            da_p = jnp.sum(dlog * (-8.0 * gaq), axis=0, keepdims=True) * sigmoid(par[7:8, ls])
            px = (g * mult * cvq * gxq * (1.0 - gxq)).astype(BF)
            pa = (-8.0 * dlog * sp * gaq * (1.0 - gaq)).astype(BF)
            dp[q, :, 0:128] = px
            dp[q, :, 128:256] = pa
            sm[7:8, ls] = jnp.sum(px.astype(F32), axis=0, keepdims=True)
            sm[8:9, ls] = jnp.sum(pa.astype(F32), axis=0, keepdims=True)
            sm[9:10, ls] = da_p
            db = dot(dp[q], wg[q]).astype(BF)
            for p in range(4):
                pb[q, p] = db[:, lanes(p)]
            re.send(q)
            if q: re.mid(q - 1)
        re.mid(4)
        for old in S.f[0].values():
            cm.sent(old)
        drt = dr[...].reshape(256, 2560)
        for c in range(4):
            fts[c] = drt[:, c * 640:c * 640 + 640].T.reshape(4, 160, 256)
        S.send_f(4)
        at("C3")
        for c in range(4):
            cs = slice(c * 640, c * 640 + 640)
            dna[c] = dot(dxy[1], wbuf[1, :, cs])
        low = lax.broadcasted_iota(jnp.int32, (64, 128), 1) < 64
        for q in range(5):
            lhs = jnp.concatenate([cv[p, :, lanes(q)] for p in range(4)], axis=1)
            gwt = dot_tn(lhs, dp[q])
            for p in range(4):
                for k in range(2):
                    blk = gwt[p * 128:p * 128 + 128, k * 128:k * 128 + 128]
                    sg[p, k, q] = jnp.where(low, blk[0:64], blk[64:128]).astype(BF)
        g1 = spread(cm, lambda d: sg.at[:, :, :, pl.ds(pl.multiple_of((z + d) % 4 * 16, 16), 16)], sgr, "z")
        at("C3b")
        live = msk[4, own, 0:1]
        for c in range(4):
            bo[c] = (live * (h1[:, c * 640:c * 640 + 640] + rm.fin(c))).astype(BF)
        sbo = Swap(cm, bo, bob)
        for q in range(5):
            ls = lanes(q)
            d = dc1[:, ls] + re.fin(q)
            xq = xb[:, ls]
            sm[6:7, ls] = jnp.sum(d, axis=0, keepdims=True)
            sm[2:3, ls] = jnp.sum(d * xq, axis=0, keepdims=True)
            dx = par[0:1, ls] * d
            for k in (1, 2, 3):
                m = d * msk[k]
                sm[2 + k:3 + k, ls] = jnp.sum(m * pltpu.roll(xq, k, axis=0), axis=0, keepdims=True)
                dx = dx + par[k:k + 1, ls] * pltpu.roll(m, 256 - k, axis=0)
            dxy[0, :, ls] = dx.astype(BF)
        S.send_u(9)
        lw0.wait()
        rf = Reduce(cm, dnp, f1, f2, f3)
        for c in range(4):
            cs = slice(c * 640, c * 640 + 640)
            dnp[c] = (dna[c] + dot(dxy[0], wbuf[0, :, cs])).astype(BF).reshape(4, 64, 640)
            rf.send(c)
            if c: rf.mid(c - 1)
        rf.mid(3)
        at("C5")
        r1 = rb[own, 0:1]
        acc = jnp.zeros((64, 1), F32)
        for c in range(4):
            dn = rf.fin(c)
            xr = tk[c].astype(F32)
            gs[c, 0:1, :] = jnp.sum(dn * xr * r1, axis=0, keepdims=True)
            v = dn * gnb[c, 0:1, :]
            dna[c, 0:64, :] = v
            acc = acc + jnp.sum(v * xr, axis=-1, keepdims=True)
        acc = acc * (1.0 / 2560) * (r1 * r1 * r1)
        for c in range(4):
            dob[c] = (dh1[:, c * 640:c * 640 + 640] + r1 * dna[c, 0:64, :] - tk[c].astype(F32) * acc).astype(BF)
        sdt = Swap(cm, dob, dto)
        gcp = []
        for d in (3, 2, 1):
            _, t = fpeer(d)
            gcp.append(cm.remote(gs.at[t], gr.at[d - 1], ("f", d)))
        sbo.finish()
        outs = [cm.local(bob, bo_o)]
        at("C6")
        arrived(g1)
        t = sg[:, :, :, pl.ds(pl.multiple_of(z * 16, 16), 16), :].astype(F32)
        sgt[...] = ((t + sgr[0].astype(F32)) + (sgr[1].astype(F32) + sgr[2].astype(F32))).astype(BF)
        small["g2"] = spread(cm, lambda d: sgt.at[(x + d) % 4], sgr2, "x")
        arrived(gcp)
        sm[0:2, :] = (gs[f, 0:2, :] + gr[0, 0:2, :]) + (gr[1, 0:2, :] + gr[2, 0:2, :])
        sm[10:16, :] = jnp.zeros((6, 640), F32)
        sma[0] = sm[...]
        small["v1"] = spread(cm, lambda d: sma.at[0], smr.at[0], "x")
        sdt.finish()
        dxx[...] = dto[...].astype(F32).reshape(256, 640)
        outs.append(cm.local(dxx, dtok_o))
        at("E")
        for c in outs:
            c.wait()
        cm.drain()

    pl.run_scoped(chain_phase, pltpu.VMEM((4, 256, 640), BF), w, w, w, w, w, pltpu.VMEM((5, 256, 128), F32), pltpu.VMEM((5, 256, 512), BF), pltpu.VMEM((2, 640, 2560), BF),
                  w, w, w, w, pltpu.VMEM((5, 256, 256), BF), pltpu.VMEM((4, 256, 640), F32),
                  pltpu.VMEM((3, 4, 160, 1024), BF), pltpu.VMEM((2, 4, 256, 640), BF), pltpu.VMEM((4, 4, 160, 640), BF), pltpu.VMEM((2, 3, 160, 640), BF), pltpu.VMEM((12, 2, 80, 640), BF),
                  pltpu.VMEM((4, 64, 640), BF), pltpu.VMEM((4, 64, 640), BF), pltpu.VMEM((4, 2, 5, 64, 128), BF), pltpu.VMEM((2, 256, 640), BF), w,
                  pltpu.VMEM((5, 4, 256, 128), BF), pltpu.VMEM((4, 4, 64, 640), BF), pltpu.VMEM((64, 2560), F32))

def tail(par, n2, dt, w_in, w_dn, n1t, dtt, pf, pu, z, cv, xb, yb, gx, ga, hs, msk, r, g, wg, tk, h1, w_t, wo, plan=PLAN):
    s = jax.ShapeDtypeStruct
    R = 256
    V = pltpu.VMEM
    out_shape = [s((4, 64, 640), BF), s((R, 640), F32), s((2, 80, 1920), F32), s((80, 1920), F32), s((2, 640, 80), F32), s((640, 80), F32),
                 s((2, 5, 8, 128), F32), s((16, 640), F32), s((11, 3, R, 640), BF), s((12, 3, 160, 640), BF), s((2, 3, 4, 160, 256), BF)]
    blk = V((4, 4, 64, 640), BF)
    row = V((4, 64, 640), BF)
    red = [V((4, 2, 64, 640), BF), row, row]
    red5 = [V((5, 2, R, 128), BF), V((5, R, 128), BF), V((5, R, 128), BF)]
    scratch = [V((3, R, 640), BF), V((3, R, 1280), BF), V((12, 80, 640), BF), V((4, 4, 160, 256), BF), V((4, 64, 2560), BF), blk, blk, row, row,
               V((4, 8, 640), F32), V((3, 8, 640), F32), V((16, 640), F32),
               V((3, 4, 2, 5, 16, 128), BF), V((4, 2, 5, 16, 128), BF), V((3, 2, 5, 16, 128), BF), V((2, 2, 5, 16, 128), F32),
               V((3, 16, 640), F32), V((2, 3, 16, 640), F32), V((16, 640), F32)] + red + red + red5 + red + [
               V((4, 8, 640), F32), V((320, 128), F32), V((64, 2560), F32), V((64, 2560), BF), V((4, 64, 640), BF),
               pltpu.SemaphoreType.DMA((224,)), pltpu.SemaphoreType.DMA((224,)), pltpu.SemaphoreType.DMA((128,))]
    return pl.pallas_call(
        functools.partial(tail_kernel, plan), out_shape=out_shape,
        in_specs=[VMEM] + [ANY] * 23,
        out_specs=[ANY] * 2 + [VMEM] * 6 + [ANY] * 3,
        scratch_shapes=scratch,
        compiler_params=pltpu.CompilerParams(collective_id=5, has_side_effects=True, vmem_limit_bytes=VM),
        name="tail",
    )(par, n2, dt, w_in, w_dn, n1t, dtt, pf, pu, z, cv, xb, yb, gx, ga, hs, msk, r, g, wg, tk, h1, w_t, wo)

def body_of(plan, tokens, seq_len, seq_owner, gain_1, gain_2, w_xy, conv_w, conv_b, gate_w, gate_b, a_param, w_out, w_in, w_down, cotangent):
    small, w_t, gw_t, wo = prep(seq_len, seq_owner, gain_1, gain_2, w_xy, conv_w, conv_b, gate_w, gate_b, a_param, w_out)
    (n1, cv, xb, yb, gx, ga, hs, z, n2, dt, h1, msk, r, g, wg, tk, n1t, dtt, pf, pu, par) = forward(*small, tokens, cotangent, w_t, gw_t, wo)
    sums = tail(par, n2.reshape(256, 2560), dt, w_in, w_down, n1t, dtt, pf, pu, z, cv, xb, yb, gx, ga, hs, msk, r, g, wg, tk, h1, w_t, wo, plan)[:8]
    bo, dtok, d_in, d_dn, d_xy, d_wo, gate, g1, g2, cw, cb, gb, da = finish(*sums)
    return (bo.reshape(256, 640), dtok, g1, g2, jnp.transpose(d_xy.reshape(2, 10, 64, 80), (0, 3, 1, 2)), jnp.transpose(cw, (1, 0, 2)), cb,
            gate, jnp.transpose(gb, (1, 0, 2)), da, d_wo.reshape(10, 64, 80), d_in, d_dn.T)

def body(*args):
    return body_of(PLAN, *args)


def solution(mesh):
    return jax.shard_map(
        body,
        mesh=mesh,
        in_specs=(
            P("rep", "fsdp"), P(), P(), P("fsdp"), P("fsdp"), P(None, None, None, "fsdp"), P(None, None, "fsdp"), P(None, "fsdp"),
            P(None, None, None, "fsdp"), P(None, None, "fsdp"), P(None, "fsdp"), P(None, "fsdp", None), P(None, None, "fsdp"), P("fsdp", None), P("rep", "fsdp"),
        ),
        out_specs=(
            P("rep", "fsdp"), P("rep", "fsdp"), P("fsdp"), P("fsdp"), P(None, "rep", None, "fsdp"), P(None, None, "fsdp"), P(None, "fsdp"),
            P(None, None, "rep", "fsdp"), P(None, None, "fsdp"), P(None, "fsdp"), P(None, "fsdp", "rep"), P(None, "rep", "fsdp"), P("fsdp", "rep"),
        ),
        check_vma=False,
    )
```

```python
import functools

import jax
import jax.numpy as jnp
from jax import lax
from jax.experimental import pallas as pl
from jax.experimental.pallas import tpu as pltpu
from jax.sharding import PartitionSpec as P

MESH = pl.DeviceIdType.MESH
VM = 63 * 2**20
GC = 0.7978845608028654

def gelu_parts(v):
    v2 = v * v
    t = jnp.tanh(GC * v * (1.0 + 0.044715 * v2))
    half = 0.5 * (1.0 + t)
    g = v * half
    dg = half + 0.5 * v * (1.0 - t * t) * (GC * (1.0 + 3 * 0.044715 * v2))
    return g, dg

def dot(a, b):
    return jnp.dot(a, b, preferred_element_type=jnp.float32)

def dot_nt(a, b):
    return lax.dot_general(a, b, (((1,), (1,)), ((), ())), preferred_element_type=jnp.float32)

def ffn_kernel(n2, dt, w_in, w_dn, hid, dg, du, mlp, dn2, n2t, dtt, am, ad):
    i = pl.program_id(0)
    @pl.when(i == 1)
    def _():
        for c in range(4):
            n2t[c] = n2[:, c * 640:c * 640 + 640].T.reshape(4, 160, 256)
            dtt[c] = dt[:, c * 640:c * 640 + 640].T.reshape(4, 160, 256)
    @pl.when(i == 0)
    def _():
        am[...] = jnp.zeros_like(am)
        ad[...] = jnp.zeros_like(ad)
    gate = dot(n2[...], w_in[0])
    up = dot(n2[...], w_in[1])
    g, dgl = gelu_parts(gate)
    h = (g * up).astype(jnp.bfloat16)
    hid[0] = h
    dh = dot_nt(dt[...], w_dn[...])
    a = (dh * up * dgl).astype(jnp.bfloat16)
    b = (dh * g).astype(jnp.bfloat16)
    dg[0] = a
    du[0] = b
    am[...] += dot(h, w_dn[...])
    ad[...] += dot_nt(a, w_in[0])
    ad[...] += dot_nt(b, w_in[1])
    @pl.when(i == 2)
    def _():
        for c in range(4):
            mlp[c] = am[:, c * 640:c * 640 + 640].astype(jnp.bfloat16).reshape(4, 64, 640)
            dn2[c] = ad[:, c * 640:c * 640 + 640].astype(jnp.bfloat16).reshape(4, 64, 640)

def ffn(n2, dt, w_in, w_dn):
    R, D = n2.shape
    T = 640
    nt = w_dn.shape[0] // T
    full = pl.BlockSpec((R, D), lambda i: (0, 0))
    tile = pl.BlockSpec((1, R, T), lambda i: (i, 0, 0))
    ch = jax.ShapeDtypeStruct((nt, R, T), jnp.bfloat16)
    rd = jax.ShapeDtypeStruct((4, 4, 64, 640), jnp.bfloat16)
    td = jax.ShapeDtypeStruct((4, 4, 160, 256), jnp.bfloat16)
    part = pl.BlockSpec((4, 4, 64, 640), lambda i: (0, 0, 0, 0))
    turned = pl.BlockSpec((4, 4, 160, 256), lambda i: (0, 0, 0, 0))
    return pl.pallas_call(
        ffn_kernel, grid=(nt,),
        in_specs=[full, full, pl.BlockSpec((2, D, T), lambda i: (0, 0, i)), pl.BlockSpec((T, D), lambda i: (i, 0))],
        out_specs=[tile, tile, tile, part, part, turned, turned],
        out_shape=[ch, ch, ch, rd, rd, td, td],
        scratch_shapes=[pltpu.VMEM((R, D), jnp.float32)] * 2,
        compiler_params=pltpu.CompilerParams(vmem_limit_bytes=VM),
        name="ffn",
    )(n2, dt, w_in, w_dn)

def coords():
    r = lax.axis_index("rep")
    f = lax.axis_index("fsdp")
    return r // 8, (r // 2) % 4, r % 2, f

def peer(axis, d):
    x, z, y, f = coords()
    if axis == "x":
        x = (x + d) % 4
    elif axis == "z":
        z = (z + d) % 4
    elif axis == "y":
        y = 1 - y
    else:
        f = (f + d) % 4
    return ((x * 4 + z) * 2 + y, f)

class Grads:
    def __init__(self, plan, fplan):
        self.plan = plan
        self.fplan = fplan
    def scratch(self):
        n, m = len(self.plan), len(self.fplan)
        b = jnp.bfloat16
        return [
            pltpu.VMEM((n, 4, 256, 640), b),
            pltpu.VMEM((m, 4, 160, 1024), b),
            pltpu.VMEM((n, 4, 160, 640), b),
            pltpu.VMEM((n, 3, 160, 640), b),
            pltpu.VMEM((n, 2, 80, 640), b),
            pltpu.VMEM((n, 80, 640), b),
            pltpu.SemaphoreType.DMA((n, 3)), pltpu.SemaphoreType.DMA((n, 3)),
            pltpu.SemaphoreType.DMA((m, 3)), pltpu.SemaphoreType.DMA((m, 3)),
            pltpu.SemaphoreType.DMA((n, 3)), pltpu.SemaphoreType.DMA((n, 3)),
            pltpu.SemaphoreType.DMA((n,)), pltpu.SemaphoreType.DMA((n,)),
            pltpu.SemaphoreType.DMA((n,)), pltpu.SemaphoreType.DMA((m,)),
        ]
    def bind(self, refs, usrc, fsrc, out):
        (self.ub, self.ft, self.st, self.rr, self.tt, self.yr, self.us, self.ur, self.fs, self.fr,
         self.rq, self.rv, self.ys, self.yv, self.lu, self.lf) = refs
        self.usrc, self.fsrc, self.out = usrc, fsrc, out
    def rc(self, src, dst, s, r, axis, d):
        return pltpu.make_async_remote_copy(src_ref=src, dst_ref=dst, send_sem=s, recv_sem=r, device_id=peer(axis, d), device_id_type=MESH)
    def fcopies(self, k):
        i, axis = self.fplan[k]
        x, z, y, f = coords()
        src = self.fsrc[i]
        me = x if axis == "x" else z
        pick = (lambda t: src.at[t]) if axis == "x" else (lambda t: src.at[:, t])
        loc = pltpu.make_async_copy(pick(me), self.ft.at[k, :, :, pl.ds(0, 256)], self.lf.at[k])
        rem = [self.rc(pick((me + d) % 4), self.ft.at[k, :, :, pl.ds(d * 256, 256)], self.fs.at[k, d - 1], self.fr.at[k, d - 1], axis, d) for d in (1, 3, 2)]
        return loc, rem
    def ucopies(self, c):
        k, axis = self.plan[c]
        src = self.usrc(c)
        loc = pltpu.make_async_copy(src, self.ub.at[c, 0], self.lu.at[c])
        rem = [self.rc(src, self.ub.at[c, d], self.us.at[c, d - 1], self.ur.at[c, d - 1], axis, d) for d in (1, 3, 2)]
        return loc, rem
    def rscopies(self, c):
        k, axis = self.plan[c]
        ra = "z" if axis == "x" else "x"
        x, z, y, f = coords()
        me = z if axis == "x" else x
        return me, [self.rc(self.st.at[c, (me + d) % 4], self.rr.at[c, d - 1], self.rq.at[c, d - 1], self.rv.at[c, d - 1], ra, d) for d in (1, 3, 2)]
    def ycopy(self, c):
        x, z, y, f = coords()
        return self.rc(self.tt.at[c, 1 - y], self.yr.at[c], self.ys.at[c], self.yv.at[c], "y", 0)
    def send_f(self, k):
        loc, rem = self.fcopies(k)
        loc.start()
        for r in rem: r.start()
    def send_u(self, c):
        loc, rem = self.ucopies(c)
        loc.start()
        for r in rem: r.start()
    def mm(self, c):
        k, axis = self.plan[c]
        loc, rem = self.ucopies(c)
        loc.wait()
        for r in rem: r.wait()
        if not self.fdone[k]:
            loc, rem = self.fcopies(k)
            loc.wait()
            for r in rem: r.wait()
            self.fdone[k] = True
        self.st[c] = dot(self.ft[k].reshape(640, 1024), self.ub[c].reshape(1024, 640)).astype(jnp.bfloat16).reshape(4, 160, 640)
        me, cps = self.rscopies(c)
        for r in cps: r.start()
    def rs(self, c):
        me, cps = self.rscopies(c)
        for r in cps: r.wait()
        f = jnp.float32
        t = (self.st[c, me].astype(f) + self.rr[c, 0].astype(f)) + (self.rr[c, 1].astype(f) + self.rr[c, 2].astype(f))
        self.tt[c] = t.astype(jnp.bfloat16).reshape(2, 80, 640)
        self.ycopy(c).start()
    def fin(self, c):
        x, z, y, f = coords()
        self.ycopy(c).wait()
        self.out[c] = self.tt[c, y].astype(jnp.float32) + self.yr[c].astype(jnp.float32)

def entry_barrier(peers):
    b = pltpu.get_barrier_semaphore()
    for axis, d in peers:
        pl.semaphore_signal(b, inc=1, device_id=peer(axis, d), device_id_type=MESH)
    pl.semaphore_wait(b, len(peers))

REP = [("x", 1), ("x", 2), ("x", 3), ("z", 1), ("z", 2), ("z", 3), ("y", 1)]

PLAN = [(0, "x")] * 6 + [(1, "z")] * 3 + [(2, "x"), (3, "z"), (4, "z")]
FPLAN = [(0, "x"), (1, "z"), (2, "x"), (2, "z"), (3, "z")]

def grads_kernel(g, n2t, dtt, n1t, drt, dgs, dus, hids, dxs, zs, out, *refs):
    def usrc(c):
        if c < 3: return dgs.at[c]
        if c < 6: return dus.at[c - 3]
        if c < 9: return hids.at[c - 6]
        if c < 11: return dxs.at[c - 9]
        return zs
    g.bind(refs, usrc, [n2t, dtt, n1t, drt], out)
    g.fdone = [False] * len(g.fplan)
    entry_barrier(REP)
    g.send_f(0); g.send_f(1)
    order = [0, 6, 1, 3, 7, 2, 4, 8, 5, 9, 10, 11]
    for j, c in enumerate(order):
        if j == 6:
            for k in (2, 3, 4): g.send_f(k)
        g.send_u(c)
    n = len(order)
    for j in range(n + 4):
        if j < n: g.mm(order[j])
        if 0 <= j - 2 < n: g.rs(order[j - 2])
        if 0 <= j - 4 < n: g.fin(order[j - 4])

def grads(n2t, dtt, n1t, drt, dgs, dus, hids, dxs, zs):
    g = Grads(PLAN, FPLAN)
    return pl.pallas_call(
        functools.partial(grads_kernel, g),
        out_shape=jax.ShapeDtypeStruct((12, 80, 640), jnp.float32),
        in_specs=[pl.BlockSpec(memory_space=pl.ANY)] * 9,
        out_specs=pl.BlockSpec(memory_space=pltpu.VMEM),
        scratch_shapes=g.scratch(),
        compiler_params=pltpu.CompilerParams(collective_id=7, has_side_effects=True, vmem_limit_bytes=VM),
        name="grads",
    )(n2t, dtt, n1t, drt, dgs, dus, hids, dxs, zs)

F32 = jnp.float32
BF = jnp.bfloat16
EPS = 1e-06
ANY = pl.BlockSpec(memory_space=pl.ANY)
VMEM = pl.BlockSpec(memory_space=pltpu.VMEM)

def fpeer(d):
    r = lax.axis_index("rep")
    f = lax.axis_index("fsdp")
    h, c = f // 2, f % 2
    if d % 2:
        c = 1 - c
    if d // 2:
        h = 1 - h
    return r, h * 2 + c

def device(to):
    axis, d = to
    return fpeer(d) if axis == "f" else peer(axis, d)

class Sent:
    def __init__(self, src, dst, to, ssem, rsem):
        self.src, self.dst, self.to, self.ssem, self.rsem = src, dst, to, ssem, rsem
    def make(self):
        return pltpu.make_async_remote_copy(
            src_ref=self.src(), dst_ref=self.dst(), send_sem=self.ssem(), recv_sem=self.rsem(), device_id=device(self.to), device_id_type=MESH)
    def wait_recv(self):
        self.make().wait_recv()
    def wait_send(self):
        self.make().wait_send()

class Comm:
    def __init__(self, ssem, rsem, lsem):
        self.ssem, self.rsem, self.lsem = ssem, rsem, lsem
        self.n = self.m = 0
        self.open = []
    def remote(self, src, dst, to):
        k = self.n
        self.n += 1
        c = Sent(src if callable(src) else lambda: src, dst if callable(dst) else lambda: dst, to, lambda: self.ssem.at[k], lambda: self.rsem.at[k])
        c.make().start()
        self.open.append(c)
        return c
    def local(self, src, dst):
        k = self.m
        self.m += 1
        c = pltpu.make_async_copy(src, dst, self.lsem.at[k])
        c.start()
        return c
    def sent(self, c):
        c.wait_send()
        self.open = [o for o in self.open if o is not c]
    def drain(self):
        for c in self.open:
            c.wait_send()
        self.open = []

class Gather:
    def __init__(self, comm, buf, own=None, parts=None):
        self.comm, self.buf = comm, buf
        self.f = lax.axis_index("fsdp")
        self.parts = parts or [()]
        self.own = own
        self.far, self.near, self.late = {}, {}, {}
    def start(self, which=None):
        f, cm = self.f, self.comm
        for i in range(len(self.parts)) if which is None else (which,):
            p = self.parts[i]
            dst = self.buf.at[(f, *p)]
            src = self.own.at[p] if self.own is not None else dst
            self.far[i] = cm.remote(src, dst, ("f", 2))
            self.near[i] = cm.remote(src, dst, ("f", 1))
    def relay(self, which=None):
        _, o = fpeer(2)
        for i in range(len(self.parts)) if which is None else (which,):
            self.far[i].wait_recv()
            dst = self.buf.at[(o, *self.parts[i])]
            self.late[i] = self.comm.remote(dst, dst, ("f", 1))
    def finish(self, which=None):
        for i in range(len(self.parts)) if which is None else (which,):
            self.near[i].wait_recv()
            self.late[i].wait_recv()

class Reduce:
    def __init__(self, comm, part, r1, s2, r2):
        self.comm, self.part, self.r1, self.s2, self.r2 = comm, part, r1, s2, r2
        self.f = lax.axis_index("fsdp")
        self.a, self.b, self.c = {}, {}, {}
    def send(self, c):
        self.a[c] = self.comm.remote(lambda: self.part.at[c, fpeer(3)[1]], lambda: self.r1.at[c, 1], ("f", 1))
        self.b[c] = self.comm.remote(lambda: self.part.at[c, fpeer(1)[1]], lambda: self.r1.at[c, 0], ("f", 1))
    def mid(self, c):
        _, o2 = fpeer(2)
        self.a[c].wait_recv()
        self.s2[c] = (self.part[c, o2].astype(F32) + self.r1[c, 1].astype(F32)).astype(BF)
        self.c[c] = self.comm.remote(lambda: self.s2.at[c], lambda: self.r2.at[c], ("f", 2))
    def fin(self, c):
        self.b[c].wait_recv()
        self.c[c].wait_recv()
        return self.part[c, self.f].astype(F32) + self.r1[c, 0].astype(F32) + self.r2[c].astype(F32)

def group_barrier(ds):
    b = pltpu.get_barrier_semaphore()
    for d in ds:
        pl.semaphore_signal(b, inc=1, device_id=fpeer(d), device_id_type=MESH)
    pl.semaphore_wait(b, len(ds))

def lanes(q):
    return slice(q * 128, q * 128 + 128)

def row_masks(lenr, ownr, msk):
    me = lax.axis_index("rep")
    j = lax.broadcasted_iota(jnp.int32, (128, 128), 0)
    i = lax.broadcasted_iota(jnp.int32, (128, 128), 1)
    counted = jnp.where(ownr[...] == me, lenr[...], 0)
    mine = jnp.sum(jnp.where(i == j, counted, 0), axis=1, keepdims=True)
    offset = jnp.sum(jnp.where(j < i, mine, 0), axis=0, keepdims=True)
    total = jnp.sum(mine, axis=0, keepdims=True)
    place = lax.broadcasted_iota(jnp.int32, (256, 128), 0)
    hit = jnp.where((ownr[...] == me) & (offset == place), 1.0, 0.0)
    start = jnp.broadcast_to(jnp.max(hit, axis=1, keepdims=True), (256, 128))
    msk[0] = start
    run = start
    for k in (1, 2, 3):
        msk[k] = jnp.where((run == 0.0) & (place >= k), 1.0, 0.0)
        run = jnp.maximum(run, jnp.where(place >= k, pltpu.roll(start, k, axis=0), 0.0))
    msk[4] = jnp.where(place < total, 1.0, 0.0)

def wide_gates(gw, wg):
    row = lax.broadcasted_iota(jnp.int32, (128, 128), 0) // 64
    col = lax.broadcasted_iota(jnp.int32, (128, 128), 1) // 64
    for q in range(5):
        for k in range(2):
            for g in range(2):
                v = gw[k, q * 128:q * 128 + 128, g * 128:g * 128 + 128].astype(F32)
                r = pltpu.roll(v, 64, axis=1)
                for e in range(2):
                    twice = jnp.where(col == e, v, r)
                    p = 2 * g + e
                    wg[q, k * 128:k * 128 + 128, p * 128:p * 128 + 128] = jnp.where(row == col, twice, 0.0).astype(BF)

def softplus(v):
    return jnp.maximum(v, 0.0) + jnp.log1p(jnp.exp(-jnp.abs(v)))

def sigmoid(v):
    return 1.0 / (1.0 + jnp.exp(-v))

def scan_rows(a_ref, u_ref, h_ref, back):
    rows = lax.broadcasted_iota(jnp.int32, (8, 640), 0)
    carry = jnp.zeros((1, 640), F32)
    order = range(31, -1, -1) if back else range(32)
    for i in order:
        a = a_ref[i * 8:i * 8 + 8, :]
        u = u_ref[i * 8:i * 8 + 8, :]
        for s in (1, 2, 4):
            if back:
                ok = rows < 8 - s
                a2 = jnp.where(ok, pltpu.roll(a, 8 - s, axis=0), 1.0)
                u2 = jnp.where(ok, pltpu.roll(u, 8 - s, axis=0), 0.0)
            else:
                ok = rows >= s
                a2 = jnp.where(ok, pltpu.roll(a, s, axis=0), 1.0)
                u2 = jnp.where(ok, pltpu.roll(u, s, axis=0), 0.0)
            u = u + a * u2
            a = a * a2
        h = u + a * carry
        h_ref[i * 8:i * 8 + 8, :] = h
        carry = h[0:1, :] if back else h[7:8, :]

def gate_values(q, pre, par, start):
    gx = sigmoid(pre[:, 0:128] + par[5:6, lanes(q)])
    ga = sigmoid(pre[:, 128:256] + par[6:7, lanes(q)])
    return gx, ga

def decay_of(q, ga, par, start):
    sp = softplus(par[7:8, lanes(q)])
    a = jnp.exp(-8.0 * ga * sp)
    spread = 1.0 - a * a
    mult = jnp.where(start == 1.0, 1.0, jnp.sqrt(jnp.maximum(spread, 0.01)))
    return sp, a, spread, mult

def prep(seq_len, seq_owner, gain_1, gain_2, w_xy, conv_w, conv_b, gate_w, gate_b, a_param, w_out):
    small = (seq_len.reshape(1, 128), seq_owner.reshape(1, 128), gain_1, gain_2,
             jnp.transpose(conv_w, (1, 0, 2)), conv_b, jnp.transpose(gate_b, (1, 0, 2)), a_param)
    w_t = jnp.transpose(w_xy, (0, 2, 3, 1)).reshape(2, 640, 2560)
    gw_t = jnp.swapaxes(gate_w, 2, 3).reshape(2, 640, 256)
    return small, w_t, gw_t, w_out.reshape(640, 2560)

def dot_tn(a, b):
    return lax.dot_general(a, b, (((0,), (0,)), ((), ())), preferred_element_type=jnp.float32)

class Swap:
    def __init__(self, comm, src, dst):
        f = lax.axis_index("fsdp")
        self.cps = []
        for d in (3, 2, 1):
            _, t = fpeer(d)
            self.cps.append(comm.remote(src.at[t], dst.at[f], ("f", d)))
        self.own = comm.local(src.at[f], dst.at[f])
    def finish(self):
        self.own.wait()
        for c in self.cps:
            c.wait_recv()

def spread(cm, src, dst, axis):
    return [cm.remote(src(d), dst.at[d - 1], (axis, d)) for d in (1, 3, 2)]

def arrived(cps):
    for c in cps:
        c.wait_recv()

CHUNK_FEATURES = [0] * 6 + [1] * 3 + [2, 3, 4]
FEATURE_AXIS = ["x", "z", "x", "z", "x"]
FEATURE_SLOT = [0, 1, 0, 1, 2]

class Sums:
    def __init__(self, cm, uland, fland, rrh, yr, usrc, fsrc, out):
        self.cm, self.uland, self.fland, self.rrh, self.yr = cm, uland, fland, rrh, yr
        self.usrc, self.fsrc, self.out = usrc, fsrc, out
        self.x, self.z, self.y, f = coords()
        self.core = f % 2
        self.u, self.u2, self.f, self.f2, self.r, self.yc = {}, {}, {}, {}, {}, {}
        self.nw = self.nst = self.nr = self.ntt = 0
        self.win, self.stc, self.rwin, self.ttc = {}, {}, {}, {}
        self.loaded = {}
        self.h, self.place = {}, {}
    def work(self, ft, uw, st, rw, tt, hb):
        self.ft, self.uw, self.st, self.rw, self.tt, self.hb = ft, uw, st, rw, tt, hb
    def axis(self, c):
        return FEATURE_AXIS[CHUNK_FEATURES[c]]
    def pos(self, axis):
        return self.x if axis == "x" else self.z
    def send_f(self, k):
        axis = FEATURE_AXIS[k]
        me = self.pos(axis)
        def one(d):
            def src():
                t, h = (me + d) % 4, pl.ds(2 * self.core, 2)
                return self.fsrc[k].at[t, h] if axis == "x" else self.fsrc[k].at[h, t]
            return self.cm.remote(src, lambda: self.fland[k].at[d - 1, pl.ds(2 * self.core, 2)], (axis, d))
        self.f[k] = {d: one(d) for d in (1, 3, 2)}
    def relay_f(self, k):
        def one(d):
            self.f[k][d].wait_recv()
            half = lambda: self.fland[k].at[d - 1, pl.ds(2 * self.core, 2)]
            return self.cm.remote(half, half, ("f", 1))
        self.f2[k] = [one(d) for d in (1, 3, 2)]
    def send_u(self, c, direct=False):
        def one(d):
            return self.cm.remote(lambda: self.usrc[c], lambda: self.uland[c].at[d - 1], (self.axis(c), d))
        self.u[c] = {d: one(d) for d in ((1, 3, 2) if direct else (1, 3))}
        if direct:
            self.u2[c] = list(self.u[c].values())
    def relay_u(self, c):
        low, high = pl.ds(0, 128), pl.ds(128, 128)
        self.u[c][1].wait_recv()
        a = self.cm.remote(lambda: self.uland[c].at[0, low], lambda: self.uland[c].at[1, low], (self.axis(c), 1))
        self.u[c][3].wait_recv()
        b = self.cm.remote(lambda: self.uland[c].at[2, high], lambda: self.uland[c].at[1, high], (self.axis(c), 3))
        self.u2[c] = [a, b]
    def load_f(self, k):
        s = FEATURE_SLOT[k]
        axis = FEATURE_AXIS[k]
        me = self.pos(axis)
        own = self.fsrc[k].at[me] if axis == "x" else self.fsrc[k].at[:, me]
        cps = [self.cm.local(own, self.ft.at[s, :, :, pl.ds(0, 256)])]
        arrived(self.f2.get(k, []))
        for d in (1, 2, 3):
            cps.append(self.cm.local(self.fland[k].at[d - 1], self.ft.at[s, :, :, pl.ds(d * 256, 256)]))
        self.loaded[k] = cps
    def prep(self, c):
        k = CHUNK_FEATURES[c]
        if k not in self.loaded:
            self.load_f(k)
        w = self.nw % 2
        self.nw += 1
        cps = [self.cm.local(self.usrc[c], self.uw.at[w, 0])]
        arrived(self.u2.get(c, []))
        cps.append(self.cm.local(self.uland[c], self.uw.at[w, pl.ds(1, 3)]))
        self.win[c] = (w, cps)
    def mm(self, c, direct=False):
        k = CHUNK_FEATURES[c]
        for l in self.loaded[k]:
            l.wait()
        self.loaded[k] = []
        w, cps = self.win[c]
        for l in cps:
            l.wait()
        i = self.nst % 4
        self.nst += 1
        for old in self.stc.get(i, []):
            self.cm.sent(old)
        s = self.st
        for h in (0, 2):
            v = dot(self.ft[FEATURE_SLOT[k], h:h + 2].reshape(320, 1024), self.uw[w].reshape(1024, 640))
            s[i, h:h + 2] = v.astype(BF).reshape(2, 160, 640)
        axis = "z" if self.axis(c) == "x" else "x"
        me = self.pos(axis)
        far = (me + 2) % 4
        if direct:
            cps = [self.cm.remote(s.at[i, (me + d) % 4], self.rrh.at[c, d - 1], (axis, d)) for d in (1, 3, 2)]
            self.stc[i] = cps
        else:
            self.h[c] = [self.cm.remote(s.at[i, far, pl.ds(0, 80)], self.hb.at[c, 0], (axis, 1)), self.cm.remote(s.at[i, far, pl.ds(80, 80)], self.hb.at[c, 1], (axis, 3))]
            self.stc[i] = list(self.h[c])
        t = self.ntt % 12
        self.ntt += 1
        for old in self.ttc.get(t, []):
            self.cm.sent(old)
        self.tt[t] = s[i, me].reshape(2, 80, 640)
        self.place[c] = (i, t)
        if direct:
            self.r[c] = (t, cps)
    def wsum(self, c):
        i, t = self.place[c]
        s = self.st
        axis = "z" if self.axis(c) == "x" else "x"
        me = self.pos(axis)
        up, down = (me + 1) % 4, (me + 3) % 4
        self.h[c][0].wait_recv()
        s[i, up, 0:80] = (s[i, up, 0:80].astype(F32) + self.hb[c, 0].astype(F32)).astype(BF)
        a = self.cm.remote(s.at[i, up], self.rrh.at[c, 0], (axis, 1))
        self.h[c][1].wait_recv()
        s[i, down, 80:160] = (s[i, down, 80:160].astype(F32) + self.hb[c, 1].astype(F32)).astype(BF)
        b = self.cm.remote(s.at[i, down], self.rrh.at[c, 2], (axis, 3))
        self.stc[i] += [a, b]
        self.r[c] = (t, [a, b])
    def rprep(self, c):
        t, cps = self.r[c]
        arrived(cps)
        w = self.nr % 2
        self.nr += 1
        slots = (0, 1, 2) if len(cps) == 3 else (0, 2)
        self.rwin[c] = (w, [self.cm.local(self.rrh.at[c, j], self.rw.at[w, j]) for j in slots])
    def rsum(self, c):
        t, _ = self.r[c]
        w, ls = self.rwin[c]
        for l in ls:
            l.wait()
        total = self.tt[t].reshape(160, 640).astype(F32) + (self.rw[w, 0].astype(F32) + self.rw[w, 2].astype(F32))
        if len(ls) == 3:
            total = total + self.rw[w, 1].astype(F32)
        self.tt[t] = total.astype(BF).reshape(2, 80, 640)
        cp = self.cm.remote(self.tt.at[t, 1 - self.y], self.yr.at[c], ("y", 1))
        self.ttc[t] = [cp]
        self.yc[c] = cp
    def fin(self, c):
        self.yc[c].wait_recv()
        t, _ = self.r[c]
        self.out(c, self.tt[t, self.y].astype(F32) + self.yr[c].astype(F32))

def forward_kernel(lenr, ownr, g1r, g2r, cwt, cbt, gbt, apt, tok, cot, w_t, gw_h, wo_h,
                   n1_o, cv_o, xb_o, yb_o, gx_o, ga_o, hs_o, z_o, n2_o, dt_o, h1_o, msk_o, r_o, g_o, wg_o, tk_o, n1t_o, dtt_o, pf, pu, par_o,
                   tkb, ctb, gnb, wv, gw, wo, wg, n1, dt, cvb, xb, yb, gx, ga, aa, uu, hs, z, msk, pt, r1, s2, r2, h1, n2b, rs1, rs2, n1t, dtt, par, gn,
                   ssem, rsem, lsem):
    cm = Comm(ssem, rsem, lsem)
    f = lax.axis_index("fsdp")
    lw = [cm.local(w_t.at[0], wv.at[0]), cm.local(gw_h, gw), cm.local(w_t.at[1], wv.at[1]), cm.local(wo_h, wo)]
    lt = [cm.local(tok, tkb.at[f]), cm.local(cot, ctb.at[f])]
    gn[0, :] = g1r[...].astype(F32)
    gn[1, :] = g2r[...].astype(F32)
    lt.append(cm.local(gn, gnb.at[f]))
    b = pltpu.get_barrier_semaphore()
    for axis, d in REP[:6]:
        pl.semaphore_signal(b, inc=1, device_id=peer(axis, d), device_id_type=MESH)
    for d in (1, 2):
        pl.semaphore_signal(b, inc=1, device_id=fpeer(d), device_id_type=MESH)
    pl.semaphore_wait(b, 8)
    S = Sums(cm, [None] * 11 + [pu], [None, pf.at[0], pf.at[1], pf.at[2]], None, None, [None] * 11 + [z], [None, dtt, n1t, n1t], None)
    gtk = Gather(cm, tkb, tok, [(pl.ds(i * 64, 64),) for i in range(4)])
    ggn = Gather(cm, gnb, gn)
    gct = Gather(cm, ctb, cot)
    ggn.start()
    gtk.start()
    for h in range(10):
        ls = slice(h * 64, h * 64 + 64)
        par[0:4, ls] = cwt[h].astype(F32)
        par[4:5, ls] = cbt[h:h + 1].astype(F32)
        par[5:7, ls] = gbt[h].astype(F32)
        par[7:8, ls] = apt[h:h + 1]
    row_masks(lenr, ownr, msk)
    lw[1].wait()
    wide_gates(gw, wg)
    outs = [cm.local(msk, msk_o), cm.local(wg, wg_o), cm.local(par, par_o)]
    ggn.relay()
    for c in lt:
        c.wait()
    ggn.finish()
    gtk.relay(0)
    gtk.relay(1)
    for j in range(4):
        gtk.finish(j)
        @pl.loop(j * 4, j * 4 + 4)
        def _(i):
            rows = pl.ds(pl.multiple_of(i * 16, 16), 16)
            xs = [tkb[p, rows, :].astype(F32) for p in range(4)]
            ss = sum(jnp.sum(x * x, axis=-1, keepdims=True) for x in xs)
            r = lax.rsqrt(ss * (1.0 / 2560) + EPS)
            rs1[rows, :] = jnp.broadcast_to(r, (16, 128))
            for p in range(4):
                n1[rows, p * 640:p * 640 + 640] = (xs[p] * r * gnb[p, 0:1, :]).astype(BF)
        if j < 2:
            gtk.relay(j + 2)
    outs += [cm.local(n1, n1_o), cm.local(gnb, g_o), cm.local(tkb, tk_o)]
    lw[0].wait()
    gcv = Gather(cm, cvb, None, [(q,) for q in range(5)])
    for qs in ((0, 1), (2, 3), (4,)):
        cs = slice(qs[0] * 128, qs[-1] * 128 + 128)
        xb[:, cs] = dot_nt(n1[...], wv[0, cs, :])
        for q in qs:
            x = xb[:, lanes(q)]
            acc = par[4:5, lanes(q)] + par[0:1, lanes(q)] * x
            for k in (1, 2, 3):
                acc = acc + par[k:k + 1, lanes(q)] * pltpu.roll(x, k, axis=0) * msk[k]
            cvb[f, q] = acc.astype(BF)
            gcv.start(q)
    gct.start()
    outs.append(cm.local(xb, xb_o))
    lw[2].wait()
    yb[...] = dot_nt(n1[...], wv[1])
    outs.append(cm.local(yb, yb_o))
    gcv.relay(0)
    gcv.relay(1)
    for q in range(5):
        gcv.finish(q)
        lhs = jnp.concatenate([cvb[p, q] for p in range(4)], axis=1)
        pre = dot_nt(lhs, wg[q])
        gxq, gaq = gate_values(q, pre, par, msk[0])
        sp, a, spread, mult = decay_of(q, gaq, par, msk[0])
        gx[:, lanes(q)] = gxq
        ga[:, lanes(q)] = gaq
        aa[:, lanes(q)] = jnp.where(msk[0] == 1.0, 0.0, a)
        uu[:, lanes(q)] = mult * gxq * cvb[f, q].astype(F32)
        if q < 3:
            gcv.relay(q + 2)
        if q < 4:
            n1t[q] = n1[:, q * 640:q * 640 + 640].T.reshape(4, 160, 256)
    outs.append(cm.local(cvb, cv_o))
    S.send_f(2)
    S.send_f(3)
    outs.append(cm.local(n1t, n1t_o))
    outs += [cm.local(gx, gx_o), cm.local(ga, ga_o)]
    scan_rows(aa, uu, hs, False)
    for q in range(5):
        yg, _ = gelu_parts(yb[:, lanes(q)])
        z[:, lanes(q)] = (hs[:, lanes(q)] * yg).astype(BF)
    S.send_u(11, direct=True)
    outs += [cm.local(hs, hs_o), cm.local(z, z_o)]
    lw[3].wait()
    red = Reduce(cm, pt, r1, s2, r2)
    for c in range(4):
        pt[c] = dot(z[...], wo[:, c * 640:c * 640 + 640]).astype(BF).reshape(4, 64, 640)
        red.send(c)
        if c: red.mid(c - 1)
    red.mid(3)
    gct.relay()
    gct.finish()
    @pl.loop(0, 16)
    def _(i):
        rows = pl.ds(pl.multiple_of(i * 16, 16), 16)
        live = jnp.broadcast_to(msk[4, rows, 0:1], (16, 640))
        for p in range(4):
            dt[rows, p * 640:p * 640 + 640] = (ctb[p, rows, :].astype(F32) * live).astype(BF)
    outs.append(cm.local(dt, dt_o))
    for c in range(4):
        dtt[c] = dt[:, c * 640:c * 640 + 640].T.reshape(4, 160, 256)
    S.send_f(1)
    outs.append(cm.local(dtt, dtt_o))
    for k in (2, 3):
        S.relay_f(k)
    own = pl.ds(pl.multiple_of(f * 64, 64), 64)
    ss = jnp.zeros((64, 1), F32)
    for c in range(4):
        h = tkb[c, own, :].astype(F32) + red.fin(c)
        h1[:, c * 640:c * 640 + 640] = h
        ss = ss + jnp.sum(h * h, axis=-1, keepdims=True)
    r = lax.rsqrt(ss * (1.0 / 2560) + EPS)
    rs2[...] = jnp.broadcast_to(r, (64, 128))
    for c in range(4):
        cs = slice(c * 640, c * 640 + 640)
        n2b[f, :, cs] = (h1[:, cs] * r * gnb[c, 1:2, :]).astype(BF)
    gn2 = Gather(cm, n2b, None, [(pl.ds(i * 16, 16),) for i in range(4)])
    gn2.start()
    outs += [cm.local(h1, h1_o), cm.local(rs1, r_o.at[pl.ds(0, 256)]), cm.local(rs2, r_o.at[pl.ds(256, 64)])]
    for i in range(4):
        gn2.relay(i)
    S.relay_f(1)
    gn2.finish()
    outs.append(cm.local(n2b, n2_o))
    for k in (2, 3, 1):
        arrived(S.f2[k])
    arrived(S.u[11].values())
    for c in outs:
        c.wait()
    cm.drain()

def forward(lenr, ownr, g1r, g2r, cwt, cbt, gbt, apt, tok, cot, w_t, gw_t, wo):
    s = jax.ShapeDtypeStruct
    R = 256
    fw = s((R, 640), F32)
    out_shape = [s((R, 2560), BF), s((4, 5, R, 128), BF), fw, fw, fw, fw, fw, s((R, 640), BF), s((4, 64, 2560), BF), s((R, 2560), BF),
                 s((64, 2560), F32), s((5, R, 128), F32), s((320, 128), F32), s((4, 8, 640), F32), s((5, 256, 512), BF), s((4, R, 640), BF), s((4, 4, 160, 256), BF), s((4, 4, 160, 256), BF), s((3, 3, 4, 160, 256), BF), s((3, R, 640), BF), s((8, 640), F32)]
    V = pltpu.VMEM
    f640 = V((R, 640), F32)
    scratch = [V((4, R, 640), BF), V((4, R, 640), BF), V((4, 8, 640), F32), V((2, 640, 2560), BF), V((2, 640, 256), BF), V((640, 2560), BF),
               V((5, 256, 512), BF), V((R, 2560), BF), V((R, 2560), BF), V((4, 5, R, 128), BF), f640, f640, f640, f640, f640, f640, f640,
               V((R, 640), BF), V((5, R, 128), F32), V((4, 4, 64, 640), BF), V((4, 2, 64, 640), BF), V((4, 64, 640), BF), V((4, 64, 640), BF),
               V((64, 2560), F32), V((4, 64, 2560), BF), V((R, 128), F32), V((64, 128), F32), V((4, 4, 160, 256), BF), V((4, 4, 160, 256), BF), V((8, 640), F32), V((8, 640), F32),
               pltpu.SemaphoreType.DMA((80,)), pltpu.SemaphoreType.DMA((80,)), pltpu.SemaphoreType.DMA((40,))]
    return pl.pallas_call(
        forward_kernel, out_shape=out_shape,
        in_specs=[VMEM] * 8 + [ANY] * 5,
        out_specs=[ANY] * len(out_shape),
        scratch_shapes=scratch,
        compiler_params=pltpu.CompilerParams(collective_id=3, has_side_effects=True, vmem_limit_bytes=VM),
        name="forward",
    )(lenr, ownr, g1r, g2r, cwt, cbt, gbt, apt, tok, cot, w_t, gw_t, wo)

def finish_kernel(bo, dtok, d_in, d_dn, d_xy, d_wo, gate, sm, bo_o, dtok_o, in_o, dn_o, xy_o, wo_o, gate_o, g1_o, g2_o, cw_o, cb_o, gb_o, a_o,
                  b0, b1, b2, b3, b4, b5, seml, sems):
    ways = ((d_in, b2, in_o), (d_xy, b4, xy_o), (dtok, b1, dtok_o), (d_dn, b3, dn_o), (bo, b0, bo_o), (d_wo, b5, wo_o))
    loads = [pltpu.make_async_copy(s, v, seml.at[i]) for i, (s, v, d) in enumerate(ways)]
    stores = [pltpu.make_async_copy(v, d, sems.at[i]) for i, (s, v, d) in enumerate(ways)]
    for c in loads:
        c.start()
    for l, c in zip(loads, stores):
        l.wait()
        c.start()
    g1_o[...] = sm[0]
    g2_o[...] = sm[1]
    for h in range(10):
        ls = slice(h * 64, h * 64 + 64)
        cw_o[h] = sm[2:6, ls]
        cb_o[h:h + 1] = sm[6:7, ls]
        gb_o[h] = sm[7:9, ls]
        a_o[h:h + 1] = sm[9:10, ls]
        for k in range(2):
            gate_o[k, h] = gate[k, h // 2, :, h % 2 * 64:h % 2 * 64 + 64]
    for c in stores:
        c.wait()

def finish(bo, dtok, d_in, d_dn, d_xy, d_wo, gate, sm):
    s = jax.ShapeDtypeStruct
    out_shape = [s((4, 64, 640), BF), s((256, 640), F32), s((2, 80, 1920), F32), s((80, 1920), F32), s((2, 640, 80), F32), s((640, 80), F32),
                 s((2, 10, 8, 64), F32), s((640,), F32), s((640,), F32), s((10, 4, 64), F32), s((10, 64), F32), s((10, 2, 64), F32), s((10, 64), F32)]
    return pl.pallas_call(
        finish_kernel, out_shape=out_shape,
        in_specs=[ANY] * 6 + [VMEM] * 2,
        out_specs=[ANY] * 6 + [VMEM] * 7,
        scratch_shapes=[pltpu.VMEM(o.shape, o.dtype) for o in out_shape[:6]] + [pltpu.SemaphoreType.DMA((6,)), pltpu.SemaphoreType.DMA((6,))],
        compiler_params=pltpu.CompilerParams(vmem_limit_bytes=VM),
        name="finish",
    )(bo, dtok, d_in, d_dn, d_xy, d_wo, gate, sm)

PLAN = {
    "F0h": "d6",
    "F0g": "u0",
    "F0": "",
    "F1h": "q0 u3",
    "F1g": "u7",
    "F1": "",
    "F2h": "r0",
    "F2g": "",
    "F2": "d8 u1",
    "C0": "r3",
    "C1": "r7 r1 p0 u4 m0 p6 m6",
    "C2": "p3 p1 m3 u2 m1",
    "C2b": "w0 u5 w6 p7 r4 w1 w3",
    "C3": "",
    "C3b": "r2 m7 r5",
    "C5": "p4 m4 r10 v6 q4 p2 w4 v0 s6",
    "C6": "s0 m2 p5 m5 p8 w7 f0 w2 v3 p11 s3 v1",
    "E": "s1 w5 m8 v7 n11 p10 v2 r9 f6 m10 s7 w8 p9 s2 n9 g0 v4 f3 w10 s4 v5 f2 f7 s5 v8 f4 v11 s8 s11 v10 f5 s10 v9 s9 f8 f1 f10 g1 f9 f11 g2",
}

def tail_kernel(plan, par, n2_h, dt_h, w_in, w_dn, n1t_h, dtt_h, pf, pu, z_h, cv_h, xb_h, yb_h, gx_h, ga_h, hs_h, msk_h, r_h, g_h, wg_h, tk_h, h1_h, w_t, wo_h,
                bo_o, dtok_o, in_o, dn_o, xy_o, wout_o, gate_o, sm_o, ubh, rrh, fth,
                un, gu, hb, yr, fts, dr, pd, pm, bob, dto, gs, gr, sm, sgr, sgt, sgr2, sgy, sma, smr, smy,
                m1, m2, m3, d1, d2, d3, e1, e2, e3, f1, f2, f3, gnb, rb, h1, dtb, tk,
                ssem, rsem, lsem):
    cm = Comm(ssem, rsem, lsem)
    f = lax.axis_index("fsdp")
    x, z, y, _ = coords()
    own = pl.ds(pl.multiple_of(f * 64, 64), 64)
    rd = Reduce(cm, pd, d1, d2, d3)
    rm = Reduce(cm, pm, m1, m2, m3)
    def put(c, v):
        if c < 6:
            in_o[c // 3, :, c % 3 * 640:c % 3 * 640 + 640] = v
        elif c < 9:
            dn_o[:, (c - 6) * 640:(c - 6) * 640 + 640] = v
        elif c < 11:
            xy_o[c - 9] = v.T
        else:
            wout_o[...] = v.T
    usrc = [gu.at[i, :, pl.ds(j, 640)] for j in (0, 640) for i in range(3)] + [un.at[i] for i in range(3)] + [None, None, z_h]
    uland = [ubh.at[c] for c in range(11)] + [pu]
    fland = [fth.at[0], pf.at[0], pf.at[1], pf.at[2], fth.at[1]]
    S = Sums(cm, uland, fland, rrh, yr, usrc, [fts, dtt_h, n1t_h, n1t_h, fts], put)

    w = pltpu.VMEM((256, 640), F32)

    small = {}
    def at(point):
        for t in plan[point].split():
            run(t[0], int(t[1:]))
    def run(t, c):
        if t == "u": S.send_u(c)
        elif t == "d": S.send_u(c, direct=True)
        elif t == "r": S.relay_u(c)
        elif t == "q": S.relay_f(c)
        elif t == "p": S.prep(c)
        elif t == "m": S.mm(c)
        elif t == "n": S.mm(c, direct=True)
        elif t == "w": S.wsum(c)
        elif t == "v": S.rprep(c)
        elif t == "s": S.rsum(c)
        elif t == "f": S.fin(c)
        else: small_step(c)
    def small_step(j):
        if j == 0:
            arrived(small["g2"])
            sgy[0] = sgt[x].astype(F32) + sgr2[0].astype(F32) + sgr2[1].astype(F32) + sgr2[2].astype(F32)
            small[0] = cm.remote(sgy.at[0], sgy.at[1], ("y", 1))
            arrived(small["v1"])
            sma[1] = (sma[0] + smr[0, 0]) + (smr[0, 1] + smr[0, 2])
            small[1] = spread(cm, lambda d: sma.at[1], smr.at[1], "z")
        if j == 1:
            arrived(small[1])
            sma[2] = (sma[1] + smr[1, 0]) + (smr[1, 1] + smr[1, 2])
            small[2] = cm.remote(sma.at[2], smy, ("y", 1))
            small[0].wait_recv()
            half = pl.ds(pl.multiple_of(y * 8, 8), 8)
            gate_o[...] = sgy[0, :, :, half, :] + sgy[1, :, :, half, :]
        if j == 2:
            small[2].wait_recv()
            sm_o[...] = sma[2] + smy[...]

    def ffn_phase(wa, wd, am, ad, fg, fd, n2, dt):
        def load(i):
            s = i % 2
            cols = pl.ds(i * 640, 640)
            return [cm.local(w_in.at[0, :, cols], wa.at[s, :, pl.ds(0, 640)]), cm.local(w_in.at[1, :, cols], wa.at[s, :, pl.ds(640, 640)]), cm.local(w_dn.at[cols], wd.at[s])]
        ln = cm.local(n2_h, n2)
        lw = {0: load(0)}
        ld = cm.local(dt_h, dt)
        b = pltpu.get_barrier_semaphore()
        for axis, d in REP:
            pl.semaphore_signal(b, inc=1, device_id=peer(axis, d), device_id_type=MESH)
        for d in (1, 2, 3):
            pl.semaphore_signal(b, inc=1, device_id=fpeer(d), device_id_type=MESH)
        ln.wait()
        for c in range(4):
            fts[c] = n2[:, c * 640:c * 640 + 640].T.reshape(4, 160, 256)
        pl.semaphore_wait(b, len(REP) + 3)
        S.send_f(0)
        for i in range(3):
            s = i % 2
            lw[i][0].wait()
            lw[i][1].wait()
            fg[...] = dot(n2[...], wa[s])
            for q in range(5):
                gl, _ = gelu_parts(fg[:, lanes(q)])
                un[i, :, lanes(q)] = (gl * fg[:, lanes(q + 5)]).astype(BF)
            at(f"F{i}h")
            lw[i][2].wait()
            if i == 0:
                lw[1] = load(1)
                ld.wait()
            fd[...] = dot_nt(dt[...], wd[s])
            for q in range(5):
                gl, dgl = gelu_parts(fg[:, lanes(q)])
                dh = fd[:, lanes(q)]
                gu[i, :, lanes(q)] = (dh * fg[:, lanes(q + 5)] * dgl).astype(BF)
                gu[i, :, lanes(q + 5)] = (dh * gl).astype(BF)
            at(f"F{i}g")
            for c in range(4):
                cs = slice(c * 640, c * 640 + 640)
                v = dot_nt(gu[i], wa[s, cs, :])
                if i == 0:
                    ad[:, cs] = v
                elif i == 1:
                    ad[:, cs] = ad[:, cs] + v
                else:
                    pd[c] = (ad[:, cs] + v).astype(BF).reshape(4, 64, 640)
                    rd.send(c)
                    if c: rd.mid(c - 1)
            if i == 2:
                rd.mid(3)
            for c in range(4):
                cs = slice(c * 640, c * 640 + 640)
                v = dot(un[i], wd[s, :, cs])
                if i == 0:
                    am[:, cs] = v
                elif i == 1:
                    am[:, cs] = am[:, cs] + v
                else:
                    pm[c] = (am[:, cs] + v).astype(BF).reshape(4, 64, 640)
            if i == 0:
                lw[2] = load(2)
            at(f"F{i}")

    pl.run_scoped(ffn_phase, pltpu.VMEM((2, 2560, 1280), BF), pltpu.VMEM((2, 640, 2560), BF), pltpu.VMEM((256, 2560), F32), pltpu.VMEM((256, 2560), F32), pltpu.VMEM((256, 1280), F32), w, pltpu.VMEM((256, 2560), BF), pltpu.VMEM((256, 2560), BF))

    def chain_phase(cv, xb, yb, gx, ga, hs, msk, wg, wbuf, aa, uu, gg, dc1, dp, dna, ft, uw, st, rw, tt, bo, dob, sg, dxy, dxx, pb, dnp, dh1):
        S.work(ft, uw, st, rw, tt, hb)
        S.usrc[9], S.usrc[10] = dxy.at[0], dxy.at[1]
        lh = [cm.local(h1_h, h1), cm.local(g_h, gnb), cm.local(r_h, rb), cm.local(dt_h.at[own], dtb), cm.local(tk_h.at[:, own], tk)]
        lb = [cm.local(wo_h, wbuf.at[0]), cm.local(yb_h, yb), cm.local(hs_h, hs), cm.local(ga_h, ga), cm.local(msk_h, msk), cm.local(gx_h, gx), cm.local(cv_h, cv),
              cm.local(wg_h, wg), cm.local(xb_h, xb), cm.local(w_t.at[1], wbuf.at[1])]
        for c in range(4):
            rm.send(c)
        at("C0")
        for c in lh:
            c.wait()
        gs[...] = jnp.zeros_like(gs)
        r2 = rb[256:320, 0:1]
        acc = jnp.zeros((64, 1), F32)
        for c in range(4):
            cs = slice(c * 640, c * 640 + 640)
            dn = rd.fin(c)
            h = h1[:, cs]
            gs[c, 1:2, :] = jnp.sum(dn * h * r2, axis=0, keepdims=True)
            v = dn * gnb[c, 1:2, :]
            dh1[:, cs] = v
            acc = acc + jnp.sum(v * h, axis=-1, keepdims=True)
        acc = acc * (1.0 / 2560) * (r2 * r2 * r2)
        for c in range(4):
            cs = slice(c * 640, c * 640 + 640)
            d = dtb[:, cs].astype(F32) + r2 * dh1[:, cs] - h1[:, cs] * acc
            dh1[:, cs] = d
            dr[f, :, cs] = d.astype(BF)
        gdr = Gather(cm, dr, None, [(pl.ds(0, 32),), (pl.ds(32, 32),)])
        gdr.start()
        for c in range(4):
            rm.mid(c)
        at("C1")
        for c in lb:
            c.wait()
        for q in range(5):
            sp, a, spread_, mult = decay_of(q, ga[:, lanes(q)], par, msk[0])
            up = pltpu.roll(jnp.where(msk[0] == 1.0, 0.0, a), 255, axis=0)
            rows = lax.broadcasted_iota(jnp.int32, (256, 128), 0)
            aa[:, lanes(q)] = jnp.where(rows == 255, 0.0, up)
        gdr.relay()
        at("C2")
        gdr.finish()
        uu[...] = dot_nt(dr[...].reshape(256, 2560), wbuf[0])
        lw0 = cm.local(w_t.at[0], wbuf.at[0])
        for q in range(5):
            yg, dgl = gelu_parts(yb[:, lanes(q)])
            dz = uu[:, lanes(q)]
            dxy[1, :, lanes(q)] = (dz * hs[:, lanes(q)] * dgl).astype(BF)
            uu[:, lanes(q)] = dz * yg
        S.send_u(10)
        at("C2b")
        scan_rows(aa, uu, gg, True)
        re = Reduce(cm, pb, e1, e2, e3)
        for q in range(5):
            ls = lanes(q)
            start = msk[0]
            gxq, gaq, g = gx[:, ls], ga[:, ls], gg[:, ls]
            sp, a, spread_, mult = decay_of(q, gaq, par, start)
            cvq = cv[f, q].astype(F32)
            prev = jnp.where(start == 1.0, 0.0, pltpu.roll(hs[:, ls], 1, axis=0))
            slope = jnp.where((start == 1.0) | (spread_ <= 0.01), 0.0, -a / mult)
            da = g * prev + g * gxq * cvq * slope
            dc1[:, ls] = g * mult * gxq
            dlog = da * a
            da_p = jnp.sum(dlog * (-8.0 * gaq), axis=0, keepdims=True) * sigmoid(par[7:8, ls])
            px = (g * mult * cvq * gxq * (1.0 - gxq)).astype(BF)
            pa = (-8.0 * dlog * sp * gaq * (1.0 - gaq)).astype(BF)
            dp[q, :, 0:128] = px
            dp[q, :, 128:256] = pa
            sm[7:8, ls] = jnp.sum(px.astype(F32), axis=0, keepdims=True)
            sm[8:9, ls] = jnp.sum(pa.astype(F32), axis=0, keepdims=True)
            sm[9:10, ls] = da_p
            db = dot(dp[q], wg[q]).astype(BF)
            for p in range(4):
                pb[q, p] = db[:, lanes(p)]
            re.send(q)
            if q: re.mid(q - 1)
        re.mid(4)
        for old in S.f[0].values():
            cm.sent(old)
        drt = dr[...].reshape(256, 2560)
        for c in range(4):
            fts[c] = drt[:, c * 640:c * 640 + 640].T.reshape(4, 160, 256)
        S.send_f(4)
        at("C3")
        for c in range(4):
            cs = slice(c * 640, c * 640 + 640)
            dna[c] = dot(dxy[1], wbuf[1, :, cs])
        low = lax.broadcasted_iota(jnp.int32, (64, 128), 1) < 64
        for q in range(5):
            lhs = jnp.concatenate([cv[p, q] for p in range(4)], axis=1)
            gwt = dot_tn(lhs, dp[q])
            for p in range(4):
                for k in range(2):
                    blk = gwt[p * 128:p * 128 + 128, k * 128:k * 128 + 128]
                    sg[p, k, q] = jnp.where(low, blk[0:64], blk[64:128]).astype(BF)
        g1 = spread(cm, lambda d: sg.at[:, :, :, pl.ds(pl.multiple_of((z + d) % 4 * 16, 16), 16)], sgr, "z")
        at("C3b")
        live = msk[4, own, 0:1]
        for c in range(4):
            bo[c] = (live * (h1[:, c * 640:c * 640 + 640] + rm.fin(c))).astype(BF)
        sbo = Swap(cm, bo, bob)
        for q in range(5):
            ls = lanes(q)
            d = dc1[:, ls] + re.fin(q)
            xq = xb[:, ls]
            sm[6:7, ls] = jnp.sum(d, axis=0, keepdims=True)
            sm[2:3, ls] = jnp.sum(d * xq, axis=0, keepdims=True)
            dx = par[0:1, ls] * d
            for k in (1, 2, 3):
                m = d * msk[k]
                sm[2 + k:3 + k, ls] = jnp.sum(m * pltpu.roll(xq, k, axis=0), axis=0, keepdims=True)
                dx = dx + par[k:k + 1, ls] * pltpu.roll(m, 256 - k, axis=0)
            dxy[0, :, ls] = dx.astype(BF)
        S.send_u(9)
        lw0.wait()
        rf = Reduce(cm, dnp, f1, f2, f3)
        for c in range(4):
            cs = slice(c * 640, c * 640 + 640)
            dnp[c] = (dna[c] + dot(dxy[0], wbuf[0, :, cs])).astype(BF).reshape(4, 64, 640)
            rf.send(c)
            if c: rf.mid(c - 1)
        rf.mid(3)
        at("C5")
        r1 = rb[own, 0:1]
        acc = jnp.zeros((64, 1), F32)
        for c in range(4):
            dn = rf.fin(c)
            xr = tk[c].astype(F32)
            gs[c, 0:1, :] = jnp.sum(dn * xr * r1, axis=0, keepdims=True)
            v = dn * gnb[c, 0:1, :]
            dna[c, 0:64, :] = v
            acc = acc + jnp.sum(v * xr, axis=-1, keepdims=True)
        acc = acc * (1.0 / 2560) * (r1 * r1 * r1)
        for c in range(4):
            dob[c] = (dh1[:, c * 640:c * 640 + 640] + r1 * dna[c, 0:64, :] - tk[c].astype(F32) * acc).astype(BF)
        sdt = Swap(cm, dob, dto)
        gcp = []
        for d in (3, 2, 1):
            _, t = fpeer(d)
            gcp.append(cm.remote(gs.at[t], gr.at[d - 1], ("f", d)))
        sbo.finish()
        outs = [cm.local(bob, bo_o)]
        at("C6")
        arrived(g1)
        t = sg[:, :, :, pl.ds(pl.multiple_of(z * 16, 16), 16), :].astype(F32)
        sgt[...] = ((t + sgr[0].astype(F32)) + (sgr[1].astype(F32) + sgr[2].astype(F32))).astype(BF)
        small["g2"] = spread(cm, lambda d: sgt.at[(x + d) % 4], sgr2, "x")
        arrived(gcp)
        sm[0:2, :] = (gs[f, 0:2, :] + gr[0, 0:2, :]) + (gr[1, 0:2, :] + gr[2, 0:2, :])
        sm[10:16, :] = jnp.zeros((6, 640), F32)
        sma[0] = sm[...]
        small["v1"] = spread(cm, lambda d: sma.at[0], smr.at[0], "x")
        sdt.finish()
        dxx[...] = dto[...].astype(F32).reshape(256, 640)
        outs.append(cm.local(dxx, dtok_o))
        at("E")
        for c in outs:
            c.wait()
        cm.drain()

    pl.run_scoped(chain_phase, pltpu.VMEM((4, 5, 256, 128), BF), w, w, w, w, w, pltpu.VMEM((5, 256, 128), F32), pltpu.VMEM((5, 256, 512), BF), pltpu.VMEM((2, 640, 2560), BF),
                  w, w, w, w, pltpu.VMEM((5, 256, 256), BF), pltpu.VMEM((4, 256, 640), F32),
                  pltpu.VMEM((3, 4, 160, 1024), BF), pltpu.VMEM((2, 4, 256, 640), BF), pltpu.VMEM((4, 4, 160, 640), BF), pltpu.VMEM((2, 3, 160, 640), BF), pltpu.VMEM((12, 2, 80, 640), BF),
                  pltpu.VMEM((4, 64, 640), BF), pltpu.VMEM((4, 64, 640), BF), pltpu.VMEM((4, 2, 5, 64, 128), BF), pltpu.VMEM((2, 256, 640), BF), w,
                  pltpu.VMEM((5, 4, 256, 128), BF), pltpu.VMEM((4, 4, 64, 640), BF), pltpu.VMEM((64, 2560), F32))

def tail(par, n2, dt, w_in, w_dn, n1t, dtt, pf, pu, z, cv, xb, yb, gx, ga, hs, msk, r, g, wg, tk, h1, w_t, wo, plan=PLAN):
    s = jax.ShapeDtypeStruct
    R = 256
    V = pltpu.VMEM
    out_shape = [s((4, 64, 640), BF), s((R, 640), F32), s((2, 80, 1920), F32), s((80, 1920), F32), s((2, 640, 80), F32), s((640, 80), F32),
                 s((2, 5, 8, 128), F32), s((16, 640), F32), s((11, 3, R, 640), BF), s((12, 3, 160, 640), BF), s((2, 3, 4, 160, 256), BF)]
    blk = V((4, 4, 64, 640), BF)
    row = V((4, 64, 640), BF)
    red = [V((4, 2, 64, 640), BF), row, row]
    red5 = [V((5, 2, R, 128), BF), V((5, R, 128), BF), V((5, R, 128), BF)]
    scratch = [V((3, R, 640), BF), V((3, R, 1280), BF), V((12, 2, 80, 640), BF), V((12, 80, 640), BF), V((4, 4, 160, 256), BF), V((4, 64, 2560), BF), blk, blk, row, row,
               V((4, 8, 640), F32), V((3, 8, 640), F32), V((16, 640), F32),
               V((3, 4, 2, 5, 16, 128), BF), V((4, 2, 5, 16, 128), BF), V((3, 2, 5, 16, 128), BF), V((2, 2, 5, 16, 128), F32),
               V((3, 16, 640), F32), V((2, 3, 16, 640), F32), V((16, 640), F32)] + red + red + red5 + red + [
               V((4, 8, 640), F32), V((320, 128), F32), V((64, 2560), F32), V((64, 2560), BF), V((4, 64, 640), BF),
               pltpu.SemaphoreType.DMA((224,)), pltpu.SemaphoreType.DMA((224,)), pltpu.SemaphoreType.DMA((128,))]
    return pl.pallas_call(
        functools.partial(tail_kernel, plan), out_shape=out_shape,
        in_specs=[VMEM] + [ANY] * 23,
        out_specs=[ANY] * 2 + [VMEM] * 6 + [ANY] * 3,
        scratch_shapes=scratch,
        compiler_params=pltpu.CompilerParams(collective_id=5, has_side_effects=True, vmem_limit_bytes=VM),
        name="tail",
    )(par, n2, dt, w_in, w_dn, n1t, dtt, pf, pu, z, cv, xb, yb, gx, ga, hs, msk, r, g, wg, tk, h1, w_t, wo)

def body_of(plan, tokens, seq_len, seq_owner, gain_1, gain_2, w_xy, conv_w, conv_b, gate_w, gate_b, a_param, w_out, w_in, w_down, cotangent):
    small, w_t, gw_t, wo = prep(seq_len, seq_owner, gain_1, gain_2, w_xy, conv_w, conv_b, gate_w, gate_b, a_param, w_out)
    (n1, cv, xb, yb, gx, ga, hs, z, n2, dt, h1, msk, r, g, wg, tk, n1t, dtt, pf, pu, par) = forward(*small, tokens, cotangent, w_t, gw_t, wo)
    sums = tail(par, n2.reshape(256, 2560), dt, w_in, w_down, n1t, dtt, pf, pu, z, cv, xb, yb, gx, ga, hs, msk, r, g, wg, tk, h1, w_t, wo, plan)[:8]
    bo, dtok, d_in, d_dn, d_xy, d_wo, gate, g1, g2, cw, cb, gb, da = finish(*sums)
    return (bo.reshape(256, 640), dtok, g1, g2, jnp.transpose(d_xy.reshape(2, 10, 64, 80), (0, 3, 1, 2)), jnp.transpose(cw, (1, 0, 2)), cb,
            gate, jnp.transpose(gb, (1, 0, 2)), da, d_wo.reshape(10, 64, 80), d_in, d_dn.T)

def body(*args):
    return body_of(PLAN, *args)


def solution(mesh):
    return jax.shard_map(
        body,
        mesh=mesh,
        in_specs=(
            P("rep", "fsdp"), P(), P(), P("fsdp"), P("fsdp"), P(None, None, None, "fsdp"), P(None, None, "fsdp"), P(None, "fsdp"),
            P(None, None, None, "fsdp"), P(None, None, "fsdp"), P(None, "fsdp"), P(None, "fsdp", None), P(None, None, "fsdp"), P("fsdp", None), P("rep", "fsdp"),
        ),
        out_specs=(
            P("rep", "fsdp"), P("rep", "fsdp"), P("fsdp"), P("fsdp"), P(None, "rep", None, "fsdp"), P(None, None, "fsdp"), P(None, "fsdp"),
            P(None, None, "rep", "fsdp"), P(None, None, "fsdp"), P(None, "fsdp"), P(None, "fsdp", "rep"), P(None, "rep", "fsdp"), P("fsdp", "rep"),
        ),
        check_vma=False,
    )
```

```python
import functools

import jax
import jax.numpy as jnp
from jax import lax
from jax.experimental import pallas as pl
from jax.experimental.pallas import tpu as pltpu
from jax.sharding import PartitionSpec as P

MESH = pl.DeviceIdType.MESH
VM = 63 * 2**20
GC = 0.7978845608028654

def gelu_parts(v):
    v2 = v * v
    t = jnp.tanh(GC * v * (1.0 + 0.044715 * v2))
    half = 0.5 * (1.0 + t)
    g = v * half
    dg = half + 0.5 * v * (1.0 - t * t) * (GC * (1.0 + 3 * 0.044715 * v2))
    return g, dg

def dot(a, b):
    return jnp.dot(a, b, preferred_element_type=jnp.float32)

def dot_nt(a, b):
    return lax.dot_general(a, b, (((1,), (1,)), ((), ())), preferred_element_type=jnp.float32)

def ffn_kernel(n2, dt, w_in, w_dn, hid, dg, du, mlp, dn2, n2t, dtt, am, ad):
    i = pl.program_id(0)
    @pl.when(i == 1)
    def _():
        for c in range(4):
            n2t[c] = n2[:, c * 640:c * 640 + 640].T.reshape(4, 160, 256)
            dtt[c] = dt[:, c * 640:c * 640 + 640].T.reshape(4, 160, 256)
    @pl.when(i == 0)
    def _():
        am[...] = jnp.zeros_like(am)
        ad[...] = jnp.zeros_like(ad)
    gate = dot(n2[...], w_in[0])
    up = dot(n2[...], w_in[1])
    g, dgl = gelu_parts(gate)
    h = (g * up).astype(jnp.bfloat16)
    hid[0] = h
    dh = dot_nt(dt[...], w_dn[...])
    a = (dh * up * dgl).astype(jnp.bfloat16)
    b = (dh * g).astype(jnp.bfloat16)
    dg[0] = a
    du[0] = b
    am[...] += dot(h, w_dn[...])
    ad[...] += dot_nt(a, w_in[0])
    ad[...] += dot_nt(b, w_in[1])
    @pl.when(i == 2)
    def _():
        for c in range(4):
            mlp[c] = am[:, c * 640:c * 640 + 640].astype(jnp.bfloat16).reshape(4, 64, 640)
            dn2[c] = ad[:, c * 640:c * 640 + 640].astype(jnp.bfloat16).reshape(4, 64, 640)

def ffn(n2, dt, w_in, w_dn):
    R, D = n2.shape
    T = 640
    nt = w_dn.shape[0] // T
    full = pl.BlockSpec((R, D), lambda i: (0, 0))
    tile = pl.BlockSpec((1, R, T), lambda i: (i, 0, 0))
    ch = jax.ShapeDtypeStruct((nt, R, T), jnp.bfloat16)
    rd = jax.ShapeDtypeStruct((4, 4, 64, 640), jnp.bfloat16)
    td = jax.ShapeDtypeStruct((4, 4, 160, 256), jnp.bfloat16)
    part = pl.BlockSpec((4, 4, 64, 640), lambda i: (0, 0, 0, 0))
    turned = pl.BlockSpec((4, 4, 160, 256), lambda i: (0, 0, 0, 0))
    return pl.pallas_call(
        ffn_kernel, grid=(nt,),
        in_specs=[full, full, pl.BlockSpec((2, D, T), lambda i: (0, 0, i)), pl.BlockSpec((T, D), lambda i: (i, 0))],
        out_specs=[tile, tile, tile, part, part, turned, turned],
        out_shape=[ch, ch, ch, rd, rd, td, td],
        scratch_shapes=[pltpu.VMEM((R, D), jnp.float32)] * 2,
        compiler_params=pltpu.CompilerParams(vmem_limit_bytes=VM),
        name="ffn",
    )(n2, dt, w_in, w_dn)

def coords():
    r = lax.axis_index("rep")
    f = lax.axis_index("fsdp")
    return r // 8, (r // 2) % 4, r % 2, f

def peer(axis, d):
    x, z, y, f = coords()
    if axis == "x":
        x = (x + d) % 4
    elif axis == "z":
        z = (z + d) % 4
    elif axis == "y":
        y = 1 - y
    else:
        f = (f + d) % 4
    return ((x * 4 + z) * 2 + y, f)

class Grads:
    def __init__(self, plan, fplan):
        self.plan = plan
        self.fplan = fplan
    def scratch(self):
        n, m = len(self.plan), len(self.fplan)
        b = jnp.bfloat16
        return [
            pltpu.VMEM((n, 4, 256, 640), b),
            pltpu.VMEM((m, 4, 160, 1024), b),
            pltpu.VMEM((n, 4, 160, 640), b),
            pltpu.VMEM((n, 3, 160, 640), b),
            pltpu.VMEM((n, 2, 80, 640), b),
            pltpu.VMEM((n, 80, 640), b),
            pltpu.SemaphoreType.DMA((n, 3)), pltpu.SemaphoreType.DMA((n, 3)),
            pltpu.SemaphoreType.DMA((m, 3)), pltpu.SemaphoreType.DMA((m, 3)),
            pltpu.SemaphoreType.DMA((n, 3)), pltpu.SemaphoreType.DMA((n, 3)),
            pltpu.SemaphoreType.DMA((n,)), pltpu.SemaphoreType.DMA((n,)),
            pltpu.SemaphoreType.DMA((n,)), pltpu.SemaphoreType.DMA((m,)),
        ]
    def bind(self, refs, usrc, fsrc, out):
        (self.ub, self.ft, self.st, self.rr, self.tt, self.yr, self.us, self.ur, self.fs, self.fr,
         self.rq, self.rv, self.ys, self.yv, self.lu, self.lf) = refs
        self.usrc, self.fsrc, self.out = usrc, fsrc, out
    def rc(self, src, dst, s, r, axis, d):
        return pltpu.make_async_remote_copy(src_ref=src, dst_ref=dst, send_sem=s, recv_sem=r, device_id=peer(axis, d), device_id_type=MESH)
    def fcopies(self, k):
        i, axis = self.fplan[k]
        x, z, y, f = coords()
        src = self.fsrc[i]
        me = x if axis == "x" else z
        pick = (lambda t: src.at[t]) if axis == "x" else (lambda t: src.at[:, t])
        loc = pltpu.make_async_copy(pick(me), self.ft.at[k, :, :, pl.ds(0, 256)], self.lf.at[k])
        rem = [self.rc(pick((me + d) % 4), self.ft.at[k, :, :, pl.ds(d * 256, 256)], self.fs.at[k, d - 1], self.fr.at[k, d - 1], axis, d) for d in (1, 3, 2)]
        return loc, rem
    def ucopies(self, c):
        k, axis = self.plan[c]
        src = self.usrc(c)
        loc = pltpu.make_async_copy(src, self.ub.at[c, 0], self.lu.at[c])
        rem = [self.rc(src, self.ub.at[c, d], self.us.at[c, d - 1], self.ur.at[c, d - 1], axis, d) for d in (1, 3, 2)]
        return loc, rem
    def rscopies(self, c):
        k, axis = self.plan[c]
        ra = "z" if axis == "x" else "x"
        x, z, y, f = coords()
        me = z if axis == "x" else x
        return me, [self.rc(self.st.at[c, (me + d) % 4], self.rr.at[c, d - 1], self.rq.at[c, d - 1], self.rv.at[c, d - 1], ra, d) for d in (1, 3, 2)]
    def ycopy(self, c):
        x, z, y, f = coords()
        return self.rc(self.tt.at[c, 1 - y], self.yr.at[c], self.ys.at[c], self.yv.at[c], "y", 0)
    def send_f(self, k):
        loc, rem = self.fcopies(k)
        loc.start()
        for r in rem: r.start()
    def send_u(self, c):
        loc, rem = self.ucopies(c)
        loc.start()
        for r in rem: r.start()
    def mm(self, c):
        k, axis = self.plan[c]
        loc, rem = self.ucopies(c)
        loc.wait()
        for r in rem: r.wait()
        if not self.fdone[k]:
            loc, rem = self.fcopies(k)
            loc.wait()
            for r in rem: r.wait()
            self.fdone[k] = True
        self.st[c] = dot(self.ft[k].reshape(640, 1024), self.ub[c].reshape(1024, 640)).astype(jnp.bfloat16).reshape(4, 160, 640)
        me, cps = self.rscopies(c)
        for r in cps: r.start()
    def rs(self, c):
        me, cps = self.rscopies(c)
        for r in cps: r.wait()
        f = jnp.float32
        t = (self.st[c, me].astype(f) + self.rr[c, 0].astype(f)) + (self.rr[c, 1].astype(f) + self.rr[c, 2].astype(f))
        self.tt[c] = t.astype(jnp.bfloat16).reshape(2, 80, 640)
        self.ycopy(c).start()
    def fin(self, c):
        x, z, y, f = coords()
        self.ycopy(c).wait()
        self.out[c] = self.tt[c, y].astype(jnp.float32) + self.yr[c].astype(jnp.float32)

def entry_barrier(peers):
    b = pltpu.get_barrier_semaphore()
    for axis, d in peers:
        pl.semaphore_signal(b, inc=1, device_id=peer(axis, d), device_id_type=MESH)
    pl.semaphore_wait(b, len(peers))

REP = [("x", 1), ("x", 2), ("x", 3), ("z", 1), ("z", 2), ("z", 3), ("y", 1)]

PLAN = [(0, "x")] * 6 + [(1, "z")] * 3 + [(2, "x"), (3, "z"), (4, "z")]
FPLAN = [(0, "x"), (1, "z"), (2, "x"), (2, "z"), (3, "z")]

def grads_kernel(g, n2t, dtt, n1t, drt, dgs, dus, hids, dxs, zs, out, *refs):
    def usrc(c):
        if c < 3: return dgs.at[c]
        if c < 6: return dus.at[c - 3]
        if c < 9: return hids.at[c - 6]
        if c < 11: return dxs.at[c - 9]
        return zs
    g.bind(refs, usrc, [n2t, dtt, n1t, drt], out)
    g.fdone = [False] * len(g.fplan)
    entry_barrier(REP)
    g.send_f(0); g.send_f(1)
    order = [0, 6, 1, 3, 7, 2, 4, 8, 5, 9, 10, 11]
    for j, c in enumerate(order):
        if j == 6:
            for k in (2, 3, 4): g.send_f(k)
        g.send_u(c)
    n = len(order)
    for j in range(n + 4):
        if j < n: g.mm(order[j])
        if 0 <= j - 2 < n: g.rs(order[j - 2])
        if 0 <= j - 4 < n: g.fin(order[j - 4])

def grads(n2t, dtt, n1t, drt, dgs, dus, hids, dxs, zs):
    g = Grads(PLAN, FPLAN)
    return pl.pallas_call(
        functools.partial(grads_kernel, g),
        out_shape=jax.ShapeDtypeStruct((12, 80, 640), jnp.float32),
        in_specs=[pl.BlockSpec(memory_space=pl.ANY)] * 9,
        out_specs=pl.BlockSpec(memory_space=pltpu.VMEM),
        scratch_shapes=g.scratch(),
        compiler_params=pltpu.CompilerParams(collective_id=7, has_side_effects=True, vmem_limit_bytes=VM),
        name="grads",
    )(n2t, dtt, n1t, drt, dgs, dus, hids, dxs, zs)

F32 = jnp.float32
BF = jnp.bfloat16
EPS = 1e-06
ANY = pl.BlockSpec(memory_space=pl.ANY)
VMEM = pl.BlockSpec(memory_space=pltpu.VMEM)

def fpeer(d):
    r = lax.axis_index("rep")
    f = lax.axis_index("fsdp")
    h, c = f // 2, f % 2
    if d % 2:
        c = 1 - c
    if d // 2:
        h = 1 - h
    return r, h * 2 + c

def device(to):
    axis, d = to
    return fpeer(d) if axis == "f" else peer(axis, d)

class Sent:
    def __init__(self, src, dst, to, ssem, rsem):
        self.src, self.dst, self.to, self.ssem, self.rsem = src, dst, to, ssem, rsem
    def make(self):
        return pltpu.make_async_remote_copy(
            src_ref=self.src(), dst_ref=self.dst(), send_sem=self.ssem(), recv_sem=self.rsem(), device_id=device(self.to), device_id_type=MESH)
    def wait_recv(self):
        self.make().wait_recv()
    def wait_send(self):
        self.make().wait_send()

class Comm:
    def __init__(self, ssem, rsem, lsem):
        self.ssem, self.rsem, self.lsem = ssem, rsem, lsem
        self.n = self.m = 0
        self.open = []
    def remote(self, src, dst, to):
        k = self.n
        self.n += 1
        c = Sent(src if callable(src) else lambda: src, dst if callable(dst) else lambda: dst, to, lambda: self.ssem.at[k], lambda: self.rsem.at[k])
        c.make().start()
        self.open.append(c)
        return c
    def local(self, src, dst):
        k = self.m
        self.m += 1
        c = pltpu.make_async_copy(src, dst, self.lsem.at[k])
        c.start()
        return c
    def sent(self, c):
        c.wait_send()
        self.open = [o for o in self.open if o is not c]
    def drain(self):
        for c in self.open:
            c.wait_send()
        self.open = []

class Gather:
    def __init__(self, comm, buf, own=None, parts=None):
        self.comm, self.buf = comm, buf
        self.f = lax.axis_index("fsdp")
        self.parts = parts or [()]
        self.own = own
        self.far, self.near, self.late = {}, {}, {}
    def start(self, which=None):
        f, cm = self.f, self.comm
        for i in range(len(self.parts)) if which is None else (which,):
            p = self.parts[i]
            dst = self.buf.at[(f, *p)]
            src = self.own.at[p] if self.own is not None else dst
            self.far[i] = cm.remote(src, dst, ("f", 2))
            self.near[i] = cm.remote(src, dst, ("f", 1))
    def relay(self, which=None):
        _, o = fpeer(2)
        for i in range(len(self.parts)) if which is None else (which,):
            self.far[i].wait_recv()
            dst = self.buf.at[(o, *self.parts[i])]
            self.late[i] = self.comm.remote(dst, dst, ("f", 1))
    def finish(self, which=None):
        for i in range(len(self.parts)) if which is None else (which,):
            self.near[i].wait_recv()
            self.late[i].wait_recv()

class Reduce:
    def __init__(self, comm, part, r1, s2, r2):
        self.comm, self.part, self.r1, self.s2, self.r2 = comm, part, r1, s2, r2
        self.f = lax.axis_index("fsdp")
        self.a, self.b, self.c = {}, {}, {}
    def send(self, c):
        self.a[c] = self.comm.remote(lambda: self.part.at[c, fpeer(3)[1]], lambda: self.r1.at[c, 1], ("f", 1))
        self.b[c] = self.comm.remote(lambda: self.part.at[c, fpeer(1)[1]], lambda: self.r1.at[c, 0], ("f", 1))
    def mid(self, c):
        _, o2 = fpeer(2)
        self.a[c].wait_recv()
        self.s2[c] = (self.part[c, o2].astype(F32) + self.r1[c, 1].astype(F32)).astype(BF)
        self.c[c] = self.comm.remote(lambda: self.s2.at[c], lambda: self.r2.at[c], ("f", 2))
    def fin(self, c):
        self.b[c].wait_recv()
        self.c[c].wait_recv()
        return self.part[c, self.f].astype(F32) + self.r1[c, 0].astype(F32) + self.r2[c].astype(F32)

def group_barrier(ds):
    b = pltpu.get_barrier_semaphore()
    for d in ds:
        pl.semaphore_signal(b, inc=1, device_id=fpeer(d), device_id_type=MESH)
    pl.semaphore_wait(b, len(ds))

def lanes(q):
    return slice(q * 128, q * 128 + 128)

def row_masks(lenr, ownr, msk):
    me = lax.axis_index("rep")
    j = lax.broadcasted_iota(jnp.int32, (128, 128), 0)
    i = lax.broadcasted_iota(jnp.int32, (128, 128), 1)
    counted = jnp.where(ownr[...] == me, lenr[...], 0)
    mine = jnp.sum(jnp.where(i == j, counted, 0), axis=1, keepdims=True)
    offset = jnp.sum(jnp.where(j < i, mine, 0), axis=0, keepdims=True)
    total = jnp.sum(mine, axis=0, keepdims=True)
    place = lax.broadcasted_iota(jnp.int32, (256, 128), 0)
    hit = jnp.where((ownr[...] == me) & (offset == place), 1.0, 0.0)
    start = jnp.broadcast_to(jnp.max(hit, axis=1, keepdims=True), (256, 128))
    msk[0] = start
    run = start
    for k in (1, 2, 3):
        msk[k] = jnp.where((run == 0.0) & (place >= k), 1.0, 0.0)
        run = jnp.maximum(run, jnp.where(place >= k, pltpu.roll(start, k, axis=0), 0.0))
    msk[4] = jnp.where(place < total, 1.0, 0.0)

def wide_gates(gw, wg):
    row = lax.broadcasted_iota(jnp.int32, (128, 128), 0) // 64
    col = lax.broadcasted_iota(jnp.int32, (128, 128), 1) // 64
    for q in range(5):
        for k in range(2):
            for g in range(2):
                v = gw[k, q * 128:q * 128 + 128, g * 128:g * 128 + 128].astype(F32)
                r = pltpu.roll(v, 64, axis=1)
                for e in range(2):
                    twice = jnp.where(col == e, v, r)
                    p = 2 * g + e
                    wg[q, k * 128:k * 128 + 128, p * 128:p * 128 + 128] = jnp.where(row == col, twice, 0.0).astype(BF)

def softplus(v):
    return jnp.maximum(v, 0.0) + jnp.log1p(jnp.exp(-jnp.abs(v)))

def sigmoid(v):
    return 1.0 / (1.0 + jnp.exp(-v))

def scan_rows(a_ref, u_ref, h_ref, back):
    rows = lax.broadcasted_iota(jnp.int32, (8, 640), 0)
    carry = jnp.zeros((1, 640), F32)
    order = range(31, -1, -1) if back else range(32)
    for i in order:
        a = a_ref[i * 8:i * 8 + 8, :]
        u = u_ref[i * 8:i * 8 + 8, :]
        for s in (1, 2, 4):
            if back:
                ok = rows < 8 - s
                a2 = jnp.where(ok, pltpu.roll(a, 8 - s, axis=0), 1.0)
                u2 = jnp.where(ok, pltpu.roll(u, 8 - s, axis=0), 0.0)
            else:
                ok = rows >= s
                a2 = jnp.where(ok, pltpu.roll(a, s, axis=0), 1.0)
                u2 = jnp.where(ok, pltpu.roll(u, s, axis=0), 0.0)
            u = u + a * u2
            a = a * a2
        h = u + a * carry
        h_ref[i * 8:i * 8 + 8, :] = h
        carry = h[0:1, :] if back else h[7:8, :]

def gate_values(q, pre, par, start):
    gx = sigmoid(pre[:, 0:128] + par[5:6, lanes(q)])
    ga = sigmoid(pre[:, 128:256] + par[6:7, lanes(q)])
    return gx, ga

def decay_of(q, ga, par, start):
    sp = softplus(par[7:8, lanes(q)])
    a = jnp.exp(-8.0 * ga * sp)
    spread = 1.0 - a * a
    mult = jnp.where(start == 1.0, 1.0, jnp.sqrt(jnp.maximum(spread, 0.01)))
    return sp, a, spread, mult

def prep(seq_len, seq_owner, gain_1, gain_2, w_xy, conv_w, conv_b, gate_w, gate_b, a_param, w_out):
    small = (seq_len.reshape(1, 128), seq_owner.reshape(1, 128), gain_1, gain_2,
             jnp.transpose(conv_w, (1, 0, 2)), conv_b, jnp.transpose(gate_b, (1, 0, 2)), a_param)
    w_t = jnp.transpose(w_xy, (0, 2, 3, 1)).reshape(2, 640, 2560)
    gw_t = jnp.swapaxes(gate_w, 2, 3).reshape(2, 640, 256)
    return small, w_t, gw_t, w_out.reshape(640, 2560)

def dot_tn(a, b):
    return lax.dot_general(a, b, (((0,), (0,)), ((), ())), preferred_element_type=jnp.float32)

class Swap:
    def __init__(self, comm, src, dst):
        f = lax.axis_index("fsdp")
        self.cps = []
        for d in (3, 2, 1):
            _, t = fpeer(d)
            self.cps.append(comm.remote(src.at[t], dst.at[f], ("f", d)))
        self.own = comm.local(src.at[f], dst.at[f])
    def finish(self):
        self.own.wait()
        for c in self.cps:
            c.wait_recv()

def spread(cm, src, dst, axis):
    return [cm.remote(src(d), dst.at[d - 1], (axis, d)) for d in (1, 3, 2)]

def arrived(cps):
    for c in cps:
        c.wait_recv()

CHUNK_FEATURES = [0] * 6 + [1] * 3 + [2, 3, 4]
FEATURE_AXIS = ["x", "z", "x", "z", "x"]
FEATURE_SLOT = [0, 1, 0, 1, 2]

class Sums:
    def __init__(self, cm, uland, fland, rrh, yr, usrc, fsrc, out):
        self.cm, self.uland, self.fland, self.rrh, self.yr = cm, uland, fland, rrh, yr
        self.usrc, self.fsrc, self.out = usrc, fsrc, out
        self.x, self.z, self.y, f = coords()
        self.core = f % 2
        self.u, self.u2, self.f, self.f2, self.r, self.yc = {}, {}, {}, {}, {}, {}
        self.nw = self.nst = self.nr = self.ntt = 0
        self.win, self.stc, self.rwin, self.ttc = {}, {}, {}, {}
        self.loaded = {}
        self.h, self.place = {}, {}
    def work(self, ft, uw, st, rw, tt, hb):
        self.ft, self.uw, self.st, self.rw, self.tt, self.hb = ft, uw, st, rw, tt, hb
    def axis(self, c):
        return FEATURE_AXIS[CHUNK_FEATURES[c]]
    def pos(self, axis):
        return self.x if axis == "x" else self.z
    def send_f(self, k):
        axis = FEATURE_AXIS[k]
        me = self.pos(axis)
        def one(d):
            def src():
                t, h = (me + d) % 4, pl.ds(2 * self.core, 2)
                return self.fsrc[k].at[t, h] if axis == "x" else self.fsrc[k].at[h, t]
            return self.cm.remote(src, lambda: self.fland[k].at[d - 1, pl.ds(2 * self.core, 2)], (axis, d))
        self.f[k] = {d: one(d) for d in (1, 3, 2)}
    def relay_f(self, k):
        def one(d):
            self.f[k][d].wait_recv()
            half = lambda: self.fland[k].at[d - 1, pl.ds(2 * self.core, 2)]
            return self.cm.remote(half, half, ("f", 1))
        self.f2[k] = [one(d) for d in (1, 3, 2)]
    def send_u(self, c, direct=False):
        def one(d):
            return self.cm.remote(lambda: self.usrc[c], lambda: self.uland[c].at[d - 1], (self.axis(c), d))
        self.u[c] = {d: one(d) for d in ((1, 3, 2) if direct else (1, 3))}
        if direct:
            self.u2[c] = list(self.u[c].values())
    def relay_u(self, c):
        low, high = pl.ds(0, 128), pl.ds(128, 128)
        self.u[c][1].wait_recv()
        a = self.cm.remote(lambda: self.uland[c].at[0, low], lambda: self.uland[c].at[1, low], (self.axis(c), 1))
        self.u[c][3].wait_recv()
        b = self.cm.remote(lambda: self.uland[c].at[2, high], lambda: self.uland[c].at[1, high], (self.axis(c), 3))
        self.u2[c] = [a, b]
    def load_f(self, k):
        s = FEATURE_SLOT[k]
        axis = FEATURE_AXIS[k]
        me = self.pos(axis)
        own = self.fsrc[k].at[me] if axis == "x" else self.fsrc[k].at[:, me]
        cps = [self.cm.local(own, self.ft.at[s, :, :, pl.ds(0, 256)])]
        arrived(self.f2.get(k, []))
        for d in (1, 2, 3):
            cps.append(self.cm.local(self.fland[k].at[d - 1], self.ft.at[s, :, :, pl.ds(d * 256, 256)]))
        self.loaded[k] = cps
    def prep(self, c):
        k = CHUNK_FEATURES[c]
        if k not in self.loaded:
            self.load_f(k)
        w = self.nw % 2
        self.nw += 1
        cps = [self.cm.local(self.usrc[c], self.uw.at[w, 0])]
        arrived(self.u2.get(c, []))
        cps.append(self.cm.local(self.uland[c], self.uw.at[w, pl.ds(1, 3)]))
        self.win[c] = (w, cps)
    def mm(self, c, direct=False):
        k = CHUNK_FEATURES[c]
        for l in self.loaded[k]:
            l.wait()
        self.loaded[k] = []
        w, cps = self.win[c]
        for l in cps:
            l.wait()
        i = self.nst % 4
        self.nst += 1
        for old in self.stc.get(i, []):
            self.cm.sent(old)
        s = self.st
        for h in (0, 2):
            v = dot(self.ft[FEATURE_SLOT[k], h:h + 2].reshape(320, 1024), self.uw[w].reshape(1024, 640))
            s[i, h:h + 2] = v.astype(BF).reshape(2, 160, 640)
        axis = "z" if self.axis(c) == "x" else "x"
        me = self.pos(axis)
        far = (me + 2) % 4
        if direct:
            cps = [self.cm.remote(s.at[i, (me + d) % 4], self.rrh.at[c, d - 1], (axis, d)) for d in (1, 3, 2)]
            self.stc[i] = cps
        else:
            self.h[c] = [self.cm.remote(s.at[i, far, pl.ds(0, 80)], self.hb.at[c, 0], (axis, 1)), self.cm.remote(s.at[i, far, pl.ds(80, 80)], self.hb.at[c, 1], (axis, 3))]
            self.stc[i] = list(self.h[c])
        t = self.ntt % 12
        self.ntt += 1
        for old in self.ttc.get(t, []):
            self.cm.sent(old)
        self.tt[t] = s[i, me].reshape(2, 80, 640)
        self.place[c] = (i, t)
        if direct:
            self.r[c] = (t, cps)
    def wsum(self, c):
        i, t = self.place[c]
        s = self.st
        axis = "z" if self.axis(c) == "x" else "x"
        me = self.pos(axis)
        up, down = (me + 1) % 4, (me + 3) % 4
        self.h[c][0].wait_recv()
        s[i, up, 0:80] = (s[i, up, 0:80].astype(F32) + self.hb[c, 0].astype(F32)).astype(BF)
        a = self.cm.remote(s.at[i, up], self.rrh.at[c, 0], (axis, 1))
        self.h[c][1].wait_recv()
        s[i, down, 80:160] = (s[i, down, 80:160].astype(F32) + self.hb[c, 1].astype(F32)).astype(BF)
        b = self.cm.remote(s.at[i, down], self.rrh.at[c, 2], (axis, 3))
        self.stc[i] += [a, b]
        self.r[c] = (t, [a, b])
    def rprep(self, c):
        t, cps = self.r[c]
        arrived(cps)
        w = self.nr % 2
        self.nr += 1
        slots = (0, 1, 2) if len(cps) == 3 else (0, 2)
        self.rwin[c] = (w, [self.cm.local(self.rrh.at[c, j], self.rw.at[w, j]) for j in slots])
    def rsum(self, c):
        t, _ = self.r[c]
        w, ls = self.rwin[c]
        for l in ls:
            l.wait()
        total = self.tt[t].reshape(160, 640).astype(F32) + (self.rw[w, 0].astype(F32) + self.rw[w, 2].astype(F32))
        if len(ls) == 3:
            total = total + self.rw[w, 1].astype(F32)
        self.tt[t] = total.astype(BF).reshape(2, 80, 640)
        cp = self.cm.remote(self.tt.at[t, 1 - self.y], self.yr.at[c], ("y", 1))
        self.ttc[t] = [cp]
        self.yc[c] = cp
    def fin(self, c):
        self.yc[c].wait_recv()
        t, _ = self.r[c]
        self.out(c, self.tt[t, self.y].astype(F32) + self.yr[c].astype(F32))

def forward_kernel(lenr, ownr, g1r, g2r, cwt, cbt, gbt, apt, tok, cot, w_t, gw_h, wo_h,
                   n1_o, cv_o, xb_o, yb_o, gx_o, ga_o, hs_o, z_o, n2_o, dt_o, h1_o, msk_o, r_o, g_o, wg_o, tk_o, n1t_o, dtt_o, pf, pu, par_o,
                   tkb, ctb, gnb, wv, gw, wo, wg, n1, dt, cvb, xb, yb, gx, ga, aa, uu, hs, z, msk, pt, r1, s2, r2, h1, n2b, rs1, rs2, n1t, dtt, par, gn,
                   ssem, rsem, lsem):
    cm = Comm(ssem, rsem, lsem)
    f = lax.axis_index("fsdp")
    lw = [cm.local(w_t.at[0], wv.at[0]), cm.local(gw_h, gw), cm.local(w_t.at[1], wv.at[1]), cm.local(wo_h, wo)]
    lt = [cm.local(tok, tkb.at[f]), cm.local(cot, ctb.at[f])]
    gn[0, :] = g1r[...].astype(F32)
    gn[1, :] = g2r[...].astype(F32)
    lt.append(cm.local(gn, gnb.at[f]))
    b = pltpu.get_barrier_semaphore()
    for axis, d in REP[:6]:
        pl.semaphore_signal(b, inc=1, device_id=peer(axis, d), device_id_type=MESH)
    for d in (1, 2):
        pl.semaphore_signal(b, inc=1, device_id=fpeer(d), device_id_type=MESH)
    pl.semaphore_wait(b, 8)
    S = Sums(cm, [None] * 11 + [pu], [None, pf.at[0], pf.at[1], pf.at[2]], None, None, [None] * 11 + [z], [None, dtt, n1t, n1t], None)
    gtk = Gather(cm, tkb, tok, [(pl.ds(i * 64, 64),) for i in range(4)])
    ggn = Gather(cm, gnb, gn)
    gct = Gather(cm, ctb, cot)
    ggn.start()
    gtk.start()
    for h in range(10):
        ls = slice(h * 64, h * 64 + 64)
        par[0:4, ls] = cwt[h].astype(F32)
        par[4:5, ls] = cbt[h:h + 1].astype(F32)
        par[5:7, ls] = gbt[h].astype(F32)
        par[7:8, ls] = apt[h:h + 1]
    row_masks(lenr, ownr, msk)
    lw[1].wait()
    wide_gates(gw, wg)
    outs = [cm.local(msk, msk_o), cm.local(wg, wg_o), cm.local(par, par_o)]
    ggn.relay()
    for c in lt:
        c.wait()
    ggn.finish()
    gtk.relay(0)
    gtk.relay(1)
    for j in range(4):
        gtk.finish(j)
        @pl.loop(j * 4, j * 4 + 4)
        def _(i):
            rows = pl.ds(pl.multiple_of(i * 16, 16), 16)
            xs = [tkb[p, rows, :].astype(F32) for p in range(4)]
            ss = sum(jnp.sum(x * x, axis=-1, keepdims=True) for x in xs)
            r = lax.rsqrt(ss * (1.0 / 2560) + EPS)
            rs1[rows, :] = jnp.broadcast_to(r, (16, 128))
            for p in range(4):
                n1[rows, p * 640:p * 640 + 640] = (xs[p] * r * gnb[p, 0:1, :]).astype(BF)
        if j < 2:
            gtk.relay(j + 2)
    outs += [cm.local(n1, n1_o), cm.local(gnb, g_o), cm.local(tkb, tk_o)]
    lw[0].wait()
    gcv = Gather(cm, cvb, None, [(q,) for q in range(5)])
    for qs in ((0, 1), (2, 3), (4,)):
        cs = slice(qs[0] * 128, qs[-1] * 128 + 128)
        xb[:, cs] = dot_nt(n1[...], wv[0, cs, :])
        for q in qs:
            x = xb[:, lanes(q)]
            acc = par[4:5, lanes(q)] + par[0:1, lanes(q)] * x
            for k in (1, 2, 3):
                acc = acc + par[k:k + 1, lanes(q)] * pltpu.roll(x, k, axis=0) * msk[k]
            cvb[f, q] = acc.astype(BF)
            gcv.start(q)
    gct.start()
    outs.append(cm.local(xb, xb_o))
    lw[2].wait()
    yb[...] = dot_nt(n1[...], wv[1])
    outs.append(cm.local(yb, yb_o))
    gcv.relay(0)
    gcv.relay(1)
    for q in range(5):
        gcv.finish(q)
        lhs = jnp.concatenate([cvb[p, q] for p in range(4)], axis=1)
        pre = dot_nt(lhs, wg[q])
        gxq, gaq = gate_values(q, pre, par, msk[0])
        sp, a, spread, mult = decay_of(q, gaq, par, msk[0])
        gx[:, lanes(q)] = gxq
        ga[:, lanes(q)] = gaq
        aa[:, lanes(q)] = jnp.where(msk[0] == 1.0, 0.0, a)
        uu[:, lanes(q)] = mult * gxq * cvb[f, q].astype(F32)
        if q < 3:
            gcv.relay(q + 2)
        if q < 4:
            n1t[q] = n1[:, q * 640:q * 640 + 640].T.reshape(4, 160, 256)
    outs.append(cm.local(cvb, cv_o))
    S.send_f(2)
    S.send_f(3)
    outs.append(cm.local(n1t, n1t_o))
    outs += [cm.local(gx, gx_o), cm.local(ga, ga_o)]
    scan_rows(aa, uu, hs, False)
    for q in range(5):
        yg, _ = gelu_parts(yb[:, lanes(q)])
        z[:, lanes(q)] = (hs[:, lanes(q)] * yg).astype(BF)
    S.send_u(11, direct=True)
    outs += [cm.local(hs, hs_o), cm.local(z, z_o)]
    lw[3].wait()
    red = Reduce(cm, pt, r1, s2, r2)
    for c in range(4):
        pt[c] = dot(z[...], wo[:, c * 640:c * 640 + 640]).astype(BF).reshape(4, 64, 640)
        red.send(c)
        if c: red.mid(c - 1)
    red.mid(3)
    gct.relay()
    gct.finish()
    @pl.loop(0, 16)
    def _(i):
        rows = pl.ds(pl.multiple_of(i * 16, 16), 16)
        live = jnp.broadcast_to(msk[4, rows, 0:1], (16, 640))
        for p in range(4):
            dt[rows, p * 640:p * 640 + 640] = (ctb[p, rows, :].astype(F32) * live).astype(BF)
    outs.append(cm.local(dt, dt_o))
    for c in range(4):
        dtt[c] = dt[:, c * 640:c * 640 + 640].T.reshape(4, 160, 256)
    S.send_f(1)
    outs.append(cm.local(dtt, dtt_o))
    for k in (2, 3):
        S.relay_f(k)
    own = pl.ds(pl.multiple_of(f * 64, 64), 64)
    ss = jnp.zeros((64, 1), F32)
    for c in range(4):
        h = tkb[c, own, :].astype(F32) + red.fin(c)
        h1[:, c * 640:c * 640 + 640] = h
        ss = ss + jnp.sum(h * h, axis=-1, keepdims=True)
    r = lax.rsqrt(ss * (1.0 / 2560) + EPS)
    rs2[...] = jnp.broadcast_to(r, (64, 128))
    for c in range(4):
        cs = slice(c * 640, c * 640 + 640)
        n2b[f, :, cs] = (h1[:, cs] * r * gnb[c, 1:2, :]).astype(BF)
    gn2 = Gather(cm, n2b, None, [(pl.ds(i * 16, 16),) for i in range(4)])
    gn2.start()
    outs += [cm.local(h1, h1_o), cm.local(rs1, r_o.at[pl.ds(0, 256)]), cm.local(rs2, r_o.at[pl.ds(256, 64)])]
    for i in range(4):
        gn2.relay(i)
    S.relay_f(1)
    gn2.finish()
    outs.append(cm.local(n2b, n2_o))
    for k in (2, 3, 1):
        arrived(S.f2[k])
    arrived(S.u[11].values())
    for c in outs:
        c.wait()
    cm.drain()

def forward(lenr, ownr, g1r, g2r, cwt, cbt, gbt, apt, tok, cot, w_t, gw_t, wo):
    s = jax.ShapeDtypeStruct
    R = 256
    fw = s((R, 640), F32)
    out_shape = [s((R, 2560), BF), s((4, 5, R, 128), BF), fw, fw, fw, fw, fw, s((R, 640), BF), s((4, 64, 2560), BF), s((R, 2560), BF),
                 s((64, 2560), F32), s((5, R, 128), F32), s((320, 128), F32), s((4, 8, 640), F32), s((5, 256, 512), BF), s((4, R, 640), BF), s((4, 4, 160, 256), BF), s((4, 4, 160, 256), BF), s((3, 3, 4, 160, 256), BF), s((3, R, 640), BF), s((8, 640), F32)]
    V = pltpu.VMEM
    f640 = V((R, 640), F32)
    scratch = [V((4, R, 640), BF), V((4, R, 640), BF), V((4, 8, 640), F32), V((2, 640, 2560), BF), V((2, 640, 256), BF), V((640, 2560), BF),
               V((5, 256, 512), BF), V((R, 2560), BF), V((R, 2560), BF), V((4, 5, R, 128), BF), f640, f640, f640, f640, f640, f640, f640,
               V((R, 640), BF), V((5, R, 128), F32), V((4, 4, 64, 640), BF), V((4, 2, 64, 640), BF), V((4, 64, 640), BF), V((4, 64, 640), BF),
               V((64, 2560), F32), V((4, 64, 2560), BF), V((R, 128), F32), V((64, 128), F32), V((4, 4, 160, 256), BF), V((4, 4, 160, 256), BF), V((8, 640), F32), V((8, 640), F32),
               pltpu.SemaphoreType.DMA((80,)), pltpu.SemaphoreType.DMA((80,)), pltpu.SemaphoreType.DMA((40,))]
    return pl.pallas_call(
        forward_kernel, out_shape=out_shape,
        in_specs=[VMEM] * 8 + [ANY] * 5,
        out_specs=[ANY] * len(out_shape),
        scratch_shapes=scratch,
        compiler_params=pltpu.CompilerParams(collective_id=3, has_side_effects=True, vmem_limit_bytes=VM),
        name="forward",
    )(lenr, ownr, g1r, g2r, cwt, cbt, gbt, apt, tok, cot, w_t, gw_t, wo)

def finish_kernel(bo, dtok, d_in, d_dn, d_xy, d_wo, gate, sm, bo_o, dtok_o, in_o, dn_o, xy_o, wo_o, gate_o, g1_o, g2_o, cw_o, cb_o, gb_o, a_o):
    for source, target in ((bo, bo_o), (dtok, dtok_o), (d_in, in_o), (d_dn, dn_o), (d_xy, xy_o), (d_wo, wo_o)):
        target[...] = source[...]
    g1_o[...] = sm[0]
    g2_o[...] = sm[1]
    for h in range(10):
        ls = slice(h * 64, h * 64 + 64)
        cw_o[h] = sm[2:6, ls]
        cb_o[h:h + 1] = sm[6:7, ls]
        gb_o[h] = sm[7:9, ls]
        a_o[h:h + 1] = sm[9:10, ls]
        for k in range(2):
            gate_o[k, h] = gate[k, h // 2, :, h % 2 * 64:h % 2 * 64 + 64]

def finish(bo, dtok, d_in, d_dn, d_xy, d_wo, gate, sm):
    s = jax.ShapeDtypeStruct
    out_shape = [s((4, 64, 640), BF), s((256, 640), F32), s((2, 80, 1920), F32), s((80, 1920), F32), s((2, 640, 80), F32), s((640, 80), F32),
                 s((2, 10, 8, 64), F32), s((640,), F32), s((640,), F32), s((10, 4, 64), F32), s((10, 64), F32), s((10, 2, 64), F32), s((10, 64), F32)]
    return pl.pallas_call(
        finish_kernel, out_shape=out_shape,
        in_specs=[VMEM] * 8,
        out_specs=[VMEM] * 13,
        compiler_params=pltpu.CompilerParams(vmem_limit_bytes=VM),
        name="finish",
    )(bo, dtok, d_in, d_dn, d_xy, d_wo, gate, sm)

PLAN = {
    "F0h": "d6",
    "F0g": "u0",
    "F0": "",
    "F1h": "q0 u3",
    "F1g": "u7",
    "F1": "",
    "F2h": "r0",
    "F2g": "",
    "F2": "d8 u1",
    "C0": "r3",
    "C1": "r7 r1 p0 u4 m0 p6 m6",
    "C2": "p3 p1 m3 u2 m1",
    "C2b": "w0 u5 w6 p7 r4 w1 w3",
    "C3": "",
    "C3b": "r2 m7 r5",
    "C5": "p4 m4 r10 v6 q4 p2 w4 v0 s6",
    "C6": "s0 m2 p5 m5 p8 w7 f0 w2 v3 p11 s3 v1",
    "E": "s1 w5 m8 v7 n11 p10 v2 r9 f6 m10 s7 w8 p9 s2 n9 g0 v4 f3 w10 s4 v5 f2 f7 s5 v8 f4 v11 s8 s11 v10 f5 s10 v9 s9 f8 f1 f10 g1 f9 f11 g2",
}

def tail_kernel(plan, par, n2_h, dt_h, w_in, w_dn, n1t_h, dtt_h, pf, pu, z_h, cv_h, xb_h, yb_h, gx_h, ga_h, hs_h, msk_h, r_h, g_h, wg_h, tk_h, h1_h, w_t, wo_h,
                bo_o, dtok_o, in_o, dn_o, xy_o, wout_o, gate_o, sm_o, ubh, rrh, fth,
                un, gu, hb, yr, fts, dr, pd, pm, bob, dto, gs, gr, sm, sgr, sgt, sgr2, sgy, sma, smr, smy,
                m1, m2, m3, d1, d2, d3, e1, e2, e3, f1, f2, f3, gnb, rb, h1, dtb, tk,
                ssem, rsem, lsem):
    cm = Comm(ssem, rsem, lsem)
    f = lax.axis_index("fsdp")
    x, z, y, _ = coords()
    own = pl.ds(pl.multiple_of(f * 64, 64), 64)
    rd = Reduce(cm, pd, d1, d2, d3)
    rm = Reduce(cm, pm, m1, m2, m3)
    def put(c, v):
        if c < 6:
            in_o[c // 3, :, c % 3 * 640:c % 3 * 640 + 640] = v
        elif c < 9:
            dn_o[:, (c - 6) * 640:(c - 6) * 640 + 640] = v
        elif c < 11:
            xy_o[c - 9] = v.T
        else:
            wout_o[...] = v.T
    usrc = [gu.at[i, :, pl.ds(j, 640)] for j in (0, 640) for i in range(3)] + [un.at[i] for i in range(3)] + [None, None, z_h]
    uland = [ubh.at[c] for c in range(11)] + [pu]
    fland = [fth.at[0], pf.at[0], pf.at[1], pf.at[2], fth.at[1]]
    S = Sums(cm, uland, fland, rrh, yr, usrc, [fts, dtt_h, n1t_h, n1t_h, fts], put)

    w = pltpu.VMEM((256, 640), F32)

    small = {}
    def at(point):
        for t in plan[point].split():
            run(t[0], int(t[1:]))
    def run(t, c):
        if t == "u": S.send_u(c)
        elif t == "d": S.send_u(c, direct=True)
        elif t == "r": S.relay_u(c)
        elif t == "q": S.relay_f(c)
        elif t == "p": S.prep(c)
        elif t == "m": S.mm(c)
        elif t == "n": S.mm(c, direct=True)
        elif t == "w": S.wsum(c)
        elif t == "v": S.rprep(c)
        elif t == "s": S.rsum(c)
        elif t == "f": S.fin(c)
        else: small_step(c)
    def small_step(j):
        if j == 0:
            arrived(small["g2"])
            sgy[0] = sgt[x].astype(F32) + sgr2[0].astype(F32) + sgr2[1].astype(F32) + sgr2[2].astype(F32)
            small[0] = cm.remote(sgy.at[0], sgy.at[1], ("y", 1))
            arrived(small["v1"])
            sma[1] = (sma[0] + smr[0, 0]) + (smr[0, 1] + smr[0, 2])
            small[1] = spread(cm, lambda d: sma.at[1], smr.at[1], "z")
        if j == 1:
            arrived(small[1])
            sma[2] = (sma[1] + smr[1, 0]) + (smr[1, 1] + smr[1, 2])
            small[2] = cm.remote(sma.at[2], smy, ("y", 1))
            small[0].wait_recv()
            half = pl.ds(pl.multiple_of(y * 8, 8), 8)
            gate_o[...] = sgy[0, :, :, half, :] + sgy[1, :, :, half, :]
        if j == 2:
            small[2].wait_recv()
            sm_o[...] = sma[2] + smy[...]

    def ffn_phase(wa, wd, am, ad, fg, fd, n2, dt):
        def load(i):
            s = i % 2
            cols = pl.ds(i * 640, 640)
            return [cm.local(w_in.at[0, :, cols], wa.at[s, :, pl.ds(0, 640)]), cm.local(w_in.at[1, :, cols], wa.at[s, :, pl.ds(640, 640)]), cm.local(w_dn.at[cols], wd.at[s])]
        ln = cm.local(n2_h, n2)
        lw = {0: load(0)}
        ld = cm.local(dt_h, dt)
        b = pltpu.get_barrier_semaphore()
        for axis, d in REP:
            pl.semaphore_signal(b, inc=1, device_id=peer(axis, d), device_id_type=MESH)
        for d in (1, 2, 3):
            pl.semaphore_signal(b, inc=1, device_id=fpeer(d), device_id_type=MESH)
        ln.wait()
        for c in range(4):
            fts[c] = n2[:, c * 640:c * 640 + 640].T.reshape(4, 160, 256)
        pl.semaphore_wait(b, len(REP) + 3)
        S.send_f(0)
        for i in range(3):
            s = i % 2
            lw[i][0].wait()
            lw[i][1].wait()
            fg[...] = dot(n2[...], wa[s])
            for q in range(5):
                gl, _ = gelu_parts(fg[:, lanes(q)])
                un[i, :, lanes(q)] = (gl * fg[:, lanes(q + 5)]).astype(BF)
            at(f"F{i}h")
            lw[i][2].wait()
            if i == 0:
                lw[1] = load(1)
                ld.wait()
            fd[...] = dot_nt(dt[...], wd[s])
            for q in range(5):
                gl, dgl = gelu_parts(fg[:, lanes(q)])
                dh = fd[:, lanes(q)]
                gu[i, :, lanes(q)] = (dh * fg[:, lanes(q + 5)] * dgl).astype(BF)
                gu[i, :, lanes(q + 5)] = (dh * gl).astype(BF)
            at(f"F{i}g")
            if i == 0:
                ad[...] = dot_nt(gu[i], wa[s])
                am[...] = dot(un[i], wd[s])
            elif i == 1:
                ad[...] = ad[...] + dot_nt(gu[i], wa[s])
                am[...] = am[...] + dot(un[i], wd[s])
            else:
                for c in range(4):
                    cs = slice(c * 640, c * 640 + 640)
                    pd[c] = (ad[:, cs] + dot_nt(gu[i], wa[s, cs, :])).astype(BF).reshape(4, 64, 640)
                    rd.send(c)
                    if c: rd.mid(c - 1)
                rd.mid(3)
                for c in range(4):
                    cs = slice(c * 640, c * 640 + 640)
                    pm[c] = (am[:, cs] + dot(un[i], wd[s, :, cs])).astype(BF).reshape(4, 64, 640)
            if i == 0:
                lw[2] = load(2)
            at(f"F{i}")

    pl.run_scoped(ffn_phase, pltpu.VMEM((2, 2560, 1280), BF), pltpu.VMEM((2, 640, 2560), BF), pltpu.VMEM((256, 2560), F32), pltpu.VMEM((256, 2560), F32), pltpu.VMEM((256, 1280), F32), w, pltpu.VMEM((256, 2560), BF), pltpu.VMEM((256, 2560), BF))

    def chain_phase(cv, xb, yb, gx, ga, hs, msk, wg, wbuf, aa, uu, gg, dc1, dp, dna, ft, uw, st, rw, tt, bo, dob, sg, dxy, dxx, pb, dnp, dh1):
        S.work(ft, uw, st, rw, tt, hb)
        S.usrc[9], S.usrc[10] = dxy.at[0], dxy.at[1]
        lh = [cm.local(h1_h, h1), cm.local(g_h, gnb), cm.local(r_h, rb), cm.local(dt_h.at[own], dtb), cm.local(tk_h.at[:, own], tk)]
        lb = [cm.local(wo_h, wbuf.at[0]), cm.local(yb_h, yb), cm.local(hs_h, hs), cm.local(ga_h, ga), cm.local(msk_h, msk), cm.local(gx_h, gx), cm.local(cv_h, cv),
              cm.local(wg_h, wg), cm.local(xb_h, xb), cm.local(w_t.at[1], wbuf.at[1])]
        for c in range(4):
            rm.send(c)
        at("C0")
        for c in lh:
            c.wait()
        gs[...] = jnp.zeros_like(gs)
        r2 = rb[256:320, 0:1]
        acc = jnp.zeros((64, 1), F32)
        for c in range(4):
            cs = slice(c * 640, c * 640 + 640)
            dn = rd.fin(c)
            h = h1[:, cs]
            gs[c, 1:2, :] = jnp.sum(dn * h * r2, axis=0, keepdims=True)
            v = dn * gnb[c, 1:2, :]
            dh1[:, cs] = v
            acc = acc + jnp.sum(v * h, axis=-1, keepdims=True)
        acc = acc * (1.0 / 2560) * (r2 * r2 * r2)
        for c in range(4):
            cs = slice(c * 640, c * 640 + 640)
            d = dtb[:, cs].astype(F32) + r2 * dh1[:, cs] - h1[:, cs] * acc
            dh1[:, cs] = d
            dr[f, :, cs] = d.astype(BF)
        gdr = Gather(cm, dr, None, [(pl.ds(0, 32),), (pl.ds(32, 32),)])
        gdr.start()
        for c in range(4):
            rm.mid(c)
        at("C1")
        for c in lb:
            c.wait()
        for q in range(5):
            sp, a, spread_, mult = decay_of(q, ga[:, lanes(q)], par, msk[0])
            up = pltpu.roll(jnp.where(msk[0] == 1.0, 0.0, a), 255, axis=0)
            rows = lax.broadcasted_iota(jnp.int32, (256, 128), 0)
            aa[:, lanes(q)] = jnp.where(rows == 255, 0.0, up)
        gdr.relay()
        at("C2")
        gdr.finish()
        uu[...] = dot_nt(dr[...].reshape(256, 2560), wbuf[0])
        lw0 = cm.local(w_t.at[0], wbuf.at[0])
        for q in range(5):
            yg, dgl = gelu_parts(yb[:, lanes(q)])
            dz = uu[:, lanes(q)]
            dxy[1, :, lanes(q)] = (dz * hs[:, lanes(q)] * dgl).astype(BF)
            uu[:, lanes(q)] = dz * yg
        S.send_u(10)
        at("C2b")
        scan_rows(aa, uu, gg, True)
        re = Reduce(cm, pb, e1, e2, e3)
        for q in range(5):
            ls = lanes(q)
            start = msk[0]
            gxq, gaq, g = gx[:, ls], ga[:, ls], gg[:, ls]
            sp, a, spread_, mult = decay_of(q, gaq, par, start)
            cvq = cv[f, q].astype(F32)
            prev = jnp.where(start == 1.0, 0.0, pltpu.roll(hs[:, ls], 1, axis=0))
            slope = jnp.where((start == 1.0) | (spread_ <= 0.01), 0.0, -a / mult)
            da = g * prev + g * gxq * cvq * slope
            dc1[:, ls] = g * mult * gxq
            dlog = da * a
            da_p = jnp.sum(dlog * (-8.0 * gaq), axis=0, keepdims=True) * sigmoid(par[7:8, ls])
            px = (g * mult * cvq * gxq * (1.0 - gxq)).astype(BF)
            pa = (-8.0 * dlog * sp * gaq * (1.0 - gaq)).astype(BF)
            dp[q, :, 0:128] = px
            dp[q, :, 128:256] = pa
            sm[7:8, ls] = jnp.sum(px.astype(F32), axis=0, keepdims=True)
            sm[8:9, ls] = jnp.sum(pa.astype(F32), axis=0, keepdims=True)
            sm[9:10, ls] = da_p
            db = dot(dp[q], wg[q]).astype(BF)
            for p in range(4):
                pb[q, p] = db[:, lanes(p)]
            re.send(q)
            if q: re.mid(q - 1)
        re.mid(4)
        for old in S.f[0].values():
            cm.sent(old)
        drt = dr[...].reshape(256, 2560)
        for c in range(4):
            fts[c] = drt[:, c * 640:c * 640 + 640].T.reshape(4, 160, 256)
        S.send_f(4)
        at("C3")
        for c in range(4):
            cs = slice(c * 640, c * 640 + 640)
            dna[c] = dot(dxy[1], wbuf[1, :, cs])
        low = lax.broadcasted_iota(jnp.int32, (64, 128), 1) < 64
        for q in range(5):
            lhs = jnp.concatenate([cv[p, q] for p in range(4)], axis=1)
            gwt = dot_tn(lhs, dp[q])
            for p in range(4):
                for k in range(2):
                    blk = gwt[p * 128:p * 128 + 128, k * 128:k * 128 + 128]
                    sg[p, k, q] = jnp.where(low, blk[0:64], blk[64:128]).astype(BF)
        g1 = spread(cm, lambda d: sg.at[:, :, :, pl.ds(pl.multiple_of((z + d) % 4 * 16, 16), 16)], sgr, "z")
        at("C3b")
        live = msk[4, own, 0:1]
        for c in range(4):
            bo[c] = (live * (h1[:, c * 640:c * 640 + 640] + rm.fin(c))).astype(BF)
        sbo = Swap(cm, bo, bob)
        for q in range(5):
            ls = lanes(q)
            d = dc1[:, ls] + re.fin(q)
            xq = xb[:, ls]
            sm[6:7, ls] = jnp.sum(d, axis=0, keepdims=True)
            sm[2:3, ls] = jnp.sum(d * xq, axis=0, keepdims=True)
            dx = par[0:1, ls] * d
            for k in (1, 2, 3):
                m = d * msk[k]
                sm[2 + k:3 + k, ls] = jnp.sum(m * pltpu.roll(xq, k, axis=0), axis=0, keepdims=True)
                dx = dx + par[k:k + 1, ls] * pltpu.roll(m, 256 - k, axis=0)
            dxy[0, :, ls] = dx.astype(BF)
        S.send_u(9)
        lw0.wait()
        rf = Reduce(cm, dnp, f1, f2, f3)
        for c in range(4):
            cs = slice(c * 640, c * 640 + 640)
            dnp[c] = (dna[c] + dot(dxy[0], wbuf[0, :, cs])).astype(BF).reshape(4, 64, 640)
            rf.send(c)
            if c: rf.mid(c - 1)
        rf.mid(3)
        at("C5")
        r1 = rb[own, 0:1]
        acc = jnp.zeros((64, 1), F32)
        for c in range(4):
            dn = rf.fin(c)
            xr = tk[c].astype(F32)
            gs[c, 0:1, :] = jnp.sum(dn * xr * r1, axis=0, keepdims=True)
            v = dn * gnb[c, 0:1, :]
            dna[c, 0:64, :] = v
            acc = acc + jnp.sum(v * xr, axis=-1, keepdims=True)
        acc = acc * (1.0 / 2560) * (r1 * r1 * r1)
        for c in range(4):
            dob[c] = (dh1[:, c * 640:c * 640 + 640] + r1 * dna[c, 0:64, :] - tk[c].astype(F32) * acc).astype(BF)
        sdt = Swap(cm, dob, dto)
        gcp = []
        for d in (3, 2, 1):
            _, t = fpeer(d)
            gcp.append(cm.remote(gs.at[t], gr.at[d - 1], ("f", d)))
        sbo.finish()
        outs = [cm.local(bob, bo_o)]
        at("C6")
        arrived(g1)
        t = sg[:, :, :, pl.ds(pl.multiple_of(z * 16, 16), 16), :].astype(F32)
        sgt[...] = ((t + sgr[0].astype(F32)) + (sgr[1].astype(F32) + sgr[2].astype(F32))).astype(BF)
        small["g2"] = spread(cm, lambda d: sgt.at[(x + d) % 4], sgr2, "x")
        arrived(gcp)
        sm[0:2, :] = (gs[f, 0:2, :] + gr[0, 0:2, :]) + (gr[1, 0:2, :] + gr[2, 0:2, :])
        sm[10:16, :] = jnp.zeros((6, 640), F32)
        sma[0] = sm[...]
        small["v1"] = spread(cm, lambda d: sma.at[0], smr.at[0], "x")
        sdt.finish()
        dxx[...] = dto[...].astype(F32).reshape(256, 640)
        outs.append(cm.local(dxx, dtok_o))
        at("E")
        for c in outs:
            c.wait()
        cm.drain()

    pl.run_scoped(chain_phase, pltpu.VMEM((4, 5, 256, 128), BF), w, w, w, w, w, pltpu.VMEM((5, 256, 128), F32), pltpu.VMEM((5, 256, 512), BF), pltpu.VMEM((2, 640, 2560), BF),
                  w, w, w, w, pltpu.VMEM((5, 256, 256), BF), pltpu.VMEM((4, 256, 640), F32),
                  pltpu.VMEM((3, 4, 160, 1024), BF), pltpu.VMEM((2, 4, 256, 640), BF), pltpu.VMEM((4, 4, 160, 640), BF), pltpu.VMEM((2, 3, 160, 640), BF), pltpu.VMEM((12, 2, 80, 640), BF),
                  pltpu.VMEM((4, 64, 640), BF), pltpu.VMEM((4, 64, 640), BF), pltpu.VMEM((4, 2, 5, 64, 128), BF), pltpu.VMEM((2, 256, 640), BF), w,
                  pltpu.VMEM((5, 4, 256, 128), BF), pltpu.VMEM((4, 4, 64, 640), BF), pltpu.VMEM((64, 2560), F32))

def tail(par, n2, dt, w_in, w_dn, n1t, dtt, pf, pu, z, cv, xb, yb, gx, ga, hs, msk, r, g, wg, tk, h1, w_t, wo, plan=PLAN):
    s = jax.ShapeDtypeStruct
    R = 256
    V = pltpu.VMEM
    out_shape = [s((4, 64, 640), BF), s((R, 640), F32), s((2, 80, 1920), F32), s((80, 1920), F32), s((2, 640, 80), F32), s((640, 80), F32),
                 s((2, 5, 8, 128), F32), s((16, 640), F32), s((11, 3, R, 640), BF), s((12, 3, 160, 640), BF), s((2, 3, 4, 160, 256), BF)]
    blk = V((4, 4, 64, 640), BF)
    row = V((4, 64, 640), BF)
    red = [V((4, 2, 64, 640), BF), row, row]
    red5 = [V((5, 2, R, 128), BF), V((5, R, 128), BF), V((5, R, 128), BF)]
    scratch = [V((3, R, 640), BF), V((3, R, 1280), BF), V((12, 2, 80, 640), BF), V((12, 80, 640), BF), V((4, 4, 160, 256), BF), V((4, 64, 2560), BF), blk, blk, row, row,
               V((4, 8, 640), F32), V((3, 8, 640), F32), V((16, 640), F32),
               V((3, 4, 2, 5, 16, 128), BF), V((4, 2, 5, 16, 128), BF), V((3, 2, 5, 16, 128), BF), V((2, 2, 5, 16, 128), F32),
               V((3, 16, 640), F32), V((2, 3, 16, 640), F32), V((16, 640), F32)] + red + red + red5 + red + [
               V((4, 8, 640), F32), V((320, 128), F32), V((64, 2560), F32), V((64, 2560), BF), V((4, 64, 640), BF),
               pltpu.SemaphoreType.DMA((224,)), pltpu.SemaphoreType.DMA((224,)), pltpu.SemaphoreType.DMA((128,))]
    return pl.pallas_call(
        functools.partial(tail_kernel, plan), out_shape=out_shape,
        in_specs=[VMEM] + [ANY] * 23,
        out_specs=[ANY] * 2 + [VMEM] * 6 + [ANY] * 3,
        scratch_shapes=scratch,
        compiler_params=pltpu.CompilerParams(collective_id=5, has_side_effects=True, vmem_limit_bytes=VM),
        name="tail",
    )(par, n2, dt, w_in, w_dn, n1t, dtt, pf, pu, z, cv, xb, yb, gx, ga, hs, msk, r, g, wg, tk, h1, w_t, wo)

def body_of(plan, tokens, seq_len, seq_owner, gain_1, gain_2, w_xy, conv_w, conv_b, gate_w, gate_b, a_param, w_out, w_in, w_down, cotangent):
    small, w_t, gw_t, wo = prep(seq_len, seq_owner, gain_1, gain_2, w_xy, conv_w, conv_b, gate_w, gate_b, a_param, w_out)
    (n1, cv, xb, yb, gx, ga, hs, z, n2, dt, h1, msk, r, g, wg, tk, n1t, dtt, pf, pu, par) = forward(*small, tokens, cotangent, w_t, gw_t, wo)
    sums = tail(par, n2.reshape(256, 2560), dt, w_in, w_down, n1t, dtt, pf, pu, z, cv, xb, yb, gx, ga, hs, msk, r, g, wg, tk, h1, w_t, wo, plan)[:8]
    bo, dtok, d_in, d_dn, d_xy, d_wo, gate, g1, g2, cw, cb, gb, da = finish(*sums)
    return (bo.reshape(256, 640), dtok, g1, g2, jnp.transpose(d_xy.reshape(2, 10, 64, 80), (0, 3, 1, 2)), jnp.transpose(cw, (1, 0, 2)), cb,
            gate, jnp.transpose(gb, (1, 0, 2)), da, d_wo.reshape(10, 64, 80), d_in, d_dn.T)

def body(*args):
    return body_of(PLAN, *args)


def solution(mesh):
    return jax.shard_map(
        body,
        mesh=mesh,
        in_specs=(
            P("rep", "fsdp"), P(), P(), P("fsdp"), P("fsdp"), P(None, None, None, "fsdp"), P(None, None, "fsdp"), P(None, "fsdp"),
            P(None, None, None, "fsdp"), P(None, None, "fsdp"), P(None, "fsdp"), P(None, "fsdp", None), P(None, None, "fsdp"), P("fsdp", None), P("rep", "fsdp"),
        ),
        out_specs=(
            P("rep", "fsdp"), P("rep", "fsdp"), P("fsdp"), P("fsdp"), P(None, "rep", None, "fsdp"), P(None, None, "fsdp"), P(None, "fsdp"),
            P(None, None, "rep", "fsdp"), P(None, None, "fsdp"), P(None, "fsdp"), P(None, "fsdp", "rep"), P(None, "rep", "fsdp"), P("fsdp", "rep"),
        ),
        check_vma=False,
    )
```
